128 devices in a mesh: dp: 64 (over y, x, z_lo, core), tensor: 2 (over z_hi).
Axes of the slice: x: 4, y: 4, z: 4 (z_hi: 2, z_lo: 2; z = z_hi * 2 + z_lo), core: 2. Of those that a mesh axis runs over, the one named last changes fastest.
Arguments:
- tokens: bfloat16 [24576, 768], P('dp'), may hold values from -6 to 6
- cotangent: bfloat16 [24576, 768], P('dp'), may hold values from -6 to 6
- segment_ids: int32 [64, 384], P('dp'), may hold values from 0 to 1, as said below
- live_len: int32 [64], P('dp'), may hold values from 96 to 384, as said below
- w_square: float32 [5, 768, 768], P(None, 'dp', 'tensor')
- w_wide: float32 [3, 768, 2048], P(None, 'dp', 'tensor')
- norm_gain: float32 [2, 768], P(None, 'dp'), may hold values from 0.5 to 1.5
- qk_gain: float32 [2, 64], replicated, may hold values from 0.5 to 1.5
- forget_w: float32 [768, 12], P('dp', 'tensor'), may hold values from -0.21875 to 0.21875
- forget_b: float32 [12], P('tensor'), may hold values from 2 to 7
- m_square: float32 [5, 768, 768], P(None, 'dp', 'tensor'), may hold values from -940.60406 to 940.60406
- m_wide: float32 [3, 768, 2048], P(None, 'dp', 'tensor'), may hold values from -940.60406 to 940.60406
- m_norm: float32 [2, 768], P(None, 'dp'), may hold values from -940.60406 to 940.60406
- m_qk: float32 [2, 64], replicated, may hold values from -3762.4163 to 3762.4163
- m_forget_w: float32 [768, 12], P('dp', 'tensor'), may hold values from -282.1812 to 282.1812
- m_forget_b: float32 [12], P('tensor'), may hold values from -940.60406 to 940.60406
- ema_square: float32 [5, 768, 768], P(None, 'dp', 'tensor')
- ema_wide: float32 [3, 768, 2048], P(None, 'dp', 'tensor')
Outputs:
- result: bfloat16 [24576, 768], P('dp')
- input_grad: float32 [24576, 768], P('dp')
- new_square: float32 [5, 768, 768], P(None, 'dp', 'tensor')
- new_wide: float32 [3, 768, 2048], P(None, 'dp', 'tensor')
- new_norm: float32 [2, 768], P(None, 'dp')
- new_qk: float32 [2, 64], replicated
- new_forget_w: float32 [768, 12], P('dp', 'tensor')
- new_forget_b: float32 [12], P('tensor')
- mom_square: float32 [5, 768, 768], P(None, 'dp', 'tensor')
- mom_wide: float32 [3, 768, 2048], P(None, 'dp', 'tensor')
- mom_norm: float32 [2, 768], P(None, 'dp')
- mom_qk: float32 [2, 64], replicated
- mom_forget_w: float32 [768, 12], P('dp', 'tensor')
- mom_forget_b: float32 [12], P('tensor')
- new_ema_square: float32 [5, 768, 768], P(None, 'dp', 'tensor')
- new_ema_wide: float32 [3, 768, 2048], P(None, 'dp', 'tensor')
The draws below stay inside these ranges and needn't reach their ends.
Inputs may be any that keep to these rules, and one draw needn't show every extreme that they name: Each row of 384 slots holds live_len live tokens at its head, the rest is padding. `segment_ids`: each row holds document 0 on its first slots and, from a boundary at slot 192 or later, document 1; a row may hold document 0 alone.
All inputs are finite; a program needn't handle non-finite values.
Results may differ from the reference program's by a relative error of at most 0.04.
Values may be sent and summed in bfloat16 or wider, within the bound.
No kernel may reach another device: no remote copies, remote signals or barrier semaphores. Data moves between devices by JAX's collectives and lax.ppermute only.
A program may use at most 128 MiB of HBM per device.

```python
import math
import jax
import jax.numpy as jnp
from jax import lax

D = 768
H = 12
HD = 64
FF = 2048
TOK_DEV = 384
SEQS = 64
TOKENS = 24576


def square_law(key):
    factors = jnp.array([1.0, 1.0, 1.0, 1.0, 4.0], jnp.float32)
    normal_part = jax.random.truncated_normal(key, -4.0, 4.0, (5, D, D), jnp.float32)
    return normal_part * factors[:, None, None] / math.sqrt(D)


def wide_law(key):
    factors = jnp.array([1.0 / math.sqrt(D), 1.0 / math.sqrt(D), 1.0 / math.sqrt(FF)], jnp.float32)
    normal_part = jax.random.truncated_normal(key, -4.0, 4.0, (3, D, FF), jnp.float32)
    return normal_part * factors[:, None, None]


def draw_w_square(key, part):
    key = jax.random.fold_in(key, 21)
    return square_law(key)


def draw_ema_square(key, part):
    key = jax.random.fold_in(key, 22)
    return square_law(key)


def draw_w_wide(key, part):
    key = jax.random.fold_in(key, 23)
    return wide_law(key)


def draw_ema_wide(key, part):
    key = jax.random.fold_in(key, 24)
    return wide_law(key)


def draw_segment_ids(key, part):
    key = jax.random.fold_in(key, 12)
    row_number = jnp.arange(SEQS, dtype=jnp.int32)
    boundary = jax.random.randint(key, (SEQS,), TOK_DEV // 2, TOK_DEV + 1, dtype=jnp.int32)
    first_cut = jax.random.randint(jax.random.fold_in(key, 1), (), TOK_DEV // 2, TOK_DEV, dtype=jnp.int32)
    boundary = jnp.where(row_number == 0, first_cut, boundary)
    positions = jnp.arange(TOK_DEV, dtype=jnp.int32)
    return (positions[None, :] >= boundary[:, None]).astype(jnp.int32)


def draw_live_len(key, part):
    key = jax.random.fold_in(key, 11)
    row_number = jnp.arange(SEQS, dtype=jnp.int32)
    lowest = TOK_DEV // 4
    rising = lowest + (TOK_DEV - lowest) * row_number // max(SEQS - 1, 1)
    jitter = jax.random.randint(key, (SEQS,), 0, TOK_DEV // 8 + 1, dtype=jnp.int32)
    sampled = jnp.clip(rising - jitter, lowest, TOK_DEV)
    return jnp.where(row_number == SEQS - 1, TOK_DEV, sampled).astype(jnp.int32)


def level_of(own_key, dims, split, least, top_value):
    def one(dim, blocks):
        steps = jax.random.uniform(jax.random.fold_in(jax.random.fold_in(own_key, 6), dim), (blocks,), jnp.float32, least / len(split), top_value / len(split))
        return jnp.repeat(jnp.exp(steps), dims[dim] // blocks).reshape((-1,) + (1,) * (len(dims) - dim - 1))

    loudness = one(*split[0])
    for cut in split[1:]:
        loudness = loudness * one(*cut)
    return loudness


def gaussian(key, dims, spread, most, split=(), kind=jnp.bfloat16):
    loudness = level_of(key, dims, split, -0.22, 0.18) if split else 1.0
    values = jax.random.normal(key, dims, jnp.float32) * spread * loudness
    return jnp.minimum(jnp.maximum(values, -most), most).astype(kind)


def setup_inputs(seed: int = 0) -> dict:
    arg_keys = jax.random.split(jax.random.key(seed), 19)
    tokens = gaussian(arg_keys[0], (TOKENS, D), 1.0, 6.0, ((0, 64),))
    cotangent = gaussian(arg_keys[1], (TOKENS, D), 1.0, 6.0, ((0, 64),))
    segment_ids = draw_segment_ids(jax.random.fold_in(arg_keys[18], 71), 0)
    live_len = draw_live_len(jax.random.fold_in(arg_keys[18], 71), 0)
    w_square = draw_w_square(jax.random.fold_in(arg_keys[18], 71), 0)
    w_wide = draw_w_wide(jax.random.fold_in(arg_keys[18], 71), 0)
    norm_gain = jnp.clip(1.0 + 0.1 * jax.random.normal(arg_keys[6], (2, D), jnp.float32), 0.5, 1.5)
    qk_gain = jnp.clip(1.0 + 0.1 * jax.random.normal(arg_keys[7], (2, HD), jnp.float32), 0.5, 1.5)
    forget_w = gaussian(arg_keys[8], (D, H), D ** -0.5, 0.21875, ((0, 64), (1, 2)), jnp.float32)
    forget_b = jnp.clip(2.0 + 5.0 * jax.random.uniform(arg_keys[9], (H,), jnp.float32) ** level_of(arg_keys[9], (H,), ((0, 2),), -0.2, 0.2), 2.0, 7.0)
    m_square = gaussian(arg_keys[10], (5, D, D), (TOKENS ** 0.5), 940.60406, ((1, 64), (2, 2)), jnp.float32)
    m_wide = gaussian(arg_keys[11], (3, D, FF), (TOKENS ** 0.5), 940.60406, ((1, 64), (2, 2)), jnp.float32)
    m_norm = gaussian(arg_keys[12], (2, D), (TOKENS ** 0.5), 940.60406, ((1, 64),), jnp.float32)
    m_qk = gaussian(arg_keys[13], (2, HD), (4.0 * TOKENS ** 0.5), 3762.4163, (), jnp.float32)
    m_forget_w = gaussian(arg_keys[14], (D, H), (0.3 * TOKENS ** 0.5), 282.1812, ((0, 64), (1, 2)), jnp.float32)
    m_forget_b = gaussian(arg_keys[15], (H,), (TOKENS ** 0.5), 940.60406, ((0, 2),), jnp.float32)
    ema_square = draw_ema_square(jax.random.fold_in(arg_keys[18], 71), 0)
    ema_wide = draw_ema_wide(jax.random.fold_in(arg_keys[18], 71), 0)
    return dict(tokens=tokens, cotangent=cotangent, segment_ids=segment_ids, live_len=live_len, w_square=w_square, w_wide=w_wide, norm_gain=norm_gain, qk_gain=qk_gain, forget_w=forget_w, forget_b=forget_b, m_square=m_square, m_wide=m_wide, m_norm=m_norm, m_qk=m_qk, m_forget_w=m_forget_w, m_forget_b=m_forget_b, ema_square=ema_square, ema_wide=ema_wide)


@jax.custom_vjp
def low(v):
    return lax.optimization_barrier(v.astype(jnp.bfloat16)).astype(jnp.float32)

@jax.custom_vjp
def low_back(v):
    return v

def low_keep(v):
    return (low(v), None)

def low_pass(kept, grad):
    return (grad,)

def back_keep(v):
    return (v, None)

def back_low(kept, grad):
    return (low(grad),)
low.defvjp(low_keep, low_pass)
low_back.defvjp(back_keep, back_low)
epsilon = 1e-06
coef_a = 3.4445
coef_b = -4.775
coef_c = 2.0315
muon_decay = 0.95
plain_decay = 0.9
ema_decay = 0.7
gain_rate = 0.2
qk_rate = 0.05
forget_rate = 0.1
bias_rate = 0.5

def product(left, right):
    return jnp.dot(left, right, precision=lax.Precision.HIGHEST, preferred_element_type=jnp.float32)

def rms_norm(values, scale_row):
    return values * lax.rsqrt(lax.optimization_barrier(jnp.mean(values * values, axis=-1, keepdims=True)) + epsilon) * scale_row

def orthogonalize(matrix):
    norm_value = jnp.sqrt(jnp.sum(matrix * matrix))
    current = (matrix / (norm_value + 1e-07)).astype(jnp.bfloat16)
    for repeat in range(5):
        square = jnp.dot(current, current.T, preferred_element_type=jnp.float32).astype(jnp.bfloat16)
        poly_term = (coef_b * square.astype(jnp.float32) + coef_c * jnp.dot(square, square, preferred_element_type=jnp.float32)).astype(jnp.bfloat16)
        current = (coef_a * current.astype(jnp.float32) + jnp.dot(poly_term, current, preferred_element_type=jnp.float32)).astype(jnp.bfloat16)
    return current

def layer_row(param_set, row_in, row_docs, row_live):
    sq_w, wide_w, norm_w, qk_w, forget_wt, forget_bias = param_set
    positions = jnp.arange(TOK_DEV)
    allowed = (row_docs[:, None] == row_docs[None, :]) & (positions[None, :] <= positions[:, None])
    allowed = allowed & ((positions[None, :] < row_live) | (positions[None, :] == positions[:, None]))
    normed_one = low(rms_norm(row_in, norm_w[0]))
    query_raw = low_back(product(normed_one, sq_w[0]))
    key_raw = low_back(product(normed_one, sq_w[1]))
    value_heads = low_back(low(product(normed_one, sq_w[2]))).reshape(TOK_DEV, H, HD)
    gate_raw = low_back(product(normed_one, sq_w[3]))
    forget_logit = low_back(product(normed_one, forget_wt) + forget_bias)
    query_n = low_back(low(rms_norm(query_raw.reshape(TOK_DEV, H, HD), qk_w[0])))
    key_n = low_back(low(rms_norm(key_raw.reshape(TOK_DEV, H, HD), qk_w[1])))
    cum_decay = jnp.cumsum(jax.nn.log_sigmoid(forget_logit), axis=0)
    raw_scores = jnp.einsum('ihd,jhd->hij', query_n, key_n, precision=lax.Precision.HIGHEST) / math.sqrt(HD)
    raw_scores = raw_scores + cum_decay.T[:, :, None] - cum_decay.T[:, None, :]
    scores = low_back(jnp.where(allowed[None], raw_scores, -1e+30))
    peak = lax.optimization_barrier(jnp.max(scores, axis=-1, keepdims=True))
    log_total = peak + jnp.log(lax.optimization_barrier(jnp.sum(jnp.exp(scores - peak), axis=-1, keepdims=True)))
    probs = low(jnp.exp(scores - log_total))
    attended = low_back(jnp.einsum('hij,jhd->ihd', probs, value_heads, precision=lax.Precision.HIGHEST)).reshape(TOK_DEV, D)
    gated = low(attended * jax.nn.sigmoid(gate_raw))
    attn_out = low_back(product(gated, sq_w[4].T))
    middle = row_in + attn_out
    normed_two = low(rms_norm(middle, norm_w[1]))
    gate_v = low_back(product(normed_two, wide_w[0]))
    up_v = low_back(product(normed_two, wide_w[1]))
    activated = low(jax.nn.silu(gate_v) * up_v)
    return middle + low_back(product(activated, wide_w[2].T))

def reference(tokens, cotangent, segment_ids, live_len, w_square, w_wide, norm_gain, qk_gain, forget_w, forget_b, m_square, m_wide, m_norm, m_qk, m_forget_w, m_forget_b, ema_square, ema_wide):
    params = (low(w_square), low(w_wide), low(norm_gain), low(qk_gain), low(forget_w), low(forget_b))
    inputs = tokens.astype(jnp.float32).reshape(SEQS, TOK_DEV, D)

    def forward(param_set, input_rows):

        def per_row(carried):
            row_in, row_docs, row_live = carried
            return layer_row(param_set, row_in, row_docs, row_live)
        return lax.map(jax.checkpoint(per_row), (input_rows, segment_ids, live_len))
    outputs, pull_back = jax.vjp(forward, params, inputs)
    positions = jnp.arange(TOK_DEV)
    live_mask = (positions[None, :] < live_len[:, None]).astype(jnp.float32)[:, :, None]
    seed_grad = cotangent.astype(jnp.float32).reshape(SEQS, TOK_DEV, D) * live_mask
    grads, grad_input = pull_back(seed_grad)
    grad_sq, grad_wide, grad_norm, grad_qk, grad_fw, grad_fb = grads
    mom_square = muon_decay * m_square + grad_sq
    mom_wide = muon_decay * m_wide + grad_wide
    ortho_square = jnp.stack([orthogonalize(mom_square[number]) for number in range(5)]).astype(jnp.float32)
    ortho_wide = jnp.stack([orthogonalize(mom_wide[number]) for number in range(3)]).astype(jnp.float32)
    new_square = w_square - ortho_square
    new_wide = w_wide - math.sqrt(FF / D) * ortho_wide
    new_ema_square = ema_decay * ema_square + (1.0 - ema_decay) * new_square
    new_ema_wide = ema_decay * ema_wide + (1.0 - ema_decay) * new_wide
    root_tokens = math.sqrt(TOKENS)
    mom_norm = plain_decay * m_norm + grad_norm
    mom_qk = plain_decay * m_qk + grad_qk
    mom_forget_w = plain_decay * m_forget_w + grad_fw
    mom_forget_b = plain_decay * m_forget_b + grad_fb
    new_norm = norm_gain - gain_rate / root_tokens * mom_norm
    new_qk = qk_gain - qk_rate / root_tokens * mom_qk
    new_forget_w = forget_w - forget_rate / root_tokens * mom_forget_w
    new_forget_b = forget_b - bias_rate / root_tokens * mom_forget_b
    result = outputs.reshape(TOKENS, D).astype(jnp.bfloat16)
    input_grad = grad_input.reshape(TOKENS, D)
    return (result, input_grad, new_square, new_wide, new_norm, new_qk, new_forget_w, new_forget_b, mom_square, mom_wide, mom_norm, mom_qk, mom_forget_w, mom_forget_b, new_ema_square, new_ema_wide)
```

```python
import math

import jax
import jax.numpy as jnp
from jax import lax
import numpy as np
from jax.sharding import PartitionSpec as P

epsilon = 1e-06
coef_a = 3.4445
coef_b = -4.775
coef_c = 2.0315
muon_decay = 0.95
plain_decay = 0.9
ema_decay = 0.7
gain_rate = 0.2
qk_rate = 0.05
forget_rate = 0.1
bias_rate = 0.5


def rms_norm(values, scale_row):
    return (
        values * lax.rsqrt(jnp.mean(values * values, axis=-1, keepdims=True) + epsilon) * scale_row
    )


def swiglu(gate_part, up_part):
    return jax.nn.silu(gate_part) * up_part


def newton_step(current, square_sum):
    square = square_sum.astype(jnp.bfloat16)
    poly_term = (
        coef_b * square.astype(jnp.float32)
        + coef_c * jnp.dot(square, square, preferred_element_type=jnp.float32)
    ).astype(jnp.bfloat16)
    return (
        coef_a * current.astype(jnp.float32)
        + jnp.dot(poly_term, current, preferred_element_type=jnp.float32)
    ).astype(jnp.bfloat16)


grid_sizes = {"y": 4, "x": 4, "l": 2, "c": 2, "t": 2}


def ring_groups(names, over):
    order = [name for name in over if name not in names]
    table = np.arange(math.prod(grid_sizes[name] for name in over))
    table = table.reshape([grid_sizes[name] for name in over])
    table = table.transpose([over.index(name) for name in order + list(names)])
    return table.reshape(-1, math.prod(grid_sizes[name] for name in names)).tolist()


def exchange(blocks, names):
    if "t" in names:
        return lax.all_to_all(
            blocks,
            ("dp", "tensor"),
            split_axis=0,
            concat_axis=0,
            tiled=True,
            axis_index_groups=ring_groups(names, ["y", "x", "l", "c", "t"]),
        )
    return lax.all_to_all(
        blocks,
        "dp",
        split_axis=0,
        concat_axis=0,
        tiled=True,
        axis_index_groups=ring_groups(names, ["y", "x", "l", "c"]),
    )


def gather(block, names):
    count = math.prod(grid_sizes[name] for name in names)
    return exchange(jnp.broadcast_to(block[None], (count,) + block.shape), names)


def core_swap(array):
    return lax.ppermute(array, "dp", [(place, place ^ 1) for place in range(64)])


def tensor_swap(array):
    return lax.ppermute(array, "tensor", [(0, 1), (1, 0)])


def by_core(core, even, odd):
    return jnp.where(core == 0, even, odd)


def pair_split(core, array, axis):
    first, second = jnp.split(array, 2, axis=axis)
    return by_core(core, first, second), by_core(core, second, first)


def pair_join(core, mine, other, axis):
    return by_core(
        core,
        jnp.concatenate([mine, other], axis=axis),
        jnp.concatenate([other, mine], axis=axis),
    )


def gather_rows(core, shard):
    mine, other = pair_split(core, shard, 1)
    pair_rows = pair_join(core, mine, core_swap(other), 0)
    rows = pair_rows.shape[0]
    columns = pair_rows.shape[1]
    plane = gather(pair_rows, ("x", "l")).reshape(8 * rows, columns)
    whole = gather(plane, ("y",)).reshape(32 * rows, columns)
    return whole, core_swap(whole)


def scatter_rows(core, grads_b, count):
    blocks = exchange(grads_b.reshape(32, 24, count * 1), ("y", "x", "l"))
    summed = jnp.sum(blocks.astype(jnp.float32), axis=0)
    mine, other = pair_split(core, summed, 0)
    return mine, core_swap(other)


def half_join(core, mine, other, widths):
    out = []
    start = 0
    for width in widths:
        out.append(
            pair_join(core, mine[:, start : start + width], other[:, start : start + width], 1)
        )
        start += width
    return out


def newton_rows(current, row_start, row_count, col_start, col_count):
    for repeat in range(4):
        current = newton_step(
            current, jnp.dot(current, current.T, preferred_element_type=jnp.float32)
        )
    square = jnp.dot(current, current.T, preferred_element_type=jnp.float32).astype(jnp.bfloat16)
    few = lax.dynamic_slice_in_dim(square, row_start, row_count, 0)
    poly_term = (
        coef_b * few.astype(jnp.float32)
        + coef_c * jnp.dot(few, square, preferred_element_type=jnp.float32)
    ).astype(jnp.bfloat16)
    part = lax.dynamic_slice_in_dim(current, col_start, col_count, 1)
    own = lax.dynamic_slice_in_dim(part, row_start, row_count, 0)
    return (
        coef_a * own.astype(jnp.float32)
        + jnp.dot(poly_term, part, preferred_element_type=jnp.float32)
    ).astype(jnp.bfloat16)


def owner_update(slots_b, plane_place, tensor_place):
    columns = slots_b.shape[2]
    own_rows = exchange(slots_b, ("x",)).reshape(48, columns)
    mine = gather(own_rows, ("t", "y", "l")).reshape(2, 384, columns)
    other = core_swap(mine)
    whole = jnp.concatenate(
        [
            jnp.concatenate([mine[0], mine[1]], axis=1),
            jnp.concatenate([other[0], other[1]], axis=1),
        ],
        axis=0,
    )
    wide = whole.astype(jnp.float32)
    norm_value = jnp.sqrt(jnp.sum(wide * wide))
    current = (wide / (norm_value + 1e-07)).astype(jnp.bfloat16)
    rows = newton_rows(current, plane_place * 48, 48, tensor_place * columns, columns)
    return exchange(rows.reshape(4, 12, columns), ("x",))


def score_table(query_b, key_b, cum_decay, allowed, inv_root):
    raw_scores = (
        jnp.einsum("ihd,jhd->hij", query_b, key_b, preferred_element_type=jnp.float32) * inv_root
    )
    raw_scores = raw_scores + cum_decay.T[:, :, None] - cum_decay.T[:, None, :]
    return jnp.where(allowed[None], raw_scores, -1e30)


def on_device(
    tokens,
    cotangent,
    segment_ids,
    live_len,
    w_square,
    w_wide,
    norm_gain,
    qk_gain,
    forget_w,
    forget_b,
    m_square,
    m_wide,
    m_norm,
    m_qk,
    m_forget_w,
    m_forget_b,
    ema_square,
    ema_wide,
):
    tok_rows = tokens.shape[0]
    dp_size = lax.axis_size("dp")
    tensor_size = lax.axis_size("tensor")
    shard_rows = w_square.shape[1]
    half_width = w_square.shape[2]
    half_hidden = w_wide.shape[2]
    head_local = forget_w.shape[1]
    head_dim = qk_gain.shape[1]
    full_width = shard_rows * dp_size
    full_hidden = half_hidden * tensor_size
    total_tokens = tok_rows * dp_size
    inv_root = 1.0 / math.sqrt(head_dim)
    my_place = lax.axis_index("dp")
    tensor_place = lax.axis_index("tensor")
    core = my_place % 2
    plane_place = (my_place // 16) * 2 + (my_place // 2) % 2
    quarter_hidden = half_hidden // 2
    quarter_width = half_width // 2

    square_b = w_square.astype(jnp.bfloat16)
    wide_b = w_wide.astype(jnp.bfloat16)
    extras = jnp.concatenate(
        [
            norm_gain.astype(jnp.bfloat16).T,
            forget_w.astype(jnp.bfloat16),
            jnp.zeros((shard_rows, 120), jnp.bfloat16),
        ],
        axis=1,
    )
    first_shard = jnp.concatenate(
        [square_b[0], square_b[1], extras, square_b[4, :, :128]]
        + [square_b[2], square_b[3], square_b[4, :, 128:]],
        axis=1,
    )
    first_mine, first_other = gather_rows(core, first_shard)
    first_even = by_core(core, first_mine, first_other)
    first_odd = by_core(core, first_other, first_mine)
    second_shard = jnp.concatenate(
        [wide_b[0], wide_b[2, :, :quarter_hidden], wide_b[1], wide_b[2, :, quarter_hidden:]],
        axis=1,
    )
    second_mine, second_other = gather_rows(core, second_shard)
    second_even = by_core(core, second_mine, second_other)
    second_odd = by_core(core, second_other, second_mine)
    gath_qk = first_even[:, : 2 * half_width]
    gath_ext = first_even[:, 2 * half_width : 2 * half_width + 128]
    gath_vg = first_odd[:, : 2 * half_width]
    gath_out = jnp.concatenate(
        [first_even[:, 2 * half_width + 128 :], first_odd[:, 2 * half_width :]], axis=1
    )
    gath_gate = second_even[:, :half_hidden]
    gath_up = second_odd[:, :half_hidden]
    gath_down = jnp.concatenate([second_even[:, half_hidden:], second_odd[:, half_hidden:]], axis=1)
    gath_forget = gath_ext[:, 2 : 2 + head_local]

    gain_one = gath_ext[:, 0].astype(jnp.float32)
    gain_two = gath_ext[:, 1].astype(jnp.float32)
    qk_gains = lax.optimization_barrier(qk_gain.astype(jnp.bfloat16)).astype(jnp.float32)
    bias_row = lax.optimization_barrier(forget_b.astype(jnp.bfloat16)).astype(jnp.float32)
    positions = jnp.arange(tok_rows)
    live_count = live_len[0]
    doc_ids = segment_ids[0]
    allowed = (doc_ids[:, None] == doc_ids[None, :]) & (positions[None, :] <= positions[:, None])
    allowed = allowed & (
        (positions[None, :] < live_count) | (positions[None, :] == positions[:, None])
    )
    live_mask = (positions < live_count).astype(jnp.float32)[:, None]
    grad_out = cotangent.astype(jnp.float32) * live_mask
    grad_out_b = grad_out.astype(jnp.bfloat16)
    grad_out_pair = jnp.concatenate([grad_out_b, core_swap(grad_out_b)], axis=0)

    def qk_norm(flat, scale_row):
        return rms_norm(flat.reshape(tok_rows, head_local, head_dim), scale_row)

    def pair_tokens(array):
        return jnp.concatenate([array, core_swap(array)], axis=0)

    def pair_columns(arrays):
        halves = [pair_split(core, array, 1) for array in arrays]
        mine = jnp.concatenate([half[0] for half in halves], axis=1)
        other = jnp.concatenate([half[1] for half in halves], axis=1)
        return jnp.concatenate([mine, core_swap(other)], axis=0)

    def weight_grad(left, right):
        return jnp.dot(left.T, right, preferred_element_type=jnp.float32).astype(jnp.bfloat16)

    hidden_in = tokens.astype(jnp.float32)
    normed_one_b = rms_norm(hidden_in, gain_one).astype(jnp.bfloat16)
    normed_one_pair = pair_tokens(normed_one_b)
    proj_qk = jnp.dot(normed_one_b, gath_qk, preferred_element_type=jnp.float32)
    proj_vg = jnp.dot(normed_one_b, gath_vg, preferred_element_type=jnp.float32)
    forget_logit = jnp.dot(normed_one_b, gath_forget, preferred_element_type=jnp.float32) + bias_row
    query_raw = proj_qk[:, :half_width]
    key_raw = proj_qk[:, half_width:]
    value_heads = proj_vg[:, :half_width].astype(jnp.bfloat16)
    value_heads = value_heads.reshape(tok_rows, head_local, head_dim)
    gate_raw = proj_vg[:, half_width:]
    query_b = qk_norm(query_raw, qk_gains[0]).astype(jnp.bfloat16)
    key_b = qk_norm(key_raw, qk_gains[1]).astype(jnp.bfloat16)
    cum_decay = jnp.cumsum(jax.nn.log_sigmoid(forget_logit), axis=0)
    scores = score_table(query_b, key_b, cum_decay, allowed, inv_root)
    peak = jnp.max(scores, axis=-1, keepdims=True)
    log_total = peak + jnp.log(jnp.sum(jnp.exp(scores - peak), axis=-1, keepdims=True))
    probs = jnp.exp(scores - log_total)
    probs_b = probs.astype(jnp.bfloat16)
    attended = jnp.einsum(
        "hij,jhd->ihd", probs_b, value_heads, preferred_element_type=jnp.float32
    ).reshape(tok_rows, half_width)
    gate_sig = jax.nn.sigmoid(gate_raw)
    gated_b = (attended * gate_sig).astype(jnp.bfloat16)
    gated_pair = pair_columns([gated_b])
    attn_part = jnp.dot(gated_b, gath_out.T, preferred_element_type=jnp.float32)
    attn_part = attn_part.astype(jnp.bfloat16)
    attn_out = attn_part.astype(jnp.float32) + tensor_swap(attn_part).astype(jnp.float32)
    middle = hidden_in + attn_out
    normed_two_b = rms_norm(middle, gain_two).astype(jnp.bfloat16)
    normed_two_pair = pair_tokens(normed_two_b)
    gate_part = jnp.dot(normed_two_b, gath_gate, preferred_element_type=jnp.float32)
    up_part = jnp.dot(normed_two_b, gath_up, preferred_element_type=jnp.float32)
    activated = swiglu(gate_part, up_part).astype(jnp.bfloat16)
    mlp_part = jnp.dot(activated, gath_down.T, preferred_element_type=jnp.float32)
    mlp_part = mlp_part.astype(jnp.bfloat16)
    grad_act = jnp.dot(grad_out_b, gath_down, preferred_element_type=jnp.float32)
    unused_out, swiglu_back = jax.vjp(swiglu, gate_part, up_part)
    grad_gate, grad_up = swiglu_back(grad_act)
    grad_gate_b = grad_gate.astype(jnp.bfloat16)
    grad_up_b = grad_up.astype(jnp.bfloat16)
    grad_norm_two = jnp.dot(
        grad_gate_b, gath_gate.T, preferred_element_type=jnp.float32
    ) + jnp.dot(grad_up_b, gath_up.T, preferred_element_type=jnp.float32)
    grad_norm_two = grad_norm_two.astype(jnp.bfloat16)
    grad_norm_two = grad_norm_two.astype(jnp.float32) + tensor_swap(grad_norm_two).astype(
        jnp.float32
    )
    hidden_pair = pair_columns([grad_gate_b, grad_up_b, activated])
    grad_wide_b = jnp.concatenate(
        [
            weight_grad(normed_two_pair, hidden_pair[:, :half_hidden]),
            weight_grad(grad_out_pair, hidden_pair[:, half_hidden:]),
        ],
        axis=1,
    )
    wide_mine, wide_other = scatter_rows(core, grad_wide_b, 3 * quarter_hidden)
    wide_shard = jnp.stack(half_join(core, wide_mine, wide_other, [quarter_hidden] * 3))
    mom_wide = muon_decay * m_wide + wide_shard

    mlp_out = mlp_part.astype(jnp.float32) + tensor_swap(mlp_part).astype(jnp.float32)
    result = (middle + mlp_out).astype(jnp.bfloat16)
    unused_two, norm_two_back = jax.vjp(rms_norm, middle, gain_two)
    grad_mid_part, grad_gain_two = norm_two_back(grad_norm_two)
    grad_middle = grad_out + grad_mid_part
    grad_middle_b = grad_middle.astype(jnp.bfloat16)
    grad_middle_pair = pair_tokens(grad_middle_b)
    grad_gated = jnp.dot(grad_middle_b, gath_out, preferred_element_type=jnp.float32)
    grad_outw_b = weight_grad(grad_middle_pair, gated_pair)
    out_mine, out_other = scatter_rows(core, grad_outw_b, quarter_width)
    out_shard = half_join(core, out_mine, out_other, [quarter_width])[0]
    mom_out = muon_decay * m_square[4] + out_shard

    grad_att_b = (grad_gated * gate_sig).astype(jnp.bfloat16)
    grad_og_b = (grad_gated * attended * gate_sig * (1.0 - gate_sig)).astype(jnp.bfloat16)
    grad_att_heads = grad_att_b.reshape(tok_rows, head_local, head_dim)
    grad_probs = jnp.einsum(
        "ihd,jhd->hij", grad_att_heads, value_heads, preferred_element_type=jnp.float32
    )
    row_dot = jnp.sum(probs * grad_probs, axis=-1, keepdims=True)
    grad_scores_b = (probs * (grad_probs - row_dot)).astype(jnp.bfloat16)
    grad_qn_b = (
        jnp.einsum("hij,jhd->ihd", grad_scores_b, key_b, preferred_element_type=jnp.float32)
        * inv_root
    ).astype(jnp.bfloat16)
    grad_kn_b = (
        jnp.einsum("hij,ihd->jhd", grad_scores_b, query_b, preferred_element_type=jnp.float32)
        * inv_root
    ).astype(jnp.bfloat16)
    grad_value_b = (
        jnp.einsum("hij,ihd->jhd", probs_b, grad_att_heads, preferred_element_type=jnp.float32)
        .reshape(tok_rows, half_width)
        .astype(jnp.bfloat16)
    )
    grad_scores_f = grad_scores_b.astype(jnp.float32)
    grad_cum = (jnp.sum(grad_scores_f, axis=-1) - jnp.sum(grad_scores_f, axis=-2)).T
    grad_logf = jnp.flip(jnp.cumsum(jnp.flip(grad_cum, 0), axis=0), 0)
    grad_forget_b = (grad_logf * jax.nn.sigmoid(-forget_logit)).astype(jnp.bfloat16)
    unused_q, query_back = jax.vjp(qk_norm, query_raw, qk_gains[0])
    grad_query, grad_gain_q = query_back(grad_qn_b.astype(jnp.float32))
    unused_k, key_back = jax.vjp(qk_norm, key_raw, qk_gains[1])
    grad_key, grad_gain_k = key_back(grad_kn_b.astype(jnp.float32))
    grad_query_b = grad_query.astype(jnp.bfloat16)
    grad_key_b = grad_key.astype(jnp.bfloat16)
    proj_pair = pair_columns([grad_query_b, grad_key_b, grad_value_b, grad_og_b])
    grad_proj_b = weight_grad(normed_one_pair, proj_pair)
    proj_mine, proj_other = scatter_rows(core, grad_proj_b, 4 * quarter_width)
    proj_shard = jnp.stack(half_join(core, proj_mine, proj_other, [quarter_width] * 4))
    mom_proj = muon_decay * m_square[:4] + proj_shard
    mom_square = jnp.concatenate([mom_proj, mom_out[None]], axis=0)

    wide_slots = jnp.concatenate(
        [
            mom_wide.astype(jnp.bfloat16),
            jnp.pad(mom_out.astype(jnp.bfloat16), ((0, 0), (0, half_hidden - half_width)))[None],
        ],
        axis=0,
    )
    update_wide = owner_update(wide_slots, plane_place, tensor_place)
    update_proj = owner_update(mom_proj.astype(jnp.bfloat16), plane_place, tensor_place)
    update_square = jnp.concatenate([update_proj, update_wide[3:, :, :half_width]], axis=0)
    update_square = update_square.astype(jnp.float32)
    update_wide = update_wide[:3].astype(jnp.float32)

    grad_norm_one = jnp.dot(
        jnp.concatenate([grad_query_b, grad_key_b], axis=1),
        gath_qk.T,
        preferred_element_type=jnp.float32,
    )
    grad_norm_one = grad_norm_one + jnp.dot(
        jnp.concatenate([grad_value_b, grad_og_b], axis=1),
        gath_vg.T,
        preferred_element_type=jnp.float32,
    )
    grad_norm_one = grad_norm_one + jnp.dot(
        grad_forget_b, gath_forget.T, preferred_element_type=jnp.float32
    )
    grad_norm_one = grad_norm_one.astype(jnp.bfloat16)
    grad_norm_one = grad_norm_one.astype(jnp.float32) + tensor_swap(grad_norm_one).astype(
        jnp.float32
    )
    unused_one, norm_one_back = jax.vjp(rms_norm, hidden_in, gain_one)
    grad_in_part, grad_gain_one = norm_one_back(grad_norm_one)
    input_grad = grad_middle + grad_in_part

    grad_forget_w = jnp.dot(grad_forget_b.T, normed_one_b, preferred_element_type=jnp.float32)
    grad_bias = jnp.sum(grad_forget_b.astype(jnp.float32), axis=0)
    tiny_row = jnp.concatenate(
        [
            grad_gain_q,
            grad_gain_k,
            grad_bias,
            jnp.zeros((full_width - 2 * head_dim - head_local,), jnp.float32),
        ]
    )
    small = jnp.concatenate(
        [
            jnp.stack([grad_gain_one, grad_gain_two]),
            grad_forget_w,
            tiny_row[None],
            jnp.zeros((7, full_width), jnp.float32),
        ],
        axis=0,
    )
    small = small + core_swap(small)
    small = jnp.sum(gather(small, ("x", "l")), axis=0)
    small = jnp.sum(gather(small, ("y",)), axis=0)
    tiny = small[8, : 2 * head_dim + head_local]
    own_small = lax.dynamic_slice_in_dim(small, my_place * shard_rows, shard_rows, 1)
    gains_shard = own_small[:2]
    forget_shard = own_small[2 : 2 + head_local].T
    bias_total = tiny[2 * head_dim :]
    qk_part = tiny[: 2 * head_dim].reshape(2, head_dim)
    qk_total = qk_part + tensor_swap(qk_part)
    new_square = w_square - update_square
    new_wide = w_wide - math.sqrt(full_hidden / full_width) * update_wide
    new_ema_square = ema_decay * ema_square + (1.0 - ema_decay) * new_square
    new_ema_wide = ema_decay * ema_wide + (1.0 - ema_decay) * new_wide
    root_tokens = math.sqrt(total_tokens)
    mom_norm = plain_decay * m_norm + gains_shard
    mom_qk = plain_decay * m_qk + qk_total
    mom_forget_w = plain_decay * m_forget_w + forget_shard
    mom_forget_b = plain_decay * m_forget_b + bias_total
    new_norm = norm_gain - gain_rate / root_tokens * mom_norm
    new_qk = qk_gain - qk_rate / root_tokens * mom_qk
    new_forget_w = forget_w - forget_rate / root_tokens * mom_forget_w
    new_forget_b = forget_b - bias_rate / root_tokens * mom_forget_b
    return (
        result,
        input_grad,
        new_square,
        new_wide,
        new_norm,
        new_qk,
        new_forget_w,
        new_forget_b,
        mom_square,
        mom_wide,
        mom_norm,
        mom_qk,
        mom_forget_w,
        mom_forget_b,
        new_ema_square,
        new_ema_wide,
    )


def solution(mesh):
    placed = (
        P("dp", None),
        P("dp", None),
        P("dp", None),
        P("dp"),
        P(None, "dp", "tensor"),
        P(None, "dp", "tensor"),
        P(None, "dp"),
        P(),
        P("dp", "tensor"),
        P("tensor"),
        P(None, "dp", "tensor"),
        P(None, "dp", "tensor"),
        P(None, "dp"),
        P(),
        P("dp", "tensor"),
        P("tensor"),
        P(None, "dp", "tensor"),
        P(None, "dp", "tensor"),
    )
    return jax.shard_map(
        on_device,
        mesh=mesh,
        in_specs=placed,
        out_specs=(
            P("dp", None),
            P("dp", None),
            P(None, "dp", "tensor"),
            P(None, "dp", "tensor"),
            P(None, "dp"),
            P(),
            P("dp", "tensor"),
            P("tensor"),
            P(None, "dp", "tensor"),
            P(None, "dp", "tensor"),
            P(None, "dp"),
            P(),
            P("dp", "tensor"),
            P("tensor"),
            P(None, "dp", "tensor"),
            P(None, "dp", "tensor"),
        ),
        check_vma=False,
    )
```

```python
import math

import jax
import jax.numpy as jnp
from jax import lax
import numpy as np
from jax.experimental import pallas as pl
from jax.experimental.pallas import tpu as pltpu
from jax.sharding import PartitionSpec as P

epsilon = 1e-06
coef_a = 3.4445
coef_b = -4.775
coef_c = 2.0315
muon_decay = 0.95
plain_decay = 0.9
ema_decay = 0.7
gain_rate = 0.2
qk_rate = 0.05
forget_rate = 0.1
bias_rate = 0.5


grid_sizes = {"y": 4, "x": 4, "l": 2, "c": 2, "t": 2}


def ring_groups(names, over):
    order = [name for name in over if name not in names]
    table = np.arange(math.prod(grid_sizes[name] for name in over))
    table = table.reshape([grid_sizes[name] for name in over])
    table = table.transpose([over.index(name) for name in order + list(names)])
    return table.reshape(-1, math.prod(grid_sizes[name] for name in names)).tolist()


def exchange(blocks, names):
    if "t" in names:
        return lax.all_to_all(
            blocks,
            ("dp", "tensor"),
            split_axis=0,
            concat_axis=0,
            tiled=True,
            axis_index_groups=ring_groups(names, ["y", "x", "l", "c", "t"]),
        )
    return lax.all_to_all(
        blocks,
        "dp",
        split_axis=0,
        concat_axis=0,
        tiled=True,
        axis_index_groups=ring_groups(names, ["y", "x", "l", "c"]),
    )


def gather(block, names):
    count = math.prod(grid_sizes[name] for name in names)
    return exchange(jnp.broadcast_to(block[None], (count,) + block.shape), names)


def core_swap(array):
    return lax.ppermute(array, "dp", [(place, place ^ 1) for place in range(64)])


def tensor_swap(array):
    return lax.ppermute(array, "tensor", [(0, 1), (1, 0)])


def by_core(core, even, odd):
    return jnp.where(core == 0, even, odd)


def pair_split(core, array, axis):
    first, second = jnp.split(array, 2, axis=axis)
    return by_core(core, first, second), by_core(core, second, first)


def pair_join(core, mine, other, axis):
    return by_core(
        core,
        jnp.concatenate([mine, other], axis=axis),
        jnp.concatenate([other, mine], axis=axis),
    )


def gather_rows(core, shard):
    mine, other = pair_split(core, shard, 1)
    pair_rows = pair_join(core, mine, core_swap(other), 0)
    rows = pair_rows.shape[0]
    columns = pair_rows.shape[1]
    plane = gather(pair_rows, ("x", "l")).reshape(8 * rows, columns)
    whole = gather(plane, ("y",)).reshape(32 * rows, columns)
    return whole, core_swap(whole)


def scatter_rows(core, grads_b, count):
    blocks = exchange(grads_b.reshape(32, 24, count * 1), ("y", "x", "l"))
    summed = jnp.sum(blocks.astype(jnp.float32), axis=0)
    mine, other = pair_split(core, summed, 0)
    return mine, core_swap(other)


def half_join(core, mine, other, widths):
    out = []
    start = 0
    for width in widths:
        out.append(
            pair_join(core, mine[:, start : start + width], other[:, start : start + width], 1)
        )
        start += width
    return out


def dot_nn(left, right):
    return jnp.dot(left, right, preferred_element_type=jnp.float32)


def dot_nt(left, right):
    return lax.dot_general(
        left, right, (((1,), (1,)), ((), ())), preferred_element_type=jnp.float32
    )


def dot_tn(left, right):
    return lax.dot_general(
        left, right, (((0,), (0,)), ((), ())), preferred_element_type=jnp.float32
    )


def three_parts(value):
    high = value.astype(jnp.bfloat16)
    rest = value - high.astype(jnp.float32)
    middle = rest.astype(jnp.bfloat16)
    low = (rest - middle.astype(jnp.float32)).astype(jnp.bfloat16)
    return high, middle, low


def exact_nn(ones, value):
    high, middle, low = three_parts(value)
    return dot_nn(ones, high) + dot_nn(ones, middle) + dot_nn(ones, low)


def gain_rows(ext):
    rows = lax.broadcasted_iota(jnp.int32, (16, 128), 0)
    columns = lax.broadcasted_iota(jnp.int32, (16, 128), 1)
    pick = (columns == rows + 6).astype(jnp.float32).astype(jnp.bfloat16)
    return dot_nt(pick, ext)


def head_mask(rows, head):
    lanes = lax.broadcasted_iota(jnp.int32, (rows, 128), 1)
    return (lanes // 64) == head


def lane_pick(array, lane):
    lanes = lax.broadcasted_iota(jnp.int32, array.shape, 1)
    return jnp.sum(jnp.where(lanes == lane, array, 0.0), axis=1, keepdims=True)


def pair_rms(raw, gain):
    first = head_mask(raw.shape[0], 0)
    square = raw * raw
    sum_first = jnp.sum(jnp.where(first, square, 0.0), axis=1, keepdims=True)
    sum_second = jnp.sum(jnp.where(first, 0.0, square), axis=1, keepdims=True)
    mean = jnp.where(first, sum_first, sum_second) * (1.0 / 64.0)
    scale = lax.rsqrt(mean + epsilon)
    return raw * scale * gain, scale


def block_scores(query, keys, decay_col, decay_row, allowed, inv_root):
    raw = dot_nt(query, keys) * inv_root + decay_col - decay_row
    return jnp.where(allowed, raw, -1e30)


def allowed_block(doc_col, doc_row, live_count, start, rows, columns):
    queries = start + lax.broadcasted_iota(jnp.int32, (rows, columns), 0)
    keys = lax.broadcasted_iota(jnp.int32, (rows, columns), 1)
    same = doc_col == doc_row
    return same & (keys <= queries) & ((keys < live_count) | (keys == queries))


def load_halves(mine_ref, other_ref, held, sems):
    core = lax.rem(lax.axis_index("dp"), 2)
    first = pltpu.make_async_copy(mine_ref, held.at[core], sems.at[0])
    second = pltpu.make_async_copy(other_ref, held.at[1 - core], sems.at[1])
    first.start()
    second.start()
    return core, first, second


def attend_kernel(
    live_ref,
    tokens_ref,
    mine_ref,
    other_ref,
    gains_ref,
    bias_ref,
    doc_col_ref,
    doc_row_ref,
    normed_ref,
    query_raw_ref,
    key_raw_ref,
    query_ref,
    key_ref,
    value_ref,
    gate_ref,
    attended_ref,
    gated_ref,
    part_ref,
    logit_ref,
    decay_ref,
    total_ref,
    held,
    sems,
):
    core, first_copy, second_copy = load_halves(mine_ref, other_ref, held, sems)
    live_count = live_ref[0]
    inv_root = 0.125
    hidden = tokens_ref[...].astype(jnp.float32)
    scale = lax.rsqrt(jnp.mean(hidden * hidden, axis=1, keepdims=True) + epsilon)
    first_copy.wait()
    second_copy.wait()
    ext = held[0, :, 768:896]
    gains = gain_rows(ext)
    normed = (hidden * scale * gains[0:1]).astype(jnp.bfloat16)
    normed_ref[...] = normed
    for block in range(3):
        lanes = slice(block * 128, block * 128 + 128)
        query_raw = dot_nn(normed, held[0, :, block * 128 : block * 128 + 128])
        key_raw = dot_nn(normed, held[0, :, 384 + block * 128 : 512 + block * 128])
        query_raw_ref[:, lanes] = query_raw
        key_raw_ref[:, lanes] = key_raw
        query_ref[:, lanes] = pair_rms(query_raw, gains_ref[0:1])[0].astype(jnp.bfloat16)
        key_ref[:, lanes] = pair_rms(key_raw, gains_ref[1:2])[0].astype(jnp.bfloat16)
    value_ref[...] = dot_nn(normed, held[1, :, 0:384]).astype(jnp.bfloat16)
    gate_ref[...] = dot_nn(normed, held[1, :, 384:768])
    lane = lax.broadcasted_iota(jnp.int32, (384, 128), 1)
    logit = dot_nn(normed, ext) + bias_ref[...]
    logit = jnp.where(lane < 6, logit, 0.0)
    logit_ref[...] = logit
    log_sig = jnp.minimum(logit, 0.0) - jnp.log1p(jnp.exp(-jnp.abs(logit)))
    rows = lax.broadcasted_iota(jnp.int32, (384, 384), 0)
    columns = lax.broadcasted_iota(jnp.int32, (384, 384), 1)
    lower = (columns <= rows).astype(jnp.float32).astype(jnp.bfloat16)
    decay = exact_nn(lower, log_sig)
    decay_ref[...] = decay
    decay_t = decay.T
    for step in range(3):
        begin, count = step * 128, step * 128 + 128
        allowed = allowed_block(
            doc_col_ref[begin : begin + 128, :],
            doc_row_ref[:, 0:count],
            live_count,
            begin,
            128,
            count,
        )
        totals = jnp.zeros((128, 128), jnp.float32)
        small_lane = lax.broadcasted_iota(jnp.int32, (128, 128), 1)
        for block in range(3):
            lanes = slice(block * 128, block * 128 + 128)
            keys = key_ref[0:count, lanes]
            values = value_ref[0:count, lanes]
            query_pair = query_ref[begin : begin + 128, lanes]
            outs = []
            for half in range(2):
                head = block * 2 + half
                query = jnp.where(head_mask(128, half), query_pair, jnp.zeros_like(query_pair))
                scores = block_scores(
                    query,
                    keys,
                    lane_pick(decay[begin : begin + 128], head),
                    decay_t[head : head + 1, 0:count],
                    allowed,
                    inv_root,
                )
                peak = jnp.max(scores, axis=1, keepdims=True)
                grown = jnp.exp(scores - peak)
                total = jnp.sum(grown, axis=1, keepdims=True)
                totals = jnp.where(small_lane == head, peak + jnp.log(total), totals)
                probs = (grown * (1.0 / total)).astype(jnp.bfloat16)
                outs.append(dot_nn(probs, values))
            attended_ref[begin : begin + 128, lanes] = jnp.where(
                head_mask(128, 0), outs[0], outs[1]
            )
        total_ref[begin : begin + 128, :] = totals
    gated = (attended_ref[...] * jax.nn.sigmoid(gate_ref[...])).astype(jnp.bfloat16)
    gated_ref[core] = gated[:, 0:256]
    gated_ref[1 - core] = gated[:, 128:384]
    part = dot_nt(gated[:, 0:128], held[0, :, 896:1024]) + dot_nt(
        gated[:, 128:384], held[1, :, 768:1024]
    )
    part_ref[...] = part.astype(jnp.bfloat16)


def mlp_kernel(
    live_ref,
    tokens_ref,
    part_ref,
    peer_ref,
    cotangent_ref,
    ext_ref,
    mine_ref,
    other_ref,
    middle_ref,
    normed_ref,
    hidden_ref,
    out_ref,
    grad_ref,
    held,
    sems,
):
    core, first_copy, second_copy = load_halves(mine_ref, other_ref, held, sems)
    middle = tokens_ref[...].astype(jnp.float32) + (
        part_ref[...].astype(jnp.float32) + peer_ref[...].astype(jnp.float32)
    )
    middle_ref[...] = middle
    gains = gain_rows(ext_ref[...])
    scale = lax.rsqrt(jnp.mean(middle * middle, axis=1, keepdims=True) + epsilon)
    normed = (middle * scale * gains[1:2]).astype(jnp.bfloat16)
    normed_ref[...] = normed
    live_rows = lax.broadcasted_iota(jnp.int32, (384, 1), 0) < live_ref[0]
    grad_out = jnp.where(live_rows, cotangent_ref[...].astype(jnp.float32), 0.0)
    grad_out = grad_out.astype(jnp.bfloat16)
    first_copy.wait()
    second_copy.wait()
    out_total = jnp.zeros((384, 768), jnp.float32)
    grad_total = jnp.zeros((384, 768), jnp.float32)
    for half in range(2):
        slot = jnp.where(core == half, 0, 1)
        begin = half * 512
        gate_w = held[0, :, begin : begin + 512]
        up_w = held[1, :, begin : begin + 512]
        down_w = held[half, :, 1024:1536]
        gate = dot_nn(normed, gate_w)
        up = dot_nn(normed, up_w)
        sig = jax.nn.sigmoid(gate)
        silu = gate * sig
        active = (silu * up).astype(jnp.bfloat16)
        hidden_ref[slot, :, 1024:1536] = active
        out_total = out_total + dot_nt(active, down_w)
        grad_act = dot_nn(grad_out, down_w)
        grad_up = (grad_act * silu).astype(jnp.bfloat16)
        grad_gate = (grad_act * up * (sig * (1.0 + gate * (1.0 - sig)))).astype(jnp.bfloat16)
        hidden_ref[slot, :, 0:512] = grad_gate
        hidden_ref[slot, :, 512:1024] = grad_up
        grad_total = grad_total + dot_nt(grad_gate, gate_w) + dot_nt(grad_up, up_w)
    out_ref[...] = out_total.astype(jnp.bfloat16)
    grad_ref[...] = grad_total.astype(jnp.bfloat16)


def attend_back_kernel(
    live_ref,
    cotangent_ref,
    middle_ref,
    grad_part_ref,
    grad_peer_ref,
    mine_ref,
    other_ref,
    gains_ref,
    doc_col_ref,
    doc_row_ref,
    normed_ref,
    query_raw_ref,
    key_raw_ref,
    query_ref,
    key_ref,
    value_ref,
    gate_ref,
    attended_ref,
    logit_ref,
    decay_ref,
    total_ref,
    grad_middle_ref,
    grad_middle_b_ref,
    proj_ref,
    norm_part_ref,
    small_ref,
    tiny_ref,
    held,
    sems,
    grad_att_ref,
    grad_query_ref,
    grad_key_ref,
    grad_value_ref,
    column_ref,
):
    core, first_copy, second_copy = load_halves(mine_ref, other_ref, held, sems)
    live_count = live_ref[0]
    inv_root = 0.125
    middle = middle_ref[...]
    grad_normed = grad_part_ref[...].astype(jnp.float32) + grad_peer_ref[...].astype(jnp.float32)
    live_rows = lax.broadcasted_iota(jnp.int32, (384, 1), 0) < live_count
    grad_out = jnp.where(live_rows, cotangent_ref[...].astype(jnp.float32), 0.0)
    scale = lax.rsqrt(jnp.mean(middle * middle, axis=1, keepdims=True) + epsilon)
    first_copy.wait()
    second_copy.wait()
    ext = held[0, :, 768:896]
    gains = gain_rows(ext)
    gained = grad_normed * gains[1:2]
    inner = jnp.mean(gained * middle, axis=1, keepdims=True)
    grad_middle = grad_out + (scale * gained - middle * (scale * scale * scale * inner))
    grad_gain = jnp.sum(grad_normed * middle * scale, axis=0, keepdims=True)
    grad_middle_ref[...] = grad_middle
    grad_middle_b = grad_middle.astype(jnp.bfloat16)
    grad_middle_b_ref[...] = grad_middle_b
    grad_gated = jnp.concatenate(
        [
            dot_nn(grad_middle_b, held[0, :, 896:1024]),
            dot_nn(grad_middle_b, held[1, :, 768:1024]),
        ],
        axis=1,
    )
    sig = jax.nn.sigmoid(gate_ref[...])
    grad_att_ref[...] = (grad_gated * sig).astype(jnp.bfloat16)
    grad_og = (grad_gated * attended_ref[...] * sig * (1.0 - sig)).astype(jnp.bfloat16)
    proj_ref[1 - core, :, 384:768] = grad_og
    grad_key_ref[...] = jnp.zeros((384, 384), jnp.float32)
    grad_value_ref[...] = jnp.zeros((384, 384), jnp.float32)
    column_ref[...] = jnp.zeros((128, 384), jnp.float32)
    decay = decay_ref[...]
    decay_t = decay.T
    row_parts = []
    for step in range(3):
        begin, count = step * 128, step * 128 + 128
        allowed = allowed_block(
            doc_col_ref[begin : begin + 128, :],
            doc_row_ref[:, 0:count],
            live_count,
            begin,
            128,
            count,
        )
        small_lane = lax.broadcasted_iota(jnp.int32, (128, 128), 1)
        row_sums = jnp.zeros((128, 128), jnp.float32)
        for block in range(3):
            lanes = slice(block * 128, block * 128 + 128)
            keys = key_ref[0:count, lanes]
            values = value_ref[0:count, lanes]
            query_pair = query_ref[begin : begin + 128, lanes]
            att_pair = grad_att_ref[begin : begin + 128, lanes]
            outs = []
            key_outs = []
            value_outs = []
            for half in range(2):
                head = block * 2 + half
                mask = head_mask(128, half)
                query = jnp.where(mask, query_pair, jnp.zeros_like(query_pair))
                att = jnp.where(mask, att_pair, jnp.zeros_like(att_pair))
                scores = block_scores(
                    query,
                    keys,
                    lane_pick(decay[begin : begin + 128], head),
                    decay_t[head : head + 1, 0:count],
                    allowed,
                    inv_root,
                )
                probs = jnp.exp(scores - lane_pick(total_ref[begin : begin + 128, :], head))
                grad_probs = dot_nt(att, values)
                row_dot = jnp.sum(probs * grad_probs, axis=1, keepdims=True)
                grad_scores = (probs * (grad_probs - row_dot)).astype(jnp.bfloat16)
                grad_scores_f = grad_scores.astype(jnp.float32)
                row_sums = jnp.where(
                    small_lane == head,
                    jnp.sum(grad_scores_f, axis=1, keepdims=True),
                    row_sums,
                )
                column_ref[head : head + 1, 0:count] += jnp.sum(
                    grad_scores_f, axis=0, keepdims=True
                )
                outs.append(dot_nn(grad_scores, keys))
                key_outs.append(dot_tn(grad_scores, query))
                value_outs.append(dot_tn(probs.astype(jnp.bfloat16), att))
            grad_query_ref[begin : begin + 128, lanes] = jnp.where(
                head_mask(128, 0), outs[0], outs[1]
            )
            grad_key_ref[0:count, lanes] += key_outs[0] + key_outs[1]
            grad_value_ref[0:count, lanes] += value_outs[0] + value_outs[1]
        row_parts.append(row_sums)
    grad_decay = jnp.concatenate(row_parts, axis=0) - column_ref[...].T
    rows = lax.broadcasted_iota(jnp.int32, (384, 384), 0)
    columns = lax.broadcasted_iota(jnp.int32, (384, 384), 1)
    upper = (columns >= rows).astype(jnp.float32).astype(jnp.bfloat16)
    grad_logit = exact_nn(upper, grad_decay) * jax.nn.sigmoid(-logit_ref[...])
    lane = lax.broadcasted_iota(jnp.int32, (384, 128), 1)
    grad_logit = jnp.where(lane < 6, grad_logit, 0.0)
    grad_forget = grad_logit.astype(jnp.bfloat16)
    proj_ref[1 - core, :, 0:384] = grad_value_ref[...].astype(jnp.bfloat16)
    gain_sums = []
    for number, raw_ref, out_ref in (
        (0, query_raw_ref, grad_query_ref),
        (1, key_raw_ref, grad_key_ref),
    ):
        gain = gains_ref[number : number + 1]
        gain_sum = jnp.zeros((1, 128), jnp.float32)
        for block in range(3):
            lanes = slice(block * 128, block * 128 + 128)
            raw = raw_ref[:, lanes]
            grad = (out_ref[:, lanes] * inv_root).astype(jnp.bfloat16).astype(jnp.float32)
            first = head_mask(384, 0)
            scaled = pair_rms(raw, 1.0)[1]
            weighted = grad * gain
            product = weighted * raw
            sum_first = jnp.sum(jnp.where(first, product, 0.0), axis=1, keepdims=True)
            sum_second = jnp.sum(jnp.where(first, 0.0, product), axis=1, keepdims=True)
            inner_head = jnp.where(first, sum_first, sum_second) * (1.0 / 64.0)
            gain_sum = gain_sum + jnp.sum(grad * raw * scaled, axis=0, keepdims=True)
            grad_raw = scaled * weighted - raw * (scaled * scaled * scaled * inner_head)
            proj_ref[core, :, number * 384 + block * 128 : number * 384 + block * 128 + 128] = (
                grad_raw.astype(jnp.bfloat16)
            )
        gain_sums.append(gain_sum)
    part = dot_nt(proj_ref[core], held[0, :, 0:768])
    part = part + dot_nt(proj_ref[1 - core], held[1, :, 0:768])
    part = part + dot_nt(grad_forget, ext)
    norm_part_ref[...] = part.astype(jnp.bfloat16)
    forget_rows = dot_tn(grad_forget, normed_ref[...])
    small_ref[0:8, :] = forget_rows[0:8]
    small_ref[6:7, :] = jnp.zeros((1, 768), jnp.float32)
    small_ref[7:8, :] = grad_gain
    bias_sum = jnp.sum(grad_forget.astype(jnp.float32), axis=0, keepdims=True)
    tiny_ref[0:1, :] = gain_sums[0]
    tiny_ref[1:2, :] = gain_sums[1]
    tiny_ref[2:3, :] = bias_sum
    tiny_ref[3:8, :] = jnp.zeros((5, 128), jnp.float32)


def newton_kernel(mine_ref, other_ref, out_ref, held, square_ref, poly_ref):
    columns = mine_ref.shape[2]
    total = jnp.zeros((1, 1), jnp.float32)
    for source in (mine_ref, other_ref):
        for side in range(2):
            for start in range(0, 384, 64):
                piece = source[side, start : start + 64, :].astype(jnp.float32)
                piece = jnp.sum(piece * piece, axis=0, keepdims=True)
                total = total + jnp.sum(piece, axis=1, keepdims=True)
    scale = 1.0 / (jnp.sqrt(total) + 1e-07)
    for place, source in ((0, mine_ref), (384, other_ref)):
        for side in range(2):
            for start in range(0, 384, 64):
                piece = source[side, start : start + 64, :].astype(jnp.float32) * scale
                held[0, side, place + start : place + start + 64, :] = piece.astype(jnp.bfloat16)
    for repeat in range(5):
        now, later = repeat % 2, (repeat + 1) % 2
        for start in range(0, 768, 256):
            square = dot_nt(held[now, 0, start : start + 256, :], held[now, 0])
            square = square + dot_nt(held[now, 1, start : start + 256, :], held[now, 1])
            square_ref[start : start + 256, :] = square.astype(jnp.bfloat16)
        if repeat < 4:
            for start in range(0, 768, 256):
                few = square_ref[start : start + 256, :]
                poly = coef_b * few.astype(jnp.float32) + coef_c * dot_nn(few, square_ref[...])
                poly_ref[start : start + 256, :] = poly.astype(jnp.bfloat16)
            for side in range(2):
                for start in range(0, 768, 256):
                    grown = coef_a * held[now, side, start : start + 256, :].astype(jnp.float32)
                    grown = grown + dot_nn(poly_ref[start : start + 256, :], held[now, side])
                    held[later, side, start : start + 256, :] = grown.astype(jnp.bfloat16)
        else:
            place = lax.axis_index("dp")
            plane = (place // 16) * 2 + lax.rem(place // 2, 2)
            side = lax.axis_index("tensor")
            begin = pl.multiple_of(plane * 48, 16)
            few = square_ref[pl.ds(begin, 48), :]
            poly = coef_b * few.astype(jnp.float32) + coef_c * dot_nn(few, square_ref[...])
            poly = poly.astype(jnp.bfloat16)
            grown = coef_a * held[now, side, pl.ds(begin, 48), :].astype(jnp.float32)
            grown = grown + dot_nn(poly, held[now, side])
            out_ref[...] = grown.astype(jnp.bfloat16)


in_vmem = pl.BlockSpec(memory_space=pltpu.VMEM)
in_smem = pl.BlockSpec(memory_space=pltpu.SMEM)
in_any = pl.BlockSpec(memory_space=pl.ANY)


def call_kernel(kernel, in_specs, outs, scratch, flops, limit=48):
    return pl.pallas_call(
        kernel,
        out_shape=[jax.ShapeDtypeStruct(shape, dtype) for shape, dtype in outs],
        in_specs=in_specs,
        out_specs=[in_vmem] * len(outs),
        scratch_shapes=scratch,
        compiler_params=pltpu.CompilerParams(vmem_limit_bytes=limit * 1024 * 1024),
        cost_estimate=pl.CostEstimate(flops=flops, bytes_accessed=10000000, transcendentals=0),
    )


def owner_update(slots_b):
    columns = slots_b.shape[2]
    own_rows = exchange(slots_b, ("x",)).reshape(48, columns)
    mine = gather(own_rows, ("t", "y", "l")).reshape(2, 384, columns)
    other = core_swap(mine)
    rows = call_kernel(
        newton_kernel,
        [in_vmem] * 2,
        [((48, columns), jnp.bfloat16)],
        [
            pltpu.VMEM((2, 2, 768, columns), jnp.bfloat16),
            pltpu.VMEM((768, 768), jnp.bfloat16),
            pltpu.VMEM((768, 768), jnp.bfloat16),
        ],
        10 * 768 * 768 * (4 * columns + 768),
    )(mine, other)[0]
    return exchange(rows.reshape(4, 12, columns), ("x",))


def on_device(
    tokens,
    cotangent,
    segment_ids,
    live_len,
    w_square,
    w_wide,
    norm_gain,
    qk_gain,
    forget_w,
    forget_b,
    m_square,
    m_wide,
    m_norm,
    m_qk,
    m_forget_w,
    m_forget_b,
    ema_square,
    ema_wide,
):
    half_width = w_square.shape[2]
    half_hidden = w_wide.shape[2]
    shard_rows = w_square.shape[1]
    head_local = forget_w.shape[1]
    head_dim = qk_gain.shape[1]
    dp_size = lax.axis_size("dp")
    full_width = shard_rows * dp_size
    full_hidden = half_hidden * lax.axis_size("tensor")
    total_tokens = tokens.shape[0] * dp_size
    my_place = lax.axis_index("dp")
    core = my_place % 2
    quarter_hidden = half_hidden // 2
    bf16, f32 = jnp.bfloat16, jnp.float32

    square_b = w_square.astype(bf16)
    wide_b = w_wide.astype(bf16)
    extras = jnp.concatenate(
        [
            forget_w.astype(bf16),
            norm_gain.astype(bf16).T,
            jnp.zeros((shard_rows, 120), bf16),
        ],
        axis=1,
    )
    first_shard = jnp.concatenate(
        [square_b[0], square_b[1], extras, square_b[4, :, :128]]
        + [square_b[2], square_b[3], square_b[4, :, 128:]],
        axis=1,
    )
    first_mine, first_other = gather_rows(core, first_shard)
    second_shard = jnp.concatenate(
        [wide_b[0], wide_b[2, :, :quarter_hidden], wide_b[1], wide_b[2, :, quarter_hidden:]],
        axis=1,
    )
    second_shard, first_mine = lax.optimization_barrier((second_shard, first_mine))
    second_mine, second_other = gather_rows(core, second_shard)
    ext = by_core(core, first_mine[:, 768:896], first_other[:, 768:896])

    gains_b = qk_gain.astype(bf16).astype(f32)
    gains = jnp.concatenate([gains_b, gains_b], axis=1)
    bias_row = jnp.pad(forget_b.astype(bf16).astype(f32), (0, 128 - head_local))[None]
    doc_row = segment_ids
    doc_col = segment_ids.reshape(-1, 1)
    live_mask = (jnp.arange(tokens.shape[0]) < live_len[0])[:, None]
    grad_out_b = jnp.where(live_mask, cotangent, jnp.zeros_like(cotangent))

    square_f = ((384, 384), f32)
    square_h = ((384, 384), bf16)
    lane_f = ((384, 128), f32)
    token_h = ((384, 768), bf16)
    token_f = ((384, 768), f32)
    (
        normed_one,
        query_raw,
        key_raw,
        query_b,
        key_b,
        value_b,
        gate_raw,
        attended,
        gated,
        attn_part,
        logit,
        decay,
        log_total,
    ) = call_kernel(
        attend_kernel,
        [in_smem, in_vmem, in_any, in_any] + [in_vmem] * 4,
        [token_h, square_f, square_f, square_h, square_h, square_h, square_f, square_f]
        + [((2, 384, 256), bf16), token_h, lane_f, lane_f, lane_f],
        [pltpu.VMEM((2, 768, 1024), bf16), pltpu.SemaphoreType.DMA((2,))],
        4000000000,
    )(live_len, tokens, first_mine, first_other, gains, bias_row, doc_col, doc_row)
    attn_peer = tensor_swap(attn_part)
    middle, normed_two, hidden, mlp_part, grad_part = call_kernel(
        mlp_kernel,
        [in_smem] + [in_vmem] * 5 + [in_any] * 2,
        [token_f, token_h, ((2, 384, 1536), bf16), token_h, token_h],
        [pltpu.VMEM((2, 768, 1536), bf16), pltpu.SemaphoreType.DMA((2,))],
        5000000000,
    )(live_len, tokens, attn_part, attn_peer, cotangent, ext, second_mine, second_other)
    grad_peer = tensor_swap(grad_part)

    def pair_tokens(mine, other):
        return jnp.concatenate([mine, core_swap(other)], axis=0)

    def weight_grad(left, right):
        return jnp.dot(left.T, right, preferred_element_type=f32).astype(bf16)

    normed_two_pair = pair_tokens(normed_two, normed_two)
    hidden_pair = pair_tokens(hidden[0], hidden[1])
    grad_out_pair = pair_tokens(grad_out_b, grad_out_b)
    grad_wide_b = jnp.concatenate(
        [
            weight_grad(normed_two_pair, hidden_pair[:, :half_hidden]),
            weight_grad(grad_out_pair, hidden_pair[:, half_hidden:]),
        ],
        axis=1,
    )
    wide_mine, wide_other = scatter_rows(core, grad_wide_b, 3 * quarter_hidden)
    wide_shard = jnp.stack(half_join(core, wide_mine, wide_other, [quarter_hidden] * 3))
    mom_wide = muon_decay * m_wide + wide_shard

    (
        grad_middle,
        grad_middle_b,
        proj,
        norm_part,
        small_rows,
        tiny_rows,
    ) = call_kernel(
        attend_back_kernel,
        [in_smem] + [in_vmem] * 4 + [in_any] * 2 + [in_vmem] * 14,
        [token_f, token_h, ((2, 384, 768), bf16), token_h]
        + [((8, 768), f32), ((8, 128), f32)],
        [
            pltpu.VMEM((2, 768, 1024), bf16),
            pltpu.SemaphoreType.DMA((2,)),
            pltpu.VMEM((384, 384), bf16),
            pltpu.VMEM((384, 384), f32),
            pltpu.VMEM((384, 384), f32),
            pltpu.VMEM((384, 384), f32),
            pltpu.VMEM((128, 384), f32),
        ],
        6000000000,
    )(
        live_len,
        cotangent,
        middle,
        grad_part,
        grad_peer,
        first_mine,
        first_other,
        gains,
        doc_col,
        doc_row,
        normed_one,
        query_raw,
        key_raw,
        query_b,
        key_b,
        value_b,
        gate_raw,
        attended,
        logit,
        decay,
        log_total,
    )
    proj_pair = pair_tokens(proj[0], proj[1])
    normed_one_pair = pair_tokens(normed_one, normed_one)
    gated_pair = pair_tokens(gated[0], gated[1])
    grad_middle_pair = pair_tokens(grad_middle_b, grad_middle_b)
    grad_proj_b = jnp.concatenate(
        [weight_grad(normed_one_pair, proj_pair), weight_grad(grad_middle_pair, gated_pair)],
        axis=1,
    )
    blocks = exchange(grad_proj_b.reshape(32, 24, 1024), ("y", "x", "l"))
    summed = jnp.sum(blocks.astype(f32), axis=0)
    mine, other = pair_split(core, summed, 0)
    other = core_swap(other)
    even = by_core(core, mine, other)
    odd = by_core(core, other, mine)
    square_shard = jnp.stack(
        [
            even[:, :384],
            even[:, 384:768],
            odd[:, :384],
            odd[:, 384:768],
            jnp.concatenate([even[:, 768:1024], odd[:, 896:1024]], axis=1),
        ]
    )
    mom_square = muon_decay * m_square + square_shard

    wide_slots = jnp.concatenate(
        [
            mom_wide.astype(bf16),
            jnp.pad(mom_square[4].astype(bf16), ((0, 0), (0, half_hidden - half_width)))[None],
        ],
        axis=0,
    )
    update_proj = owner_update(mom_square[:4].astype(bf16))
    update_wide = owner_update(wide_slots)
    update_square = jnp.concatenate([update_proj, update_wide[3:, :, :half_width]], axis=0)
    update_square = update_square.astype(f32)
    update_wide = update_wide[:3].astype(f32)

    mlp_part, norm_part, blocks = lax.optimization_barrier((mlp_part, norm_part, blocks))
    norm_peer = tensor_swap(norm_part)
    mlp_part, norm_peer = lax.optimization_barrier((mlp_part, norm_peer))
    mlp_out = mlp_part.astype(f32) + tensor_swap(mlp_part).astype(f32)
    result = (middle + mlp_out).astype(bf16)
    hidden_in = tokens.astype(f32)
    gain_one = ext[:, head_local].astype(f32)[None]
    grad_norm_one = norm_part.astype(f32) + norm_peer.astype(f32)
    scale = lax.rsqrt(jnp.mean(hidden_in * hidden_in, axis=1, keepdims=True) + epsilon)
    gained = grad_norm_one * gain_one
    inner = jnp.mean(gained * hidden_in, axis=1, keepdims=True)
    input_grad = grad_middle + (scale * gained - hidden_in * (scale * scale * scale * inner))
    grad_gain_one = jnp.sum(grad_norm_one * hidden_in * scale, axis=0)

    tiny_row = jnp.concatenate(
        [
            tiny_rows[:2, :head_dim] + tiny_rows[:2, head_dim:],
            jnp.pad(tiny_rows[2:3, :head_local], ((0, 0), (0, head_dim - head_local))),
        ],
        axis=0,
    ).reshape(1, -1)
    tiny_row = jnp.pad(tiny_row, ((0, 7), (0, full_width - 3 * head_dim)))
    small_rows = jnp.concatenate(
        [small_rows[:6], grad_gain_one[None], small_rows[7:], tiny_row], axis=0
    )
    small = small_rows + core_swap(small_rows)
    small = jnp.sum(gather(small, ("x", "l")), axis=0)
    small = jnp.sum(gather(small, ("y",)), axis=0)
    own_small = lax.dynamic_slice_in_dim(small, my_place * shard_rows, shard_rows, 1)
    gains_shard = own_small[6:8]
    forget_shard = own_small[:head_local].T
    bias_total = small[8, 2 * head_dim : 2 * head_dim + head_local]
    qk_part = small[8, : 2 * head_dim].reshape(2, head_dim)
    qk_total = qk_part + tensor_swap(qk_part)
    new_square = w_square - update_square
    new_wide = w_wide - math.sqrt(full_hidden / full_width) * update_wide
    new_ema_square = ema_decay * ema_square + (1.0 - ema_decay) * new_square
    new_ema_wide = ema_decay * ema_wide + (1.0 - ema_decay) * new_wide
    root_tokens = math.sqrt(total_tokens)
    mom_norm = plain_decay * m_norm + gains_shard
    mom_qk = plain_decay * m_qk + qk_total
    mom_forget_w = plain_decay * m_forget_w + forget_shard
    mom_forget_b = plain_decay * m_forget_b + bias_total
    new_norm = norm_gain - gain_rate / root_tokens * mom_norm
    new_qk = qk_gain - qk_rate / root_tokens * mom_qk
    new_forget_w = forget_w - forget_rate / root_tokens * mom_forget_w
    new_forget_b = forget_b - bias_rate / root_tokens * mom_forget_b
    return (
        result,
        input_grad,
        new_square,
        new_wide,
        new_norm,
        new_qk,
        new_forget_w,
        new_forget_b,
        mom_square,
        mom_wide,
        mom_norm,
        mom_qk,
        mom_forget_w,
        mom_forget_b,
        new_ema_square,
        new_ema_wide,
    )


def solution(mesh):
    placed = (
        P("dp", None),
        P("dp", None),
        P("dp", None),
        P("dp"),
        P(None, "dp", "tensor"),
        P(None, "dp", "tensor"),
        P(None, "dp"),
        P(),
        P("dp", "tensor"),
        P("tensor"),
        P(None, "dp", "tensor"),
        P(None, "dp", "tensor"),
        P(None, "dp"),
        P(),
        P("dp", "tensor"),
        P("tensor"),
        P(None, "dp", "tensor"),
        P(None, "dp", "tensor"),
    )
    return jax.shard_map(
        on_device,
        mesh=mesh,
        in_specs=placed,
        out_specs=(
            P("dp", None),
            P("dp", None),
            P(None, "dp", "tensor"),
            P(None, "dp", "tensor"),
            P(None, "dp"),
            P(),
            P("dp", "tensor"),
            P("tensor"),
            P(None, "dp", "tensor"),
            P(None, "dp", "tensor"),
            P(None, "dp"),
            P(),
            P("dp", "tensor"),
            P("tensor"),
            P(None, "dp", "tensor"),
            P(None, "dp", "tensor"),
        ),
        check_vma=False,
    )
```

```python
import functools
import math

import jax
import jax.numpy as jnp
from jax import lax
import numpy as np
from jax.experimental import pallas as pl
from jax.experimental.pallas import tpu as pltpu
from jax.sharding import PartitionSpec as P

epsilon = 1e-06
coef_a = 3.4445
coef_b = -4.775
coef_c = 2.0315
muon_decay = 0.95
plain_decay = 0.9
ema_decay = 0.7
gain_rate = 0.2
qk_rate = 0.05
forget_rate = 0.1
bias_rate = 0.5


grid_sizes = {"y": 4, "x": 4, "l": 2, "c": 2, "t": 2}
dp_names = ["y", "x", "l", "c"]


def ring_groups(names, over):
    order = [name for name in over if name not in names]
    table = np.arange(math.prod(grid_sizes[name] for name in over))
    table = table.reshape([grid_sizes[name] for name in over])
    table = table.transpose([over.index(name) for name in order + list(names)])
    return table.reshape(-1, math.prod(grid_sizes[name] for name in names)).tolist()


def exchange(blocks, names):
    axes = ("dp", "tensor") if "t" in names else "dp"
    return lax.all_to_all(
        blocks,
        axes,
        split_axis=0,
        concat_axis=0,
        tiled=True,
        axis_index_groups=ring_groups(names, dp_names + (["t"] if "t" in names else [])),
    )


def gather(block, names):
    count = math.prod(grid_sizes[name] for name in names)
    return exchange(jnp.broadcast_to(block[None], (count,) + block.shape), names)


def place_of(name):
    place = lax.axis_index("dp")
    return {"y": place // 16, "x": (place // 4) % 4, "l": (place // 2) % 2, "c": place % 2}[name]


def fetch(array, name, step):
    table = np.arange(64).reshape(4, 4, 2, 2)
    sources = np.roll(table, -step, axis=dp_names.index(name))
    pairs = [(int(a), int(b)) for a, b in zip(sources.ravel(), table.ravel())]
    return lax.ppermute(array, "dp", pairs)


def fetch_ring(array, name):
    return [array] + [fetch(array, name, step) for step in (1, 3, 2)]


ring_steps = (0, 1, 3, 2)


def core_swap(array):
    return fetch(array, "c", 1)


def tensor_swap(array):
    return lax.ppermute(array, "tensor", [(0, 1), (1, 0)])


def by_core(core, even, odd):
    return jnp.where(core == 0, even, odd)


def pair_join(place, mine, other, axis):
    return jnp.where(
        place == 0,
        jnp.concatenate([mine, other], axis=axis),
        jnp.concatenate([other, mine], axis=axis),
    )


def pair_split(core, array, axis):
    first, second = jnp.split(array, 2, axis=axis)
    return by_core(core, first, second), by_core(core, second, first)


def assemble_kernel(*refs):
    blocks, out_ref, sems = refs[:8], refs[8], refs[9]
    place = lax.axis_index("dp")
    row, column = place // 16, lax.rem(place // 4, 4)
    width = blocks[0].shape[2]
    copies = []
    for number, step in enumerate(ring_steps):
        for inner, inner_step in enumerate(ring_steps):
            for side in range(2):
                row_step, column_step = ((step, inner_step), (inner_step, step))[side]
                copy = pltpu.make_async_copy(
                    blocks[side * 4 + number].at[inner],
                    out_ref.at[
                        lax.rem(row + row_step, 4),
                        lax.rem(column + column_step, 4),
                        :,
                        pl.ds(side * width, width),
                    ],
                    sems.at[len(copies)],
                )
                copy.start()
                copies.append(copy)
    for copy in copies:
        copy.wait()


def assemble(blocks):
    width = 2 * blocks[0].shape[2]
    whole = pl.pallas_call(
        assemble_kernel,
        out_shape=jax.ShapeDtypeStruct((4, 4, 48, width), jnp.bfloat16),
        in_specs=[pl.BlockSpec(memory_space=pl.ANY)] * 8,
        out_specs=pl.BlockSpec(memory_space=pl.ANY),
        scratch_shapes=[pltpu.SemaphoreType.DMA((32,))],
        cost_estimate=pl.CostEstimate(flops=0, bytes_accessed=3000 * width, transcendentals=0),
    )(*blocks)
    return whole.reshape(768, width)

def dot_nn(left, right):
    return jnp.dot(left, right, preferred_element_type=jnp.float32)


def dot_nt(left, right):
    return lax.dot_general(
        left, right, (((1,), (1,)), ((), ())), preferred_element_type=jnp.float32
    )


def dot_tn(left, right):
    return lax.dot_general(
        left, right, (((0,), (0,)), ((), ())), preferred_element_type=jnp.float32
    )


def three_parts(value):
    high = value.astype(jnp.bfloat16)
    rest = value - high.astype(jnp.float32)
    middle = rest.astype(jnp.bfloat16)
    low = (rest - middle.astype(jnp.float32)).astype(jnp.bfloat16)
    return high, middle, low


def exact_nn(ones, value):
    high, middle, low = three_parts(value)
    return dot_nn(ones, high) + dot_nn(ones, middle) + dot_nn(ones, low)


def gain_rows(ext):
    rows = lax.broadcasted_iota(jnp.int32, (16, 128), 0)
    columns = lax.broadcasted_iota(jnp.int32, (16, 128), 1)
    pick = (columns == rows + 6).astype(jnp.float32).astype(jnp.bfloat16)
    return dot_nt(pick, ext)


def head_mask(rows, head):
    lanes = lax.broadcasted_iota(jnp.int32, (rows, 128), 1)
    return (lanes // 64) == head


def lane_pick(array, lane):
    lanes = lax.broadcasted_iota(jnp.int32, array.shape, 1)
    return jnp.sum(jnp.where(lanes == lane, array, 0.0), axis=1, keepdims=True)


def pair_rms(raw, gain):
    first = head_mask(raw.shape[0], 0)
    square = raw * raw
    sum_first = jnp.sum(jnp.where(first, square, 0.0), axis=1, keepdims=True)
    sum_second = jnp.sum(jnp.where(first, 0.0, square), axis=1, keepdims=True)
    mean = jnp.where(first, sum_first, sum_second) * (1.0 / 64.0)
    scale = lax.rsqrt(mean + epsilon)
    return raw * scale * gain, scale


def block_scores(query, keys, decay_col, decay_row, allowed, inv_root):
    raw = dot_nt(query, keys) * inv_root + decay_col - decay_row
    return jnp.where(allowed, raw, -1e30)


def allowed_block(doc_col, doc_row, live_count, start, rows, columns):
    queries = start + lax.broadcasted_iota(jnp.int32, (rows, columns), 0)
    keys = lax.broadcasted_iota(jnp.int32, (rows, columns), 1)
    same = doc_col == doc_row
    return same & (keys <= queries) & ((keys < live_count) | (keys == queries))


def load_halves(mine_ref, other_ref, held, sems):
    core = lax.rem(lax.axis_index("dp"), 2)
    first = pltpu.make_async_copy(mine_ref, held.at[core], sems.at[0])
    second = pltpu.make_async_copy(other_ref, held.at[1 - core], sems.at[1])
    first.start()
    second.start()
    return core, first, second


def attend_kernel(
    live_ref,
    tokens_ref,
    mine_ref,
    other_ref,
    gains_ref,
    bias_ref,
    doc_col_ref,
    doc_row_ref,
    normed_ref,
    query_raw_ref,
    key_raw_ref,
    query_ref,
    key_ref,
    value_ref,
    gate_ref,
    attended_ref,
    gated_mine_ref,
    gated_other_ref,
    part_ref,
    logit_ref,
    decay_ref,
    total_ref,
    held,
    sems,
):
    core, first_copy, second_copy = load_halves(mine_ref, other_ref, held, sems)
    live_count = live_ref[0]
    inv_root = 0.125
    hidden = tokens_ref[...].astype(jnp.float32)
    scale = lax.rsqrt(jnp.mean(hidden * hidden, axis=1, keepdims=True) + epsilon)
    first_copy.wait()
    second_copy.wait()
    ext = held[0, :, 768:896]
    gains = gain_rows(ext)
    normed = (hidden * scale * gains[0:1]).astype(jnp.bfloat16)
    normed_ref[...] = normed
    for block in range(3):
        lanes = slice(block * 128, block * 128 + 128)
        query_raw = dot_nn(normed, held[0, :, block * 128 : block * 128 + 128])
        key_raw = dot_nn(normed, held[0, :, 384 + block * 128 : 512 + block * 128])
        query_raw_ref[:, lanes] = query_raw
        key_raw_ref[:, lanes] = key_raw
        query_ref[:, lanes] = pair_rms(query_raw, gains_ref[0:1])[0].astype(jnp.bfloat16)
        key_ref[:, lanes] = pair_rms(key_raw, gains_ref[1:2])[0].astype(jnp.bfloat16)
    value_ref[...] = dot_nn(normed, held[1, :, 0:384]).astype(jnp.bfloat16)
    gate_ref[...] = dot_nn(normed, held[1, :, 384:768])
    lane = lax.broadcasted_iota(jnp.int32, (384, 128), 1)
    logit = dot_nn(normed, ext) + bias_ref[...]
    logit = jnp.where(lane < 6, logit, 0.0)
    logit_ref[...] = logit
    log_sig = jnp.minimum(logit, 0.0) - jnp.log1p(jnp.exp(-jnp.abs(logit)))
    rows = lax.broadcasted_iota(jnp.int32, (384, 384), 0)
    columns = lax.broadcasted_iota(jnp.int32, (384, 384), 1)
    lower = (columns <= rows).astype(jnp.float32).astype(jnp.bfloat16)
    decay = exact_nn(lower, log_sig)
    decay_ref[...] = decay
    decay_t = decay.T
    for step in range(3):
        begin, count = step * 128, step * 128 + 128
        allowed = allowed_block(
            doc_col_ref[begin : begin + 128, :],
            doc_row_ref[:, 0:count],
            live_count,
            begin,
            128,
            count,
        )
        totals = jnp.zeros((128, 128), jnp.float32)
        small_lane = lax.broadcasted_iota(jnp.int32, (128, 128), 1)
        for block in range(3):
            lanes = slice(block * 128, block * 128 + 128)
            keys = key_ref[0:count, lanes]
            values = value_ref[0:count, lanes]
            query_pair = query_ref[begin : begin + 128, lanes]
            outs = []
            for half in range(2):
                head = block * 2 + half
                query = jnp.where(head_mask(128, half), query_pair, jnp.zeros_like(query_pair))
                scores = block_scores(
                    query,
                    keys,
                    lane_pick(decay[begin : begin + 128], head),
                    decay_t[head : head + 1, 0:count],
                    allowed,
                    inv_root,
                )
                peak = jnp.max(scores, axis=1, keepdims=True)
                grown = jnp.exp(scores - peak)
                total = jnp.sum(grown, axis=1, keepdims=True)
                totals = jnp.where(small_lane == head, peak + jnp.log(total), totals)
                probs = (grown * (1.0 / total)).astype(jnp.bfloat16)
                outs.append(dot_nn(probs, values))
            attended_ref[begin : begin + 128, lanes] = jnp.where(
                head_mask(128, 0), outs[0], outs[1]
            )
        total_ref[begin : begin + 128, :] = totals
    gated = (attended_ref[...] * jax.nn.sigmoid(gate_ref[...])).astype(jnp.bfloat16)
    gated_mine_ref[...] = jnp.where(core == 0, gated[:, 0:256], gated[:, 128:384])
    gated_other_ref[...] = jnp.where(core == 0, gated[:, 128:384], gated[:, 0:256])
    part = dot_nt(gated[:, 0:128], held[0, :, 896:1024]) + dot_nt(
        gated[:, 128:384], held[1, :, 768:1024]
    )
    part_ref[...] = part.astype(jnp.bfloat16)


def mlp_kernel(
    live_ref,
    tokens_ref,
    part_ref,
    peer_ref,
    cotangent_ref,
    ext_ref,
    mine_ref,
    other_ref,
    middle_ref,
    normed_ref,
    hidden_mine_ref,
    hidden_other_ref,
    out_ref,
    grad_ref,
    held,
    sems,
):
    core, first_copy, second_copy = load_halves(mine_ref, other_ref, held, sems)
    middle = tokens_ref[...].astype(jnp.float32) + (
        part_ref[...].astype(jnp.float32) + peer_ref[...].astype(jnp.float32)
    )
    middle_ref[...] = middle
    gains = gain_rows(ext_ref[...])
    scale = lax.rsqrt(jnp.mean(middle * middle, axis=1, keepdims=True) + epsilon)
    normed = (middle * scale * gains[1:2]).astype(jnp.bfloat16)
    normed_ref[...] = normed
    live_rows = lax.broadcasted_iota(jnp.int32, (384, 1), 0) < live_ref[0]
    grad_out = jnp.where(live_rows, cotangent_ref[...].astype(jnp.float32), 0.0)
    grad_out = grad_out.astype(jnp.bfloat16)
    first_copy.wait()
    second_copy.wait()
    out_total = jnp.zeros((384, 768), jnp.float32)
    grad_total = jnp.zeros((384, 768), jnp.float32)
    parts = []
    for half in range(2):
        begin = half * 512
        gate_w = held[0, :, begin : begin + 512]
        up_w = held[1, :, begin : begin + 512]
        down_w = held[half, :, 1024:1536]
        gate = dot_nn(normed, gate_w)
        up = dot_nn(normed, up_w)
        sig = jax.nn.sigmoid(gate)
        silu = gate * sig
        active = (silu * up).astype(jnp.bfloat16)
        out_total = out_total + dot_nt(active, down_w)
        grad_act = dot_nn(grad_out, down_w)
        grad_up = (grad_act * silu).astype(jnp.bfloat16)
        grad_gate = (grad_act * up * (sig * (1.0 + gate * (1.0 - sig)))).astype(jnp.bfloat16)
        parts.append((grad_gate, grad_up, active))
        grad_total = grad_total + dot_nt(grad_gate, gate_w) + dot_nt(grad_up, up_w)
    for number in range(3):
        lanes = slice(number * 512, number * 512 + 512)
        first, second = parts[0][number], parts[1][number]
        hidden_mine_ref[:, lanes] = jnp.where(core == 0, first, second)
        hidden_other_ref[:, lanes] = jnp.where(core == 0, second, first)
    out_ref[...] = out_total.astype(jnp.bfloat16)
    grad_ref[...] = grad_total.astype(jnp.bfloat16)


def attend_back_kernel(
    live_ref,
    cotangent_ref,
    middle_ref,
    grad_part_ref,
    grad_peer_ref,
    mine_ref,
    other_ref,
    gains_ref,
    doc_col_ref,
    doc_row_ref,
    normed_ref,
    query_raw_ref,
    key_raw_ref,
    query_ref,
    key_ref,
    value_ref,
    gate_ref,
    attended_ref,
    logit_ref,
    decay_ref,
    total_ref,
    grad_middle_ref,
    grad_middle_b_ref,
    proj_mine_ref,
    proj_other_ref,
    norm_part_ref,
    small_ref,
    tiny_ref,
    held,
    sems,
    grad_att_ref,
    grad_query_ref,
    grad_key_ref,
    grad_value_ref,
    grad_og_ref,
    column_ref,
):
    core, first_copy, second_copy = load_halves(mine_ref, other_ref, held, sems)
    live_count = live_ref[0]
    inv_root = 0.125
    middle = middle_ref[...]
    grad_normed = grad_part_ref[...].astype(jnp.float32) + grad_peer_ref[...].astype(jnp.float32)
    live_rows = lax.broadcasted_iota(jnp.int32, (384, 1), 0) < live_count
    grad_out = jnp.where(live_rows, cotangent_ref[...].astype(jnp.float32), 0.0)
    scale = lax.rsqrt(jnp.mean(middle * middle, axis=1, keepdims=True) + epsilon)
    first_copy.wait()
    second_copy.wait()
    ext = held[0, :, 768:896]
    gains = gain_rows(ext)
    gained = grad_normed * gains[1:2]
    inner = jnp.mean(gained * middle, axis=1, keepdims=True)
    grad_middle = grad_out + (scale * gained - middle * (scale * scale * scale * inner))
    grad_gain = jnp.sum(grad_normed * middle * scale, axis=0, keepdims=True)
    grad_middle_ref[...] = grad_middle
    grad_middle_b = grad_middle.astype(jnp.bfloat16)
    grad_middle_b_ref[...] = grad_middle_b
    grad_gated = jnp.concatenate(
        [
            dot_nn(grad_middle_b, held[0, :, 896:1024]),
            dot_nn(grad_middle_b, held[1, :, 768:1024]),
        ],
        axis=1,
    )
    sig = jax.nn.sigmoid(gate_ref[...])
    grad_att_ref[...] = (grad_gated * sig).astype(jnp.bfloat16)
    grad_og = (grad_gated * attended_ref[...] * sig * (1.0 - sig)).astype(jnp.bfloat16)
    grad_og_ref[...] = grad_og
    grad_key_ref[...] = jnp.zeros((384, 384), jnp.float32)
    grad_value_ref[...] = jnp.zeros((384, 384), jnp.float32)
    column_ref[...] = jnp.zeros((128, 384), jnp.float32)
    decay = decay_ref[...]
    decay_t = decay.T
    row_parts = []
    for step in range(3):
        begin, count = step * 128, step * 128 + 128
        allowed = allowed_block(
            doc_col_ref[begin : begin + 128, :],
            doc_row_ref[:, 0:count],
            live_count,
            begin,
            128,
            count,
        )
        small_lane = lax.broadcasted_iota(jnp.int32, (128, 128), 1)
        row_sums = jnp.zeros((128, 128), jnp.float32)
        for block in range(3):
            lanes = slice(block * 128, block * 128 + 128)
            keys = key_ref[0:count, lanes]
            values = value_ref[0:count, lanes]
            query_pair = query_ref[begin : begin + 128, lanes]
            att_pair = grad_att_ref[begin : begin + 128, lanes]
            outs = []
            key_outs = []
            value_outs = []
            for half in range(2):
                head = block * 2 + half
                mask = head_mask(128, half)
                query = jnp.where(mask, query_pair, jnp.zeros_like(query_pair))
                att = jnp.where(mask, att_pair, jnp.zeros_like(att_pair))
                scores = block_scores(
                    query,
                    keys,
                    lane_pick(decay[begin : begin + 128], head),
                    decay_t[head : head + 1, 0:count],
                    allowed,
                    inv_root,
                )
                probs = jnp.exp(scores - lane_pick(total_ref[begin : begin + 128, :], head))
                grad_probs = dot_nt(att, values)
                row_dot = jnp.sum(probs * grad_probs, axis=1, keepdims=True)
                grad_scores = (probs * (grad_probs - row_dot)).astype(jnp.bfloat16)
                grad_scores_f = grad_scores.astype(jnp.float32)
                row_sums = jnp.where(
                    small_lane == head,
                    jnp.sum(grad_scores_f, axis=1, keepdims=True),
                    row_sums,
                )
                column_ref[head : head + 1, 0:count] += jnp.sum(
                    grad_scores_f, axis=0, keepdims=True
                )
                outs.append(dot_nn(grad_scores, keys))
                key_outs.append(dot_tn(grad_scores, query))
                value_outs.append(dot_tn(probs.astype(jnp.bfloat16), att))
            grad_query_ref[begin : begin + 128, lanes] = jnp.where(
                head_mask(128, 0), outs[0], outs[1]
            )
            grad_key_ref[0:count, lanes] += key_outs[0] + key_outs[1]
            grad_value_ref[0:count, lanes] += value_outs[0] + value_outs[1]
        row_parts.append(row_sums)
    grad_decay = jnp.concatenate(row_parts, axis=0) - column_ref[...].T
    rows = lax.broadcasted_iota(jnp.int32, (384, 384), 0)
    columns = lax.broadcasted_iota(jnp.int32, (384, 384), 1)
    upper = (columns >= rows).astype(jnp.float32).astype(jnp.bfloat16)
    grad_logit = exact_nn(upper, grad_decay) * jax.nn.sigmoid(-logit_ref[...])
    lane = lax.broadcasted_iota(jnp.int32, (384, 128), 1)
    grad_logit = jnp.where(lane < 6, grad_logit, 0.0)
    grad_forget = grad_logit.astype(jnp.bfloat16)
    grad_vg = jnp.concatenate([grad_value_ref[...].astype(jnp.bfloat16), grad_og_ref[...]], axis=1)
    grad_qk = []
    gain_sums = []
    for number, raw_ref, out_ref in (
        (0, query_raw_ref, grad_query_ref),
        (1, key_raw_ref, grad_key_ref),
    ):
        gain = gains_ref[number : number + 1]
        gain_sum = jnp.zeros((1, 128), jnp.float32)
        for block in range(3):
            lanes = slice(block * 128, block * 128 + 128)
            raw = raw_ref[:, lanes]
            grad = (out_ref[:, lanes] * inv_root).astype(jnp.bfloat16).astype(jnp.float32)
            first = head_mask(384, 0)
            scaled = pair_rms(raw, 1.0)[1]
            weighted = grad * gain
            product = weighted * raw
            sum_first = jnp.sum(jnp.where(first, product, 0.0), axis=1, keepdims=True)
            sum_second = jnp.sum(jnp.where(first, 0.0, product), axis=1, keepdims=True)
            inner_head = jnp.where(first, sum_first, sum_second) * (1.0 / 64.0)
            gain_sum = gain_sum + jnp.sum(grad * raw * scaled, axis=0, keepdims=True)
            grad_raw = scaled * weighted - raw * (scaled * scaled * scaled * inner_head)
            grad_qk.append(grad_raw.astype(jnp.bfloat16))
        gain_sums.append(gain_sum)
    grad_qk = jnp.concatenate(grad_qk, axis=1)
    proj_mine_ref[...] = jnp.where(core == 0, grad_qk, grad_vg)
    proj_other_ref[...] = jnp.where(core == 0, grad_vg, grad_qk)
    part = dot_nt(grad_qk, held[0, :, 0:768])
    part = part + dot_nt(grad_vg, held[1, :, 0:768])
    part = part + dot_nt(grad_forget, ext)
    norm_part_ref[...] = part.astype(jnp.bfloat16)
    forget_rows = dot_tn(grad_forget, normed_ref[...])
    small_ref[0:8, :] = forget_rows[0:8]
    small_ref[6:7, :] = jnp.zeros((1, 768), jnp.float32)
    small_ref[7:8, :] = grad_gain
    bias_sum = jnp.sum(grad_forget.astype(jnp.float32), axis=0, keepdims=True)
    tiny_ref[0:1, :] = gain_sums[0]
    tiny_ref[1:2, :] = gain_sums[1]
    tiny_ref[2:3, :] = bias_sum
    tiny_ref[3:8, :] = jnp.zeros((5, 128), jnp.float32)


def pair_grad_kernel(width, start, *refs):
    first, first_peer, left, left_peer, second, second_peer, right, right_peer, out_ref = refs
    for begin in range(0, out_ref.shape[1], 256):
        if begin < width:
            lanes = slice(begin, begin + 256)
            total = dot_tn(first[...], left[:, lanes])
            total = total + dot_tn(first_peer[...], left_peer[:, lanes])
        else:
            lanes = slice(start + begin - width, start + begin - width + 256)
            total = dot_tn(second[...], right[:, lanes])
            total = total + dot_tn(second_peer[...], right_peer[:, lanes])
        out_ref[:, begin : begin + 256] = total.astype(jnp.bfloat16)


def newton_kernel(mine_ref, other_ref, out_ref, held, square_ref, poly_ref):
    columns = mine_ref.shape[2]
    total = jnp.zeros((1, 1), jnp.float32)
    for source in (mine_ref, other_ref):
        for side in range(2):
            for start in range(0, 384, 64):
                piece = source[side, start : start + 64, :].astype(jnp.float32)
                piece = jnp.sum(piece * piece, axis=0, keepdims=True)
                total = total + jnp.sum(piece, axis=1, keepdims=True)
    scale = 1.0 / (jnp.sqrt(total) + 1e-07)
    for place, source in ((0, mine_ref), (384, other_ref)):
        for side in range(2):
            for start in range(0, 384, 64):
                piece = source[side, start : start + 64, :].astype(jnp.float32) * scale
                held[0, side, place + start : place + start + 64, :] = piece.astype(jnp.bfloat16)
    for repeat in range(5):
        now, later = repeat % 2, (repeat + 1) % 2
        for start in range(0, 768, 256):
            square = dot_nt(held[now, 0, start : start + 256, :], held[now, 0])
            square = square + dot_nt(held[now, 1, start : start + 256, :], held[now, 1])
            square_ref[start : start + 256, :] = square.astype(jnp.bfloat16)
        if repeat < 4:
            for start in range(0, 768, 256):
                few = square_ref[start : start + 256, :]
                poly = coef_b * few.astype(jnp.float32) + coef_c * dot_nn(few, square_ref[...])
                poly_ref[start : start + 256, :] = poly.astype(jnp.bfloat16)
            for side in range(2):
                for start in range(0, 768, 256):
                    grown = coef_a * held[now, side, start : start + 256, :].astype(jnp.float32)
                    grown = grown + dot_nn(poly_ref[start : start + 256, :], held[now, side])
                    held[later, side, start : start + 256, :] = grown.astype(jnp.bfloat16)
        else:
            place = lax.axis_index("dp")
            plane = (place // 16) * 2 + lax.rem(place // 2, 2)
            side = lax.axis_index("tensor")
            begin = pl.multiple_of(plane * 48, 16)
            few = square_ref[pl.ds(begin, 48), :]
            poly = coef_b * few.astype(jnp.float32) + coef_c * dot_nn(few, square_ref[...])
            poly = poly.astype(jnp.bfloat16)
            grown = coef_a * held[now, side, pl.ds(begin, 48), :].astype(jnp.float32)
            grown = grown + dot_nn(poly, held[now, side])
            out_ref[...] = grown.astype(jnp.bfloat16)


in_vmem = pl.BlockSpec(memory_space=pltpu.VMEM)
in_smem = pl.BlockSpec(memory_space=pltpu.SMEM)
in_any = pl.BlockSpec(memory_space=pl.ANY)


def call_kernel(kernel, in_specs, outs, scratch, flops, limit=48):
    return pl.pallas_call(
        kernel,
        out_shape=[jax.ShapeDtypeStruct(shape, dtype) for shape, dtype in outs],
        in_specs=in_specs,
        out_specs=[in_vmem] * len(outs),
        scratch_shapes=scratch,
        compiler_params=pltpu.CompilerParams(vmem_limit_bytes=limit * 1024 * 1024),
        cost_estimate=pl.CostEstimate(flops=flops, bytes_accessed=10000000, transcendentals=0),
    )


def pair_grad(first, left, second, right, width, start, total):
    return call_kernel(
        functools.partial(pair_grad_kernel, width, start),
        [in_vmem] * 8,
        [((768, total), jnp.bfloat16)],
        [],
        2 * 768 * 768 * total,
    )(*first, *left, *second, *right)[0]


def spread_slots(slots_b):
    column = place_of("x")

    def slot(step):
        return lax.dynamic_index_in_dim(slots_b, (column + step) % 4, 0, keepdims=False)

    return jnp.concatenate([slot(0)] + [fetch(slot(4 - step), "x", step) for step in (1, 2, 3)], 0)


def newton_rows(mine, other):
    columns = mine.shape[2]
    return call_kernel(
        newton_kernel,
        [in_vmem] * 2,
        [((48, columns), jnp.bfloat16)],
        [
            pltpu.VMEM((2, 2, 768, columns), jnp.bfloat16),
            pltpu.VMEM((768, 768), jnp.bfloat16),
            pltpu.VMEM((768, 768), jnp.bfloat16),
        ],
        10 * 768 * 768 * (4 * columns + 768),
    )(mine, other)[0]


def return_slots(rows):
    column = place_of("x")
    pieces = [rows[:12]]
    for step in (1, 2, 3):
        pieces.append(fetch(rows[12 * step : 12 * step + 12], "x", -step))
    out = []
    for number in range(4):
        step = (column - number) % 4
        value = pieces[0]
        for other in (1, 2, 3):
            value = jnp.where(step == other, pieces[other], value)
        out.append(value)
    return jnp.stack(out).astype(jnp.float32)


def on_device(
    tokens,
    cotangent,
    segment_ids,
    live_len,
    w_square,
    w_wide,
    norm_gain,
    qk_gain,
    forget_w,
    forget_b,
    m_square,
    m_wide,
    m_norm,
    m_qk,
    m_forget_w,
    m_forget_b,
    ema_square,
    ema_wide,
):
    half_width = w_square.shape[2]
    half_hidden = w_wide.shape[2]
    shard_rows = w_square.shape[1]
    head_local = forget_w.shape[1]
    head_dim = qk_gain.shape[1]
    dp_size = lax.axis_size("dp")
    full_width = shard_rows * dp_size
    full_hidden = half_hidden * lax.axis_size("tensor")
    total_tokens = tokens.shape[0] * dp_size
    my_place = lax.axis_index("dp")
    core = my_place % 2
    quarter_hidden = half_hidden // 2
    bf16, f32 = jnp.bfloat16, jnp.float32

    square_b = w_square.astype(bf16)
    wide_b = w_wide.astype(bf16)
    extras = jnp.concatenate(
        [
            forget_w.astype(bf16),
            norm_gain.astype(bf16).T,
            jnp.zeros((shard_rows, 120), bf16),
        ],
        axis=1,
    )
    even = [square_b[0], square_b[1, :, :128]]
    even += [wide_b[0, :, :768]]
    even += [square_b[1, :, 128:], extras, square_b[4, :, :128]]
    even += [wide_b[0, :, 768:], wide_b[2, :, :quarter_hidden]]
    odd = [square_b[2], square_b[3, :, :128]]
    odd += [wide_b[1, :, :768]]
    odd += [square_b[3, :, 128:], square_b[4, :, 128:]]
    odd += [wide_b[1, :, 768:], wide_b[2, :, quarter_hidden:]]
    even = jnp.concatenate(even, axis=1)
    odd = jnp.concatenate(odd, axis=1)
    pair_rows = pair_join(core, by_core(core, even, odd), core_swap(by_core(core, odd, even)), 0)
    quad_rows = pair_join(place_of("l"), pair_rows, fetch(pair_rows, "l", 1), 0)
    blocks_x = fetch_ring(quad_rows[:, :1280], "x")
    blocks_y = fetch_ring(quad_rows[:, 1280:], "y")
    first_mine = assemble(
        fetch_ring(jnp.stack([block[:, :512] for block in blocks_x]), "y")
        + fetch_ring(jnp.stack([block[:, :512] for block in blocks_y]), "x")
    )
    first_other = core_swap(first_mine)
    late_x, late_y, first_other = lax.optimization_barrier((blocks_x, blocks_y, first_other))
    late_stacks = (
        jnp.stack([block[:, 512:] for block in late_x]),
        jnp.stack([block[:, 512:] for block in late_y]),
    )
    late_blocks = fetch_ring(late_stacks[0], "y") + fetch_ring(late_stacks[1], "x")
    ext = by_core(core, first_mine[:, 768:896], first_other[:, 768:896])

    gains_b = qk_gain.astype(bf16).astype(f32)
    gains = jnp.concatenate([gains_b, gains_b], axis=1)
    bias_row = jnp.pad(forget_b.astype(bf16).astype(f32), (0, 128 - head_local))[None]
    doc_row = segment_ids
    doc_col = segment_ids.reshape(-1, 1)
    live_mask = (jnp.arange(tokens.shape[0]) < live_len[0])[:, None]
    grad_out_b = jnp.where(live_mask, cotangent, jnp.zeros_like(cotangent))

    def paired(mine, other):
        return mine, core_swap(other)

    square_f = ((384, 384), f32)
    square_h = ((384, 384), bf16)
    lane_f = ((384, 128), f32)
    token_h = ((384, 768), bf16)
    token_f = ((384, 768), f32)
    (
        normed_one,
        query_raw,
        key_raw,
        query_b,
        key_b,
        value_b,
        gate_raw,
        attended,
        gated_mine,
        gated_other,
        attn_part,
        logit,
        decay,
        log_total,
    ) = call_kernel(
        attend_kernel,
        [in_smem, in_vmem, in_any, in_any] + [in_vmem] * 4,
        [token_h, square_f, square_f, square_h, square_h, square_h, square_f, square_f]
        + [((384, 256), bf16)] * 2
        + [token_h, lane_f, lane_f, lane_f],
        [pltpu.VMEM((2, 768, 1024), bf16), pltpu.SemaphoreType.DMA((2,))],
        4000000000,
    )(live_len, tokens, first_mine, first_other, gains, bias_row, doc_col, doc_row)
    attn_peer = tensor_swap(attn_part)
    late_blocks, attn_part = lax.optimization_barrier((late_blocks, attn_part))
    second_mine = assemble(late_blocks)
    second_other = core_swap(second_mine)
    normed_one_pair = paired(normed_one, normed_one)
    gated_pair = paired(gated_mine, gated_other)
    grad_out_pair = paired(grad_out_b, grad_out_b)
    attn_peer, normed_one_pair, gated_pair, grad_out_pair = lax.optimization_barrier(
        (attn_peer, normed_one_pair, gated_pair, grad_out_pair)
    )
    middle, normed_two, hidden_mine, hidden_other, mlp_part, grad_part = call_kernel(
        mlp_kernel,
        [in_smem] + [in_vmem] * 5 + [in_any] * 2,
        [token_f, token_h, ((384, 1536), bf16), ((384, 1536), bf16), token_h, token_h],
        [pltpu.VMEM((2, 768, 1536), bf16), pltpu.SemaphoreType.DMA((2,))],
        5000000000,
    )(live_len, tokens, attn_part, attn_peer, cotangent, ext, second_mine, second_other)
    grad_peer = tensor_swap(grad_part)

    normed_two_pair = paired(normed_two, normed_two)
    hidden_pair = paired(hidden_mine, hidden_other)
    grad_wide_b = pair_grad(
        normed_two_pair, hidden_pair, grad_out_pair, hidden_pair, 1024, 1024, 1536
    )
    grad_peer, grad_wide_b = lax.optimization_barrier((grad_peer, grad_wide_b))
    blocks = exchange(grad_wide_b.reshape(32, 24, 3 * quarter_hidden), ("y", "x", "l"))
    wide_blocks = blocks
    mine, other = pair_split(core, jnp.sum(blocks.astype(f32), axis=0), 0)
    other = core_swap(other)
    wide_shard = jnp.stack(
        [
            pair_join(core, mine[:, start : start + 512], other[:, start : start + 512], 1)
            for start in (0, 512, 1024)
        ]
    )
    mom_wide = muon_decay * m_wide + wide_shard

    (
        grad_middle,
        grad_middle_b,
        proj_mine,
        proj_other,
        norm_part,
        small_rows,
        tiny_rows,
    ) = call_kernel(
        attend_back_kernel,
        [in_smem] + [in_vmem] * 4 + [in_any] * 2 + [in_vmem] * 14,
        [token_f, token_h, token_h, token_h, token_h]
        + [((8, 768), f32), ((8, 128), f32)],
        [
            pltpu.VMEM((2, 768, 1024), bf16),
            pltpu.SemaphoreType.DMA((2,)),
            pltpu.VMEM((384, 384), bf16),
            pltpu.VMEM((384, 384), f32),
            pltpu.VMEM((384, 384), f32),
            pltpu.VMEM((384, 384), f32),
            pltpu.VMEM((384, 384), bf16),
            pltpu.VMEM((128, 384), f32),
        ],
        6000000000,
    )(
        live_len,
        cotangent,
        middle,
        grad_part,
        grad_peer,
        first_mine,
        first_other,
        gains,
        doc_col,
        doc_row,
        normed_one,
        query_raw,
        key_raw,
        query_b,
        key_b,
        value_b,
        gate_raw,
        attended,
        logit,
        decay,
        log_total,
    )
    proj_pair = paired(proj_mine, proj_other)
    grad_middle_pair = paired(grad_middle_b, grad_middle_b)
    grad_proj_b = pair_grad(
        normed_one_pair, proj_pair, grad_middle_pair, gated_pair, 768, 0, 1024
    )
    grad_proj_b, wide_blocks = lax.optimization_barrier((grad_proj_b, wide_blocks))
    blocks = exchange(grad_proj_b.reshape(32, 24, 1024), ("y", "x", "l"))
    summed = jnp.sum(blocks.astype(f32), axis=0)
    mine, other = pair_split(core, summed, 0)
    other = core_swap(other)
    even = by_core(core, mine, other)
    odd = by_core(core, other, mine)
    square_shard = jnp.stack(
        [
            even[:, :384],
            even[:, 384:768],
            odd[:, :384],
            odd[:, 384:768],
            jnp.concatenate([even[:, 768:1024], odd[:, 896:1024]], axis=1),
        ]
    )
    mom_square = muon_decay * m_square + square_shard

    wide_slots = jnp.concatenate(
        [
            mom_wide.astype(bf16),
            jnp.pad(mom_square[4].astype(bf16), ((0, 0), (0, half_hidden - half_width)))[None],
        ],
        axis=0,
    )
    proj_rows = spread_slots(mom_square[:4].astype(bf16))
    wide_rows = spread_slots(wide_slots)
    wide_own = gather(wide_rows, ("t", "y", "l")).reshape(2, 384, half_hidden)
    proj_rows, wide_own = lax.optimization_barrier((proj_rows, wide_own))
    proj_own = gather(proj_rows, ("t", "y", "l")).reshape(2, 384, half_width)
    wide_rows = newton_rows(wide_own, core_swap(wide_own))
    proj_own, wide_rows = lax.optimization_barrier((proj_own, wide_rows))
    update_wide = return_slots(wide_rows)
    update_proj = return_slots(newton_rows(proj_own, core_swap(proj_own)))
    update_square = jnp.concatenate([update_proj, update_wide[3:, :, :half_width]], axis=0)
    update_wide = update_wide[:3]

    norm_peer = tensor_swap(norm_part)
    mlp_part, norm_peer = lax.optimization_barrier((mlp_part, norm_peer))
    mlp_out = mlp_part.astype(f32) + tensor_swap(mlp_part).astype(f32)
    result = (middle + mlp_out).astype(bf16)
    hidden_in = tokens.astype(f32)
    gain_one = ext[:, head_local].astype(f32)[None]
    grad_norm_one = norm_part.astype(f32) + norm_peer.astype(f32)
    scale = lax.rsqrt(jnp.mean(hidden_in * hidden_in, axis=1, keepdims=True) + epsilon)
    gained = grad_norm_one * gain_one
    inner = jnp.mean(gained * hidden_in, axis=1, keepdims=True)
    input_grad = grad_middle + (scale * gained - hidden_in * (scale * scale * scale * inner))
    grad_gain_one = jnp.sum(grad_norm_one * hidden_in * scale, axis=0)

    tiny_row = jnp.concatenate(
        [
            tiny_rows[:2, :head_dim] + tiny_rows[:2, head_dim:],
            jnp.pad(tiny_rows[2:3, :head_local], ((0, 0), (0, head_dim - head_local))),
        ],
        axis=0,
    ).reshape(1, -1)
    tiny_row = jnp.pad(tiny_row, ((0, 7), (0, full_width - 3 * head_dim)))
    small_rows = jnp.concatenate(
        [small_rows[:6], grad_gain_one[None], small_rows[7:], tiny_row], axis=0
    )
    small = small_rows
    for name, step in (("c", 1), ("l", 1)):
        small = small + fetch(small, name, step)
    for name in ("x", "y"):
        small = sum(fetch_ring(small, name)[1:], small)
    own_small = lax.dynamic_slice_in_dim(small, my_place * shard_rows, shard_rows, 1)
    gains_shard = own_small[6:8]
    forget_shard = own_small[:head_local].T
    bias_total = small[8, 2 * head_dim : 2 * head_dim + head_local]
    qk_part = small[8, : 2 * head_dim].reshape(2, head_dim)
    qk_total = qk_part + tensor_swap(qk_part)
    new_square = w_square - update_square
    new_wide = w_wide - math.sqrt(full_hidden / full_width) * update_wide
    new_ema_square = ema_decay * ema_square + (1.0 - ema_decay) * new_square
    new_ema_wide = ema_decay * ema_wide + (1.0 - ema_decay) * new_wide
    root_tokens = math.sqrt(total_tokens)
    mom_norm = plain_decay * m_norm + gains_shard
    mom_qk = plain_decay * m_qk + qk_total
    mom_forget_w = plain_decay * m_forget_w + forget_shard
    mom_forget_b = plain_decay * m_forget_b + bias_total
    new_norm = norm_gain - gain_rate / root_tokens * mom_norm
    new_qk = qk_gain - qk_rate / root_tokens * mom_qk
    new_forget_w = forget_w - forget_rate / root_tokens * mom_forget_w
    new_forget_b = forget_b - bias_rate / root_tokens * mom_forget_b
    return (
        result,
        input_grad,
        new_square,
        new_wide,
        new_norm,
        new_qk,
        new_forget_w,
        new_forget_b,
        mom_square,
        mom_wide,
        mom_norm,
        mom_qk,
        mom_forget_w,
        mom_forget_b,
        new_ema_square,
        new_ema_wide,
    )


def solution(mesh):
    placed = (
        P("dp", None),
        P("dp", None),
        P("dp", None),
        P("dp"),
        P(None, "dp", "tensor"),
        P(None, "dp", "tensor"),
        P(None, "dp"),
        P(),
        P("dp", "tensor"),
        P("tensor"),
        P(None, "dp", "tensor"),
        P(None, "dp", "tensor"),
        P(None, "dp"),
        P(),
        P("dp", "tensor"),
        P("tensor"),
        P(None, "dp", "tensor"),
        P(None, "dp", "tensor"),
    )
    return jax.shard_map(
        on_device,
        mesh=mesh,
        in_specs=placed,
        out_specs=(
            P("dp", None),
            P("dp", None),
            P(None, "dp", "tensor"),
            P(None, "dp", "tensor"),
            P(None, "dp"),
            P(),
            P("dp", "tensor"),
            P("tensor"),
            P(None, "dp", "tensor"),
            P(None, "dp", "tensor"),
            P(None, "dp"),
            P(),
            P("dp", "tensor"),
            P("tensor"),
            P(None, "dp", "tensor"),
            P(None, "dp", "tensor"),
        ),
        check_vma=False,
    )
```

```python
import functools
import math

import jax
import jax.numpy as jnp
from jax import lax
import numpy as np
from jax.experimental import pallas as pl
from jax.experimental.pallas import tpu as pltpu
from jax.sharding import PartitionSpec as P

epsilon = 1e-06
coef_a = 3.4445
coef_b = -4.775
coef_c = 2.0315
muon_decay = 0.95
plain_decay = 0.9
ema_decay = 0.7
gain_rate = 0.2
qk_rate = 0.05
forget_rate = 0.1
bias_rate = 0.5


grid_sizes = {"y": 4, "x": 4, "l": 2, "c": 2, "t": 2}
dp_names = ["y", "x", "l", "c"]


def ring_groups(names, over):
    order = [name for name in over if name not in names]
    table = np.arange(math.prod(grid_sizes[name] for name in over))
    table = table.reshape([grid_sizes[name] for name in over])
    table = table.transpose([over.index(name) for name in order + list(names)])
    return table.reshape(-1, math.prod(grid_sizes[name] for name in names)).tolist()


def exchange(blocks, names):
    axes = ("dp", "tensor") if "t" in names else "dp"
    return lax.all_to_all(
        blocks,
        axes,
        split_axis=0,
        concat_axis=0,
        tiled=True,
        axis_index_groups=ring_groups(names, dp_names + (["t"] if "t" in names else [])),
    )


def gather(block, names):
    count = math.prod(grid_sizes[name] for name in names)
    return exchange(jnp.broadcast_to(block[None], (count,) + block.shape), names)


def place_of(name):
    place = lax.axis_index("dp")
    return {"y": place // 16, "x": (place // 4) % 4, "l": (place // 2) % 2, "c": place % 2}[name]


def fetch(array, name, step):
    table = np.arange(64).reshape(4, 4, 2, 2)
    sources = np.roll(table, -step, axis=dp_names.index(name))
    pairs = [(int(a), int(b)) for a, b in zip(sources.ravel(), table.ravel())]
    return lax.ppermute(array, "dp", pairs)


def fetch_ring(array, name):
    return [array] + [fetch(array, name, step) for step in (1, 3, 2)]


ring_steps = (0, 1, 3, 2)


def core_swap(array):
    return fetch(array, "c", 1)


def tensor_swap(array):
    return lax.ppermute(array, "tensor", [(0, 1), (1, 0)])


def by_core(core, even, odd):
    return jnp.where(core == 0, even, odd)


def pair_join(place, mine, other, axis):
    return jnp.where(
        place == 0,
        jnp.concatenate([mine, other], axis=axis),
        jnp.concatenate([other, mine], axis=axis),
    )


def pair_split(core, array, axis):
    first, second = jnp.split(array, 2, axis=axis)
    return by_core(core, first, second), by_core(core, second, first)


def assemble_kernel(first_ref, *refs):
    blocks, out_ref = refs[:4], refs[4]
    place = lax.axis_index("dp")
    row, column = place // 16, lax.rem(place // 4, 4)
    width = first_ref.shape[3]
    for number, step in enumerate(ring_steps):
        out_ref[number, :, :, 0:width] = first_ref[number]
        for inner, inner_step in enumerate(ring_steps):
            out_ref[
                lax.rem(row + inner_step, 4), lax.rem(column + step, 4), :, width : 2 * width
            ] = blocks[number][inner]


def assemble(first, blocks):
    width = 2 * first.shape[3]
    whole = pl.pallas_call(
        assemble_kernel,
        out_shape=jax.ShapeDtypeStruct((4, 4, 48, width), jnp.bfloat16),
        in_specs=[pl.BlockSpec(memory_space=pltpu.VMEM)] * 5,
        out_specs=pl.BlockSpec(memory_space=pltpu.VMEM),
        compiler_params=pltpu.CompilerParams(vmem_limit_bytes=12 * 1024 * 1024),
        cost_estimate=pl.CostEstimate(flops=0, bytes_accessed=3000 * width, transcendentals=0),
    )(first, *blocks)
    return whole.reshape(768, width)


def dot_nn(left, right):
    return jnp.dot(left, right, preferred_element_type=jnp.float32)


def dot_nt(left, right):
    return lax.dot_general(
        left, right, (((1,), (1,)), ((), ())), preferred_element_type=jnp.float32
    )


def dot_tn(left, right):
    return lax.dot_general(
        left, right, (((0,), (0,)), ((), ())), preferred_element_type=jnp.float32
    )


def three_parts(value):
    high = value.astype(jnp.bfloat16)
    rest = value - high.astype(jnp.float32)
    middle = rest.astype(jnp.bfloat16)
    low = (rest - middle.astype(jnp.float32)).astype(jnp.bfloat16)
    return high, middle, low


def exact_nn(ones, value):
    high, middle, low = three_parts(value)
    return dot_nn(ones, high) + dot_nn(ones, middle) + dot_nn(ones, low)


def gain_rows(ext):
    rows = lax.broadcasted_iota(jnp.int32, (16, 128), 0)
    columns = lax.broadcasted_iota(jnp.int32, (16, 128), 1)
    pick = (columns == rows + 6).astype(jnp.float32).astype(jnp.bfloat16)
    return dot_nt(pick, ext)


def head_mask(rows, head):
    lanes = lax.broadcasted_iota(jnp.int32, (rows, 128), 1)
    return (lanes // 64) == head


def lane_pick(array, lane):
    lanes = lax.broadcasted_iota(jnp.int32, array.shape, 1)
    return jnp.sum(jnp.where(lanes == lane, array, 0.0), axis=1, keepdims=True)


def pair_rms(raw, gain):
    first = head_mask(raw.shape[0], 0)
    square = raw * raw
    sum_first = jnp.sum(jnp.where(first, square, 0.0), axis=1, keepdims=True)
    sum_second = jnp.sum(jnp.where(first, 0.0, square), axis=1, keepdims=True)
    mean = jnp.where(first, sum_first, sum_second) * (1.0 / 64.0)
    scale = lax.rsqrt(mean + epsilon)
    return raw * scale * gain, scale


def block_scores(query, keys, decay_col, decay_row, allowed, inv_root):
    raw = dot_nt(query, keys) * inv_root + decay_col - decay_row
    return jnp.where(allowed, raw, -1e30)


def allowed_block(doc_col, doc_row, live_count, start, rows, columns):
    queries = start + lax.broadcasted_iota(jnp.int32, (rows, columns), 0)
    keys = lax.broadcasted_iota(jnp.int32, (rows, columns), 1)
    same = doc_col == doc_row
    return same & (keys <= queries) & ((keys < live_count) | (keys == queries))


def load_halves(mine_ref, other_ref, held, sems):
    core = lax.rem(lax.axis_index("dp"), 2)
    first = pltpu.make_async_copy(mine_ref, held.at[core], sems.at[0])
    second = pltpu.make_async_copy(other_ref, held.at[1 - core], sems.at[1])
    first.start()
    second.start()
    return core, first, second


def attend_kernel(
    live_ref,
    tokens_ref,
    mine_ref,
    other_ref,
    gains_ref,
    bias_ref,
    doc_col_ref,
    doc_row_ref,
    normed_ref,
    raw_out,
    heads_out,
    gated_mine_ref,
    gated_other_ref,
    part_ref,
    lanes_out,
    held,
    sems,
    raw_ref,
    heads_ref,
    lanes_ref,
):
    core, first_copy, second_copy = load_halves(mine_ref, other_ref, held, sems)
    query_raw_ref, key_raw_ref, gate_ref, attended_ref = [raw_ref.at[n] for n in range(4)]
    query_ref, key_ref, value_ref = [heads_ref.at[n] for n in range(3)]
    logit_ref, decay_ref, total_ref = [lanes_ref.at[n] for n in range(3)]
    live_count = live_ref[0]
    inv_root = 0.125
    hidden = tokens_ref[...].astype(jnp.float32)
    scale = lax.rsqrt(jnp.mean(hidden * hidden, axis=1, keepdims=True) + epsilon)
    first_copy.wait()
    second_copy.wait()
    ext = held[0, :, 768:896]
    gains = gain_rows(ext)
    normed = (hidden * scale * gains[0:1]).astype(jnp.bfloat16)
    normed_ref[...] = normed
    for block in range(3):
        lanes = slice(block * 128, block * 128 + 128)
        query_raw = dot_nn(normed, held[0, :, block * 128 : block * 128 + 128])
        key_raw = dot_nn(normed, held[0, :, 384 + block * 128 : 512 + block * 128])
        query_raw_ref[:, lanes] = query_raw
        key_raw_ref[:, lanes] = key_raw
        query_ref[:, lanes] = pair_rms(query_raw, gains_ref[0:1])[0].astype(jnp.bfloat16)
        key_ref[:, lanes] = pair_rms(key_raw, gains_ref[1:2])[0].astype(jnp.bfloat16)
    value_ref[...] = dot_nn(normed, held[1, :, 0:384]).astype(jnp.bfloat16)
    gate_ref[...] = dot_nn(normed, held[1, :, 384:768])
    lane = lax.broadcasted_iota(jnp.int32, (384, 128), 1)
    logit = dot_nn(normed, ext) + bias_ref[...]
    logit = jnp.where(lane < 6, logit, 0.0)
    logit_ref[...] = logit
    log_sig = jnp.minimum(logit, 0.0) - jnp.log1p(jnp.exp(-jnp.abs(logit)))
    rows = lax.broadcasted_iota(jnp.int32, (384, 384), 0)
    columns = lax.broadcasted_iota(jnp.int32, (384, 384), 1)
    lower = (columns <= rows).astype(jnp.float32).astype(jnp.bfloat16)
    decay = exact_nn(lower, log_sig)
    decay_ref[...] = decay
    decay_t = decay.T
    for step in range(3):
        begin, count = step * 128, step * 128 + 128
        allowed = allowed_block(
            doc_col_ref[begin : begin + 128, :],
            doc_row_ref[:, 0:count],
            live_count,
            begin,
            128,
            count,
        )
        totals = jnp.zeros((128, 128), jnp.float32)
        small_lane = lax.broadcasted_iota(jnp.int32, (128, 128), 1)
        for block in range(3):
            lanes = slice(block * 128, block * 128 + 128)
            keys = key_ref[0:count, lanes]
            values = value_ref[0:count, lanes]
            query_pair = query_ref[begin : begin + 128, lanes]
            outs = []
            for half in range(2):
                head = block * 2 + half
                query = jnp.where(head_mask(128, half), query_pair, jnp.zeros_like(query_pair))
                scores = block_scores(
                    query,
                    keys,
                    lane_pick(decay[begin : begin + 128], head),
                    decay_t[head : head + 1, 0:count],
                    allowed,
                    inv_root,
                )
                peak = jnp.max(scores, axis=1, keepdims=True)
                grown = jnp.exp(scores - peak)
                total = jnp.sum(grown, axis=1, keepdims=True)
                totals = jnp.where(small_lane == head, peak + jnp.log(total), totals)
                probs = (grown * (1.0 / total)).astype(jnp.bfloat16)
                outs.append(dot_nn(probs, values))
            attended_ref[begin : begin + 128, lanes] = jnp.where(
                head_mask(128, 0), outs[0], outs[1]
            )
        total_ref[begin : begin + 128, :] = totals
    copies = [
        pltpu.make_async_copy(source, target, sems.at[2 + number])
        for number, (source, target) in enumerate(
            ((raw_ref, raw_out), (heads_ref, heads_out), (lanes_ref, lanes_out))
        )
    ]
    for copy in copies:
        copy.start()
    gated = (attended_ref[...] * jax.nn.sigmoid(gate_ref[...])).astype(jnp.bfloat16)
    gated_mine_ref[...] = jnp.where(core == 0, gated[:, 0:256], gated[:, 128:384])
    gated_other_ref[...] = jnp.where(core == 0, gated[:, 128:384], gated[:, 0:256])
    part = dot_nt(gated[:, 0:128], held[0, :, 896:1024]) + dot_nt(
        gated[:, 128:384], held[1, :, 768:1024]
    )
    part_ref[...] = part.astype(jnp.bfloat16)
    for copy in copies:
        copy.wait()


def mlp_kernel(
    live_ref,
    tokens_ref,
    part_ref,
    peer_ref,
    cotangent_ref,
    ext_ref,
    mine_ref,
    other_ref,
    middle_ref,
    normed_ref,
    hidden_mine_ref,
    hidden_other_ref,
    out_ref,
    grad_ref,
    held,
    sems,
):
    core, first_copy, second_copy = load_halves(mine_ref, other_ref, held, sems)
    middle = tokens_ref[...].astype(jnp.float32) + (
        part_ref[...].astype(jnp.float32) + peer_ref[...].astype(jnp.float32)
    )
    middle_ref[...] = middle
    gains = gain_rows(ext_ref[...])
    scale = lax.rsqrt(jnp.mean(middle * middle, axis=1, keepdims=True) + epsilon)
    normed = (middle * scale * gains[1:2]).astype(jnp.bfloat16)
    normed_ref[...] = normed
    live_rows = lax.broadcasted_iota(jnp.int32, (384, 1), 0) < live_ref[0]
    grad_out = jnp.where(live_rows, cotangent_ref[...].astype(jnp.float32), 0.0)
    grad_out = grad_out.astype(jnp.bfloat16)
    first_copy.wait()
    second_copy.wait()
    out_total = jnp.zeros((384, 768), jnp.float32)
    grad_total = jnp.zeros((384, 768), jnp.float32)
    parts = []
    for half in range(2):
        begin = half * 512
        gate_w = held[0, :, begin : begin + 512]
        up_w = held[1, :, begin : begin + 512]
        down_w = held[half, :, 1024:1536]
        gate = dot_nn(normed, gate_w)
        up = dot_nn(normed, up_w)
        sig = jax.nn.sigmoid(gate)
        silu = gate * sig
        active = (silu * up).astype(jnp.bfloat16)
        out_total = out_total + dot_nt(active, down_w)
        grad_act = dot_nn(grad_out, down_w)
        grad_up = (grad_act * silu).astype(jnp.bfloat16)
        grad_gate = (grad_act * up * (sig * (1.0 + gate * (1.0 - sig)))).astype(jnp.bfloat16)
        parts.append((grad_gate, grad_up, active))
        grad_total = grad_total + dot_nt(grad_gate, gate_w) + dot_nt(grad_up, up_w)
    for number in range(3):
        lanes = slice(number * 512, number * 512 + 512)
        first, second = parts[0][number], parts[1][number]
        hidden_mine_ref[:, lanes] = jnp.where(core == 0, first, second)
        hidden_other_ref[:, lanes] = jnp.where(core == 0, second, first)
    out_ref[...] = out_total.astype(jnp.bfloat16)
    grad_ref[...] = grad_total.astype(jnp.bfloat16)


def attend_back_kernel(
    after_ref,
    live_ref,
    tokens_ref,
    cotangent_ref,
    middle_ref,
    grad_part_ref,
    grad_peer_ref,
    mine_ref,
    other_ref,
    gains_ref,
    doc_col_ref,
    doc_row_ref,
    normed_ref,
    raw_in,
    heads_in,
    lanes_in,
    grad_middle_ref,
    grad_middle_b_ref,
    proj_mine_ref,
    proj_other_ref,
    norm_part_ref,
    extra_ref,
    held,
    sems,
    grad_att_ref,
    grad_query_ref,
    grad_key_ref,
    grad_value_ref,
    grad_og_ref,
    column_ref,
    raw_ref,
    heads_ref,
    lanes_ref,
):
    core, first_copy, second_copy = load_halves(mine_ref, other_ref, held, sems)
    copies = [
        pltpu.make_async_copy(source, target, sems.at[2 + number])
        for number, (source, target) in enumerate(
            ((raw_in, raw_ref), (heads_in, heads_ref), (lanes_in, lanes_ref))
        )
    ]
    for copy in copies:
        copy.start()
    query_raw_ref, key_raw_ref, gate_ref, attended_ref = [raw_ref.at[n] for n in range(4)]
    query_ref, key_ref, value_ref = [heads_ref.at[n] for n in range(3)]
    logit_ref, decay_ref, total_ref = [lanes_ref.at[n] for n in range(3)]
    live_count = live_ref[0]
    inv_root = 0.125
    middle = middle_ref[...]
    grad_normed = grad_part_ref[...].astype(jnp.float32) + grad_peer_ref[...].astype(jnp.float32)
    live_rows = lax.broadcasted_iota(jnp.int32, (384, 1), 0) < live_count
    grad_out = jnp.where(live_rows, cotangent_ref[...].astype(jnp.float32), 0.0)
    scale = lax.rsqrt(jnp.mean(middle * middle, axis=1, keepdims=True) + epsilon)
    first_copy.wait()
    second_copy.wait()
    ext = held[0, :, 768:896]
    gains = gain_rows(ext)
    gained = grad_normed * gains[1:2]
    inner = jnp.mean(gained * middle, axis=1, keepdims=True)
    grad_middle = grad_out + (scale * gained - middle * (scale * scale * scale * inner))
    grad_gain = jnp.sum(grad_normed * middle * scale, axis=0, keepdims=True)
    grad_middle_ref[...] = grad_middle
    grad_middle_b = grad_middle.astype(jnp.bfloat16)
    grad_middle_b_ref[...] = grad_middle_b
    grad_gated = jnp.concatenate(
        [
            dot_nn(grad_middle_b, held[0, :, 896:1024]),
            dot_nn(grad_middle_b, held[1, :, 768:1024]),
        ],
        axis=1,
    )
    for copy in copies:
        copy.wait()
    sig = jax.nn.sigmoid(gate_ref[...])
    grad_att_ref[...] = (grad_gated * sig).astype(jnp.bfloat16)
    grad_og = (grad_gated * attended_ref[...] * sig * (1.0 - sig)).astype(jnp.bfloat16)
    grad_og_ref[...] = grad_og
    grad_key_ref[...] = jnp.zeros((384, 384), jnp.float32)
    grad_value_ref[...] = jnp.zeros((384, 384), jnp.float32)
    column_ref[...] = jnp.zeros((128, 384), jnp.float32)
    decay = decay_ref[...]
    decay_t = decay.T
    row_parts = []
    for step in range(3):
        begin, count = step * 128, step * 128 + 128
        allowed = allowed_block(
            doc_col_ref[begin : begin + 128, :],
            doc_row_ref[:, 0:count],
            live_count,
            begin,
            128,
            count,
        )
        small_lane = lax.broadcasted_iota(jnp.int32, (128, 128), 1)
        row_sums = jnp.zeros((128, 128), jnp.float32)
        for block in range(3):
            lanes = slice(block * 128, block * 128 + 128)
            keys = key_ref[0:count, lanes]
            values = value_ref[0:count, lanes]
            query_pair = query_ref[begin : begin + 128, lanes]
            att_pair = grad_att_ref[begin : begin + 128, lanes]
            outs = []
            key_outs = []
            value_outs = []
            for half in range(2):
                head = block * 2 + half
                mask = head_mask(128, half)
                query = jnp.where(mask, query_pair, jnp.zeros_like(query_pair))
                att = jnp.where(mask, att_pair, jnp.zeros_like(att_pair))
                scores = block_scores(
                    query,
                    keys,
                    lane_pick(decay[begin : begin + 128], head),
                    decay_t[head : head + 1, 0:count],
                    allowed,
                    inv_root,
                )
                probs = jnp.exp(scores - lane_pick(total_ref[begin : begin + 128, :], head))
                grad_probs = dot_nt(att, values)
                row_dot = jnp.sum(probs * grad_probs, axis=1, keepdims=True)
                grad_scores = (probs * (grad_probs - row_dot)).astype(jnp.bfloat16)
                grad_scores_f = grad_scores.astype(jnp.float32)
                row_sums = jnp.where(
                    small_lane == head,
                    jnp.sum(grad_scores_f, axis=1, keepdims=True),
                    row_sums,
                )
                column_ref[head : head + 1, 0:count] += jnp.sum(
                    grad_scores_f, axis=0, keepdims=True
                )
                outs.append(dot_nn(grad_scores, keys))
                key_outs.append(dot_tn(grad_scores, query))
                value_outs.append(dot_tn(probs.astype(jnp.bfloat16), att))
            grad_query_ref[begin : begin + 128, lanes] = jnp.where(
                head_mask(128, 0), outs[0], outs[1]
            )
            grad_key_ref[0:count, lanes] += key_outs[0] + key_outs[1]
            grad_value_ref[0:count, lanes] += value_outs[0] + value_outs[1]
        row_parts.append(row_sums)
    grad_decay = jnp.concatenate(row_parts, axis=0) - column_ref[...].T
    rows = lax.broadcasted_iota(jnp.int32, (384, 384), 0)
    columns = lax.broadcasted_iota(jnp.int32, (384, 384), 1)
    upper = (columns >= rows).astype(jnp.float32).astype(jnp.bfloat16)
    grad_logit = exact_nn(upper, grad_decay) * jax.nn.sigmoid(-logit_ref[...])
    lane = lax.broadcasted_iota(jnp.int32, (384, 128), 1)
    grad_logit = jnp.where(lane < 6, grad_logit, 0.0)
    grad_forget = grad_logit.astype(jnp.bfloat16)
    grad_vg = jnp.concatenate([grad_value_ref[...].astype(jnp.bfloat16), grad_og_ref[...]], axis=1)
    grad_qk = []
    gain_sums = []
    for number, raw_ref, out_ref in (
        (0, query_raw_ref, grad_query_ref),
        (1, key_raw_ref, grad_key_ref),
    ):
        gain = gains_ref[number : number + 1]
        gain_sum = jnp.zeros((1, 128), jnp.float32)
        for block in range(3):
            lanes = slice(block * 128, block * 128 + 128)
            raw = raw_ref[:, lanes]
            grad = (out_ref[:, lanes] * inv_root).astype(jnp.bfloat16).astype(jnp.float32)
            first = head_mask(384, 0)
            scaled = pair_rms(raw, 1.0)[1]
            weighted = grad * gain
            product = weighted * raw
            sum_first = jnp.sum(jnp.where(first, product, 0.0), axis=1, keepdims=True)
            sum_second = jnp.sum(jnp.where(first, 0.0, product), axis=1, keepdims=True)
            inner_head = jnp.where(first, sum_first, sum_second) * (1.0 / 64.0)
            gain_sum = gain_sum + jnp.sum(grad * raw * scaled, axis=0, keepdims=True)
            grad_raw = scaled * weighted - raw * (scaled * scaled * scaled * inner_head)
            grad_qk.append(grad_raw.astype(jnp.bfloat16))
        gain_sums.append(gain_sum)
    grad_qk = jnp.concatenate(grad_qk, axis=1)
    proj_mine_ref[...] = jnp.where(core == 0, grad_qk, grad_vg)
    proj_other_ref[...] = jnp.where(core == 0, grad_vg, grad_qk)
    part = dot_nt(grad_qk, held[0, :, 0:768])
    part = part + dot_nt(grad_vg, held[1, :, 0:768])
    part = part + dot_nt(grad_forget, ext)
    norm_part_ref[...] = part.astype(jnp.bfloat16)
    hidden = tokens_ref[...].astype(jnp.float32)
    scale = lax.rsqrt(jnp.mean(hidden * hidden, axis=1, keepdims=True) + epsilon)
    first_gain = jnp.sum(part * (hidden * scale), axis=0, keepdims=True)
    line = lax.broadcasted_iota(jnp.int32, (128, 768), 0)
    extra = jnp.where(line == 6, first_gain, jnp.where(line == 7, grad_gain, 0.0)).T
    extra = extra + dot_tn(normed_ref[...], grad_forget)
    bias_sum = jnp.sum(grad_forget.astype(jnp.float32), axis=0, keepdims=True)
    sums = [total + pltpu.roll(total, 64, 1) for total in (gain_sums[0], gain_sums[1], bias_sum)]
    line = lax.rem(lax.broadcasted_iota(jnp.int32, (768, 128), 0), 12)
    lane = lax.broadcasted_iota(jnp.int32, (768, 128), 1)
    for number in range(3):
        extra = jnp.where((line == number) & (lane >= 64), sums[number], extra)
    extra_ref[...] = extra.astype(jnp.bfloat16)


def pair_grad_kernel(width, start, total_width, *refs):
    first, first_peer, left, left_peer, second, second_peer, right, right_peer = refs[:8]
    out_ref = refs[-1]
    if len(refs) > 9:
        out_ref = refs[-2]
        out_ref[:, total_width:] = refs[8][...]
        added = refs[10][...].astype(jnp.float32) + refs[11][...].astype(jnp.float32)
        refs[-1][...] = (refs[9][...] + added).astype(jnp.bfloat16)
    for begin in range(0, total_width, 256):
        if begin < width:
            lanes = slice(begin, begin + 256)
            total = dot_tn(first[...], left[:, lanes])
            total = total + dot_tn(first_peer[...], left_peer[:, lanes])
        else:
            lanes = slice(start + begin - width, start + begin - width + 256)
            total = dot_tn(second[...], right[:, lanes])
            total = total + dot_tn(second_peer[...], right_peer[:, lanes])
        out_ref[:, begin : begin + 256] = total.astype(jnp.bfloat16)


def mirror(out_ref, block, start):
    out_ref[start : start + 256, start:768] = block.astype(jnp.bfloat16)
    for other in range(start + 256, 768, 256):
        piece = block[:, other - start : other - start + 256]
        out_ref[other : other + 256, start : start + 256] = piece.T.astype(jnp.bfloat16)


def plane_sum_kernel(after_ref, later_ref, blocks_ref, mine_ref, other_ref):
    level = lax.rem(lax.axis_index("dp") // 2, 2)
    for start in range(0, blocks_ref.shape[2], 256):
        lanes = slice(start, start + 256)
        total = blocks_ref[0, :, lanes].astype(jnp.float32)
        for number in range(1, 16):
            total = total + blocks_ref[number, :, lanes].astype(jnp.float32)
        first, second = total[0:24], total[24:48]
        mine_ref[:, lanes] = jnp.where(level == 0, first, second)
        other_ref[:, lanes] = jnp.where(level == 0, second, first)


def momentum_kernel(
    mine_ref,
    other_ref,
    old_ref,
    tokens_ref,
    grad_middle_ref,
    norm_part_ref,
    norm_peer_ref,
    ext_ref,
    new_ref,
    keep_ref,
    send_ref,
    small_ref,
    input_grad_ref,
):
    place = lax.axis_index("dp")
    core, level = lax.rem(place, 2), lax.rem(place // 2, 2)
    mine, other = mine_ref[...], other_ref[...]
    even = jnp.where(core == 0, mine, other)
    odd = jnp.where(core == 0, other, mine)
    small_ref[...] = mine[:, 1024:1152] + other[:, 1024:1152]
    fresh = [even[:, 0:384], even[:, 384:768], odd[:, 0:384], odd[:, 384:768]]
    fresh.append(jnp.concatenate([even[:, 768:1024], odd[:, 896:1024]], axis=1))
    fresh = [muon_decay * old_ref[number] + fresh[number] for number in range(5)]
    for number in range(5):
        new_ref[number] = fresh[number]
    for number in range(4):
        keep_ref[number] = jnp.where(level == 0, fresh[4], fresh[number])
        send_ref[number] = jnp.where(level == 0, fresh[number], fresh[4])
    hidden = tokens_ref[...].astype(jnp.float32)
    gain = gain_rows(ext_ref[...])[0:1]
    grad = norm_part_ref[...].astype(jnp.float32) + norm_peer_ref[...].astype(jnp.float32)
    scale = lax.rsqrt(jnp.mean(hidden * hidden, axis=1, keepdims=True) + epsilon)
    gained = grad * gain
    inner = jnp.mean(gained * hidden, axis=1, keepdims=True)
    input_grad_ref[...] = grad_middle_ref[...] + (
        scale * gained - hidden * (scale * scale * scale * inner)
    )


def small_kernel(
    mine_ref,
    peer_ref,
    norm_ref,
    qk_ref,
    forget_ref,
    bias_ref,
    m_norm_ref,
    m_qk_ref,
    m_forget_ref,
    m_bias_ref,
    after_ref,
    new_norm_ref,
    new_qk_ref,
    new_forget_ref,
    new_bias_ref,
    mom_norm_ref,
    mom_qk_ref,
    mom_forget_ref,
    mom_bias_ref,
):
    root_tokens = math.sqrt(24576.0)
    mine, both = mine_ref[...], mine_ref[...] + peer_ref[...]
    lane = lax.broadcasted_iota(jnp.int32, (12, 128), 1)
    norms = jnp.where(lane == 6, both, mine).T
    grads = (
        (norms[6:8, :], gain_rate, norm_ref, m_norm_ref, new_norm_ref, mom_norm_ref),
        (both[0:2, 64:128], qk_rate, qk_ref, m_qk_ref, new_qk_ref, mom_qk_ref),
        (mine[:, 0:6], forget_rate, forget_ref, m_forget_ref, new_forget_ref, mom_forget_ref),
        (mine[2:3, 64:70], bias_rate, bias_ref, m_bias_ref, new_bias_ref, mom_bias_ref),
    )
    for grad, rate, value_ref, old_ref, new_ref, mom_ref in grads:
        moment = plain_decay * old_ref[...] + grad
        mom_ref[...] = moment
        new_ref[...] = value_ref[...] - (rate / root_tokens) * moment


def newton_body(sources, out_ref, held, square_ref, poly_ref):
    total = jnp.zeros((1, 1), jnp.float32)
    for source in sources:
        for number in range(8):
            for start in (0, 48):
                piece = source[number, start : start + 48, :].astype(jnp.float32)
                piece = jnp.sum(piece * piece, axis=0, keepdims=True)
                total = total + jnp.sum(piece, axis=1, keepdims=True)
    scale = 1.0 / (jnp.sqrt(total) + 1e-07)
    for place, source in zip((0, 384), sources):
        for number in range(8):
            for start in (0, 48):
                piece = source[number, start : start + 48, :].astype(jnp.float32) * scale
                begin = place + (number % 4) * 96 + start
                held[0, number // 4, begin : begin + 48, :] = piece.astype(jnp.bfloat16)
    for repeat in range(5):
        now, later = repeat % 2, (repeat + 1) % 2
        for start in range(0, 768, 256):
            rows, right = slice(start, start + 256), slice(start, 768)
            square = dot_nt(held[now, 0, rows, :], held[now, 0, right, :])
            square = square + dot_nt(held[now, 1, rows, :], held[now, 1, right, :])
            mirror(square_ref, square, start)
        if repeat < 4:
            for start in range(0, 768, 256):
                rows, right = slice(start, start + 256), slice(start, 768)
                poly = coef_b * square_ref[rows, right].astype(jnp.float32)
                poly = poly + coef_c * dot_nn(square_ref[rows, :], square_ref[:, right])
                mirror(poly_ref, poly, start)
            for side in range(2):
                for start in range(0, 768, 256):
                    grown = coef_a * held[now, side, start : start + 256, :].astype(jnp.float32)
                    grown = grown + dot_nn(poly_ref[start : start + 256, :], held[now, side])
                    held[later, side, start : start + 256, :] = grown.astype(jnp.bfloat16)
        else:
            side = lax.axis_index("tensor")
            begin = pl.multiple_of((lax.axis_index("dp") // 16) * 96, 16)
            few = square_ref[pl.ds(begin, 96), :]
            poly = coef_b * few.astype(jnp.float32) + coef_c * dot_nn(few, square_ref[...])
            poly = poly.astype(jnp.bfloat16)
            grown = coef_a * held[now, side, pl.ds(begin, 96), :].astype(jnp.float32)
            grown = grown + dot_nn(poly, held[now, side])
            out_ref[...] = grown.astype(jnp.bfloat16)


def newton_kernel(wants_wide, after_ref, mine_ref, other_ref, out_ref, *scratch):
    place = lax.axis_index("dp")
    is_wide = (lax.rem(place // 2, 2) == 0) & (lax.rem(place // 4, 4) < 3)
    active = is_wide if wants_wide else jnp.logical_not(is_wide)

    @pl.when(active)
    def run():
        newton_body((mine_ref, other_ref), out_ref, *scratch)

    @pl.when(jnp.logical_not(active))
    def skip():
        out_ref[...] = jnp.zeros(out_ref.shape, jnp.bfloat16)


in_vmem = pl.BlockSpec(memory_space=pltpu.VMEM)
in_smem = pl.BlockSpec(memory_space=pltpu.SMEM)
in_any = pl.BlockSpec(memory_space=pl.ANY)
in_hbm = pl.BlockSpec(memory_space=pltpu.HBM)


def call_kernel(kernel, in_specs, outs, scratch, flops, limit=24, far=()):
    return pl.pallas_call(
        kernel,
        out_shape=[jax.ShapeDtypeStruct(shape, dtype) for shape, dtype in outs],
        in_specs=in_specs,
        out_specs=[in_hbm if number in far else in_vmem for number in range(len(outs))],
        scratch_shapes=scratch,
        compiler_params=pltpu.CompilerParams(vmem_limit_bytes=limit * 1024 * 1024),
        cost_estimate=pl.CostEstimate(flops=flops, bytes_accessed=10000000, transcendentals=0),
    )


def pair_grad(first, left, second, right, width, start, total, extra=()):
    operands = [*first, *left, *second, *right, *extra]
    outs = [((768, total + (128 if extra else 0)), jnp.bfloat16)]
    if extra:
        outs.append((extra[-1].shape, jnp.bfloat16))
    return call_kernel(
        functools.partial(pair_grad_kernel, width, start, total),
        [in_vmem] * len(operands),
        outs,
        [],
        2 * 768 * 768 * total,
        56,
    )(*operands)


def newton(wants_wide, after, mine, other):
    columns = mine.shape[2]
    return call_kernel(
        functools.partial(newton_kernel, wants_wide),
        [in_any] + [in_vmem] * 2,
        [((96, columns), jnp.bfloat16)],
        [
            pltpu.VMEM((2, 2, 768, columns), jnp.bfloat16),
            pltpu.VMEM((768, 768), jnp.bfloat16),
            pltpu.VMEM((768, 768), jnp.bfloat16),
        ],
        200000000000 if wants_wide else 10000000000,
    )(after, mine, other)[0]


def spread_slots(slots_b):
    column = place_of("x")

    def slot(step):
        number = jnp.minimum((column + step) % 4, slots_b.shape[0] - 1)
        return lax.dynamic_index_in_dim(slots_b, number, 0, keepdims=False)

    pieces = [slot(0)] + [fetch(slot(4 - step), "x", step) for step in (1, 2, 3)]
    return jnp.concatenate(pieces, axis=0)


def ring_order(rows, count):
    column = place_of("x")
    blocks = rows.reshape(4, 24, count)
    return jnp.stack(
        [lax.dynamic_index_in_dim(blocks, (n - column) % 4, 0, False) for n in range(4)]
    )


def on_device(
    tokens,
    cotangent,
    segment_ids,
    live_len,
    w_square,
    w_wide,
    norm_gain,
    qk_gain,
    forget_w,
    forget_b,
    m_square,
    m_wide,
    m_norm,
    m_qk,
    m_forget_w,
    m_forget_b,
    ema_square,
    ema_wide,
):
    half_width = w_square.shape[2]
    half_hidden = w_wide.shape[2]
    shard_rows = w_square.shape[1]
    head_local = forget_w.shape[1]
    head_dim = qk_gain.shape[1]
    dp_size = lax.axis_size("dp")
    full_width = shard_rows * dp_size
    full_hidden = half_hidden * lax.axis_size("tensor")
    my_place = lax.axis_index("dp")
    core = my_place % 2
    quarter_hidden = half_hidden // 2
    bf16, f32 = jnp.bfloat16, jnp.float32

    square_b = w_square.astype(bf16)
    wide_b = w_wide.astype(bf16)
    extras = jnp.concatenate(
        [
            forget_w.astype(bf16),
            norm_gain.astype(bf16).T,
            jnp.zeros((shard_rows, 120), bf16),
        ],
        axis=1,
    )
    even = [square_b[0], square_b[1, :, :128]]
    even += [wide_b[0, :, :768]]
    even += [square_b[1, :, 128:], extras, square_b[4, :, :128]]
    even += [wide_b[0, :, 768:], wide_b[2, :, :quarter_hidden]]
    odd = [square_b[2], square_b[3, :, :128]]
    odd += [wide_b[1, :, :768]]
    odd += [square_b[3, :, 128:], square_b[4, :, 128:]]
    odd += [wide_b[1, :, 768:], wide_b[2, :, quarter_hidden:]]
    even = jnp.concatenate(even, axis=1)
    odd = jnp.concatenate(odd, axis=1)
    pair_rows = pair_join(core, by_core(core, even, odd), core_swap(by_core(core, odd, even)), 0)
    quad_rows = pair_join(place_of("l"), pair_rows, fetch(pair_rows, "l", 1), 0)
    row_plane = gather(quad_rows[:, :1280], ("x",))
    blocks_y = fetch_ring(quad_rows[:, 1280:], "y")
    first_plane = gather(row_plane[:, :, :512], ("y",))
    first_blocks = fetch_ring(jnp.stack([block[:, :512] for block in blocks_y]), "x")
    late_plane = jnp.broadcast_to(row_plane[None, :, :, 512:], (4, 4, 48, 768))
    late_stack = jnp.stack([block[:, 512:] for block in blocks_y])
    late_plane, late_stack, first_plane, first_blocks = lax.optimization_barrier(
        (late_plane, late_stack, first_plane, first_blocks)
    )
    first_mine = assemble(first_plane.reshape(4, 4, 48, 512), first_blocks)
    first_other = core_swap(first_mine)
    late_plane = exchange(late_plane, ("y",))
    late_blocks = fetch_ring(late_stack, "x")
    ext = by_core(core, first_mine[:, 768:896], first_other[:, 768:896])

    gains_b = qk_gain.astype(bf16).astype(f32)
    gains = jnp.concatenate([gains_b, gains_b], axis=1)
    bias_row = jnp.pad(forget_b.astype(bf16).astype(f32), (0, 128 - head_local))[None]
    doc_row = segment_ids
    doc_col = segment_ids.reshape(-1, 1)
    live_mask = (jnp.arange(tokens.shape[0]) < live_len[0])[:, None]
    grad_out_b = jnp.where(live_mask, cotangent, jnp.zeros_like(cotangent))

    def paired(mine, other):
        return mine, core_swap(other)

    token_h = ((384, 768), bf16)
    token_f = ((384, 768), f32)
    (
        normed_one,
        raw,
        heads,
        gated_mine,
        gated_other,
        attn_part,
        head_lanes,
    ) = call_kernel(
        attend_kernel,
        [in_smem, in_vmem, in_any, in_any] + [in_vmem] * 4,
        [token_h, ((4, 384, 384), f32), ((3, 384, 384), bf16)]
        + [((384, 256), bf16)] * 2
        + [token_h, ((3, 384, 128), f32)],
        [
            pltpu.VMEM((2, 768, 1024), bf16),
            pltpu.SemaphoreType.DMA((5,)),
            pltpu.VMEM((4, 384, 384), f32),
            pltpu.VMEM((3, 384, 384), bf16),
            pltpu.VMEM((3, 384, 128), f32),
        ],
        4000000000,
        24,
        (1, 2, 6),
    )(live_len, tokens, first_mine, first_other, gains, bias_row, doc_col, doc_row)
    attn_peer = tensor_swap(attn_part)
    late_plane, late_blocks, attn_part = lax.optimization_barrier(
        (late_plane, late_blocks, attn_part)
    )
    second_mine = assemble(late_plane, late_blocks)
    second_other = core_swap(second_mine)
    normed_one_pair = paired(normed_one, normed_one)
    gated_pair = paired(gated_mine, gated_other)
    grad_out_pair = paired(grad_out_b, grad_out_b)
    attn_peer, normed_one_pair, gated_pair, grad_out_pair = lax.optimization_barrier(
        (attn_peer, normed_one_pair, gated_pair, grad_out_pair)
    )
    middle, normed_two, hidden_mine, hidden_other, mlp_part, grad_part = call_kernel(
        mlp_kernel,
        [in_smem] + [in_vmem] * 5 + [in_any] * 2,
        [token_f, token_h, ((384, 1536), bf16), ((384, 1536), bf16), token_h, token_h],
        [pltpu.VMEM((2, 768, 1536), bf16), pltpu.SemaphoreType.DMA((2,))],
        5000000000,
        56,
    )(live_len, tokens, attn_part, attn_peer, cotangent, ext, second_mine, second_other)
    grad_peer = tensor_swap(grad_part)

    normed_two_pair = paired(normed_two, normed_two)
    hidden_pair = paired(hidden_mine, hidden_other)
    grad_wide_b = pair_grad(
        normed_two_pair, hidden_pair, grad_out_pair, hidden_pair, 1024, 1024, 1536
    )[0]
    level = place_of("l")
    wide_blocks = exchange(grad_wide_b.reshape(16, 48, 3 * quarter_hidden), ("y", "x"))

    (
        grad_middle,
        grad_middle_b,
        proj_mine,
        proj_other,
        norm_part,
        extra,
    ) = call_kernel(
        attend_back_kernel,
        [in_any, in_smem] + [in_vmem] * 5 + [in_any] * 2 + [in_vmem] * 4 + [in_hbm] * 3,
        [token_f, token_h, token_h, token_h, token_h, ((768, 128), bf16)],
        [
            pltpu.VMEM((2, 768, 1024), bf16),
            pltpu.SemaphoreType.DMA((5,)),
            pltpu.VMEM((384, 384), bf16),
            pltpu.VMEM((384, 384), f32),
            pltpu.VMEM((384, 384), f32),
            pltpu.VMEM((384, 384), f32),
            pltpu.VMEM((384, 384), bf16),
            pltpu.VMEM((128, 384), f32),
            pltpu.VMEM((4, 384, 384), f32),
            pltpu.VMEM((3, 384, 384), bf16),
            pltpu.VMEM((3, 384, 128), f32),
        ],
        100000000000,
        56,
    )(
        grad_wide_b,
        live_len,
        tokens,
        cotangent,
        middle,
        grad_part,
        grad_peer,
        first_mine,
        first_other,
        gains,
        doc_col,
        doc_row,
        normed_one,
        raw,
        heads,
        head_lanes,
    )
    proj_pair = paired(proj_mine, proj_other)
    grad_middle_pair = paired(grad_middle_b, grad_middle_b)
    mlp_peer = tensor_swap(mlp_part)
    grad_proj_b, result = pair_grad(
        normed_one_pair,
        proj_pair,
        grad_middle_pair,
        gated_pair,
        768,
        0,
        1024,
        [extra, middle, mlp_part, mlp_peer],
    )
    norm_peer = tensor_swap(norm_part)
    mine, other = call_kernel(
        plane_sum_kernel,
        [in_any] * 2 + [in_vmem],
        [((24, 3 * quarter_hidden), f32)] * 2,
        [],
        100000000,
    )(grad_proj_b, norm_peer, wide_blocks)
    other = other.astype(bf16)
    mine, other = pair_split(core, mine + fetch(other, "l", 1).astype(f32), 0)
    other = core_swap(other)
    wide_shard = jnp.stack(
        [
            pair_join(core, mine[:, start : start + 512], other[:, start : start + 512], 1)
            for start in (0, 512, 1024)
        ]
    )
    mom_wide = muon_decay * m_wide + wide_shard

    wide_slots = mom_wide.astype(bf16)
    wide_pair = jnp.concatenate([wide_slots, fetch(wide_slots, "l", 1)], axis=1)
    wide_rows = spread_slots(wide_pair)
    proj_blocks = exchange(grad_proj_b.reshape(32, 24, 1152), ("y", "x", "l"))
    proj_blocks, wide_rows = lax.optimization_barrier((proj_blocks, wide_rows))
    wide_own = gather(wide_rows, ("t", "y"))
    mine, other = pair_split(core, jnp.sum(proj_blocks.astype(f32), axis=0), 0)
    other = core_swap(other)
    mom_square, keep_slots, send_slots, small, input_grad = call_kernel(
        momentum_kernel,
        [in_vmem] * 8,
        [
            ((5, 12, half_width), f32),
            ((4, 12, half_width), f32),
            ((4, 12, half_width), f32),
            ((12, 128), f32),
            token_f,
        ],
        [],
        10000000,
        24,
    )(mine, other, m_square, tokens, grad_middle, norm_part, norm_peer, ext)
    keep_slots, send_slots = keep_slots.astype(bf16), send_slots.astype(bf16)
    proj_rows = spread_slots(pair_join(level, keep_slots, fetch(send_slots, "l", 1), 1))
    wide_own, proj_rows = lax.optimization_barrier((wide_own, proj_rows))
    wide_other = core_swap(wide_own)
    proj_own = gather(proj_rows, ("t", "y"))
    wide_rows = newton(True, small, wide_own, wide_other)
    proj_own, wide_rows = lax.optimization_barrier((proj_own, wide_rows))
    proj_rows = newton(False, wide_rows, proj_own, core_swap(proj_own))
    proj_rows = jnp.pad(proj_rows, ((0, 0), (0, half_hidden - half_width)))
    rows = ring_order(proj_rows + wide_rows, half_hidden).reshape(8, 12, half_hidden)
    update = exchange(rows, ("x", "l")).astype(f32)
    update_wide = update[0:6:2]
    update_square = jnp.concatenate([update[1::2], update[6:7]], axis=0)[:, :, :half_width]

    small_peer = tensor_swap(small)
    (
        new_norm,
        new_qk,
        new_forget_w,
        new_forget_b,
        mom_norm,
        mom_qk,
        mom_forget_w,
        mom_forget_b,
    ) = call_kernel(
        small_kernel,
        [in_vmem] * 10 + [in_any],
        [(value.shape, f32) for value in (norm_gain, qk_gain, forget_w)]
        + [((1, head_local), f32)]
        + [(value.shape, f32) for value in (norm_gain, qk_gain, forget_w)]
        + [((1, head_local), f32)],
        [],
        100000,
        8,
    )(
        small,
        small_peer,
        norm_gain,
        qk_gain,
        forget_w,
        forget_b[None],
        m_norm,
        m_qk,
        m_forget_w,
        m_forget_b[None],
        proj_rows,
    )
    new_forget_b, mom_forget_b = new_forget_b[0], mom_forget_b[0]
    new_square = w_square - update_square
    new_wide = w_wide - math.sqrt(full_hidden / full_width) * update_wide
    new_ema_square = ema_decay * ema_square + (1.0 - ema_decay) * new_square
    new_ema_wide = ema_decay * ema_wide + (1.0 - ema_decay) * new_wide
    return (
        result,
        input_grad,
        new_square,
        new_wide,
        new_norm,
        new_qk,
        new_forget_w,
        new_forget_b,
        mom_square,
        mom_wide,
        mom_norm,
        mom_qk,
        mom_forget_w,
        mom_forget_b,
        new_ema_square,
        new_ema_wide,
    )


def solution(mesh):
    placed = (
        P("dp", None),
        P("dp", None),
        P("dp", None),
        P("dp"),
        P(None, "dp", "tensor"),
        P(None, "dp", "tensor"),
        P(None, "dp"),
        P(),
        P("dp", "tensor"),
        P("tensor"),
        P(None, "dp", "tensor"),
        P(None, "dp", "tensor"),
        P(None, "dp"),
        P(),
        P("dp", "tensor"),
        P("tensor"),
        P(None, "dp", "tensor"),
        P(None, "dp", "tensor"),
    )
    return jax.shard_map(
        on_device,
        mesh=mesh,
        in_specs=placed,
        out_specs=(
            P("dp", None),
            P("dp", None),
            P(None, "dp", "tensor"),
            P(None, "dp", "tensor"),
            P(None, "dp"),
            P(),
            P("dp", "tensor"),
            P("tensor"),
            P(None, "dp", "tensor"),
            P(None, "dp", "tensor"),
            P(None, "dp"),
            P(),
            P("dp", "tensor"),
            P("tensor"),
            P(None, "dp", "tensor"),
            P(None, "dp", "tensor"),
        ),
        check_vma=False,
    )
```

```python
import functools
import math

import jax
import jax.numpy as jnp
from jax import lax
import numpy as np
from jax.experimental import pallas as pl
from jax.experimental.pallas import tpu as pltpu
from jax.sharding import PartitionSpec as P

epsilon = 1e-06
coef_a = 3.4445
coef_b = -4.775
coef_c = 2.0315
muon_decay = 0.95
plain_decay = 0.9
ema_decay = 0.7
gain_rate = 0.2
qk_rate = 0.05
forget_rate = 0.1
bias_rate = 0.5


grid_sizes = {"y": 4, "x": 4, "l": 2, "c": 2, "t": 2}
dp_names = ["y", "x", "l", "c"]


def ring_groups(names, over):
    order = [name for name in over if name not in names]
    table = np.arange(math.prod(grid_sizes[name] for name in over))
    table = table.reshape([grid_sizes[name] for name in over])
    table = table.transpose([over.index(name) for name in order + list(names)])
    return table.reshape(-1, math.prod(grid_sizes[name] for name in names)).tolist()


def exchange(blocks, names):
    axes = ("dp", "tensor") if "t" in names else "dp"
    return lax.all_to_all(
        blocks,
        axes,
        split_axis=0,
        concat_axis=0,
        tiled=True,
        axis_index_groups=ring_groups(names, dp_names + (["t"] if "t" in names else [])),
    )


def gather(block, names):
    count = math.prod(grid_sizes[name] for name in names)
    return exchange(jnp.broadcast_to(block[None], (count,) + block.shape), names)


def place_of(name):
    place = lax.axis_index("dp")
    return {"y": place // 16, "x": (place // 4) % 4, "l": (place // 2) % 2, "c": place % 2}[name]


def fetch(array, name, step):
    table = np.arange(64).reshape(4, 4, 2, 2)
    sources = np.roll(table, -step, axis=dp_names.index(name))
    pairs = [(int(a), int(b)) for a, b in zip(sources.ravel(), table.ravel())]
    return lax.ppermute(array, "dp", pairs)


def fetch_ring(array, name):
    return [array] + [fetch(array, name, step) for step in (1, 3, 2)]


ring_steps = (0, 1, 3, 2)


def core_swap(array):
    return fetch(array, "c", 1)


def tensor_swap(array):
    return lax.ppermute(array, "tensor", [(0, 1), (1, 0)])


def by_core(core, even, odd):
    return jnp.where(core == 0, even, odd)


def pair_join(place, mine, other, axis):
    return jnp.where(
        place == 0,
        jnp.concatenate([mine, other], axis=axis),
        jnp.concatenate([other, mine], axis=axis),
    )


def pair_split(core, array, axis):
    first, second = jnp.split(array, 2, axis=axis)
    return by_core(core, first, second), by_core(core, second, first)


def pack_kernel(square_ref, wide_ref, norm_ref, forget_ref, mine_ref, other_ref):
    core = lax.rem(lax.axis_index("dp"), 2)
    eye = lax.broadcasted_iota(jnp.int32, (12, 12), 0)
    eye = eye == lax.broadcasted_iota(jnp.int32, (12, 12), 1)
    lane = lax.broadcasted_iota(jnp.int32, (12, 128), 1)
    extra = jnp.concatenate([forget_ref[...], jnp.zeros((12, 122), jnp.float32)], axis=1)
    for number in range(2):
        gain = jnp.sum(jnp.where(eye, norm_ref[number : number + 1], 0.0), axis=1, keepdims=True)
        extra = jnp.where(lane == 6 + number, gain, extra)
    even = [square_ref[0], square_ref[1, :, 0:128], wide_ref[0, :, 0:768]]
    even += [square_ref[1, :, 128:384], extra, square_ref[4, :, 0:128]]
    even += [wide_ref[0, :, 768:1024], wide_ref[2, :, 0:512]]
    odd = [square_ref[2], square_ref[3, :, 0:128], wide_ref[1, :, 0:768]]
    odd += [square_ref[3, :, 128:384], square_ref[4, :, 128:384]]
    odd += [wide_ref[1, :, 768:1024], wide_ref[2, :, 512:1024]]
    even = jnp.concatenate(even, axis=1)
    odd = jnp.concatenate(odd, axis=1)
    mine_ref[...] = jnp.where(core == 0, even, odd).astype(jnp.bfloat16)
    other_ref[...] = jnp.where(core == 0, odd, even).astype(jnp.bfloat16)


def spread_kernel(after_ref, rows_ref, out_ref):
    for number in range(8):
        out_ref[number] = rows_ref[...]


def spread_rows(after, rows):
    return call_kernel(
        spread_kernel,
        [in_any, in_vmem],
        [((8,) + rows.shape, jnp.bfloat16)],
        [],
        1000,
        8,
    )(after, rows)[0]


def prepare_kernel(begin, after_ref, plane_ref, *refs):
    spread_ref, stack_ref = refs[4:]
    lanes = slice(begin, begin + spread_ref.shape[3])
    for number in range(4):
        spread_ref[number] = plane_ref[:, :, lanes]
        stack_ref[number] = refs[number][:, lanes]


def prepare(begin, width, after, plane, blocks):
    shapes = ((4, 4, 48, width), (4, 48, width))
    return pl.pallas_call(
        functools.partial(prepare_kernel, begin),
        out_shape=[jax.ShapeDtypeStruct(shape, jnp.bfloat16) for shape in shapes],
        in_specs=[pl.BlockSpec(memory_space=pl.ANY)]
        + [pl.BlockSpec(memory_space=pltpu.VMEM)] * 5,
        out_specs=[pl.BlockSpec(memory_space=pltpu.VMEM)] * 2,
        compiler_params=pltpu.CompilerParams(vmem_limit_bytes=16 * 1024 * 1024),
        cost_estimate=pl.CostEstimate(flops=0, bytes_accessed=1000, transcendentals=0),
    )(after, plane, *blocks)


def assemble_kernel(after_ref, plain_ref, *refs):
    blocks, plain_out_ref, out_ref = refs[:4], refs[4], refs[5]
    place = lax.axis_index("dp")
    row, column = place // 16, lax.rem(place // 4, 4)
    plain_out_ref[...] = plain_ref[...]
    for number, step in enumerate(ring_steps):
        for inner, inner_step in enumerate(ring_steps):
            out_ref[lax.rem(row + inner_step, 4), lax.rem(column + step, 4)] = blocks[number][inner]


def assemble(after, plain, blocks):
    width = blocks[0].shape[2]
    shape = jax.ShapeDtypeStruct((4, 4, 48, width), jnp.bfloat16)
    plain, ring = pl.pallas_call(
        assemble_kernel,
        out_shape=[shape, shape],
        in_specs=[pl.BlockSpec(memory_space=pl.ANY)]
        + [pl.BlockSpec(memory_space=pltpu.VMEM)] * 5,
        out_specs=[pl.BlockSpec(memory_space=pltpu.VMEM)] * 2,
        compiler_params=pltpu.CompilerParams(vmem_limit_bytes=16 * 1024 * 1024),
        cost_estimate=pl.CostEstimate(flops=0, bytes_accessed=1000, transcendentals=0),
    )(after, plain.reshape(4, 4, 48, width), *blocks)
    return plain.reshape(768, width), ring.reshape(768, width)


def dot_nn(left, right):
    return jnp.dot(left, right, preferred_element_type=jnp.float32)


def dot_nt(left, right):
    return lax.dot_general(
        left, right, (((1,), (1,)), ((), ())), preferred_element_type=jnp.float32
    )


def dot_tn(left, right):
    return lax.dot_general(
        left, right, (((0,), (0,)), ((), ())), preferred_element_type=jnp.float32
    )


def three_parts(value):
    high = value.astype(jnp.bfloat16)
    rest = value - high.astype(jnp.float32)
    middle = rest.astype(jnp.bfloat16)
    low = (rest - middle.astype(jnp.float32)).astype(jnp.bfloat16)
    return high, middle, low


def exact_nn(ones, value):
    high, middle, low = three_parts(value)
    return dot_nn(ones, high) + dot_nn(ones, middle) + dot_nn(ones, low)


def gain_rows(ext):
    rows = lax.broadcasted_iota(jnp.int32, (16, 128), 0)
    columns = lax.broadcasted_iota(jnp.int32, (16, 128), 1)
    pick = (columns == rows + 6).astype(jnp.float32).astype(jnp.bfloat16)
    return dot_nt(pick, ext)


def head_mask(rows, head):
    lanes = lax.broadcasted_iota(jnp.int32, (rows, 128), 1)
    return (lanes // 64) == head


def lane_pick(array, lane):
    lanes = lax.broadcasted_iota(jnp.int32, array.shape, 1)
    return jnp.sum(jnp.where(lanes == lane, array, 0.0), axis=1, keepdims=True)


def pair_rms(raw, gain):
    first = head_mask(raw.shape[0], 0)
    square = raw * raw
    sum_first = jnp.sum(jnp.where(first, square, 0.0), axis=1, keepdims=True)
    sum_second = jnp.sum(jnp.where(first, 0.0, square), axis=1, keepdims=True)
    mean = jnp.where(first, sum_first, sum_second) * (1.0 / 64.0)
    scale = lax.rsqrt(mean + epsilon)
    return raw * scale * gain, scale


def block_scores(query, keys, decay_col, decay_row, allowed, inv_root):
    raw = dot_nt(query, keys) * inv_root + decay_col - decay_row
    return jnp.where(allowed, raw, -1e30)


def allowed_block(doc_col, doc_row, live_count, start, rows, columns):
    queries = start + lax.broadcasted_iota(jnp.int32, (rows, columns), 0)
    keys = lax.broadcasted_iota(jnp.int32, (rows, columns), 1)
    same = doc_col == doc_row
    return same & (keys <= queries) & ((keys < live_count) | (keys == queries))


def load_halves(refs, held, sems):
    core = lax.rem(lax.axis_index("dp"), 2)
    width = refs[0].shape[1]
    copies = []
    for number, ref in enumerate(refs):
        slot = core if number < 2 else 1 - core
        target = held.at[slot, :, pl.ds((number % 2) * width, width)]
        copies.append(pltpu.make_async_copy(ref, target, sems.at[number]))
    for copy in copies:
        copy.start()
    return core, copies


def attend_kernel(
    live_ref,
    tokens_ref,
    mine_plain_ref,
    mine_ring_ref,
    other_plain_ref,
    other_ring_ref,
    gains_ref,
    bias_ref,
    doc_col_ref,
    doc_row_ref,
    normed_ref,
    raw_out,
    heads_out,
    gated_mine_ref,
    gated_other_ref,
    part_ref,
    lanes_out,
    held,
    sems,
    raw_ref,
    heads_ref,
    lanes_ref,
):
    core, loads = load_halves(
        (mine_plain_ref, mine_ring_ref, other_plain_ref, other_ring_ref), held, sems
    )
    query_raw_ref, key_raw_ref, gate_ref, attended_ref = [raw_ref.at[n] for n in range(4)]
    query_ref, key_ref, value_ref = [heads_ref.at[n] for n in range(3)]
    logit_ref, decay_ref, total_ref = [lanes_ref.at[n] for n in range(3)]
    live_count = live_ref[0]
    inv_root = 0.125
    hidden = tokens_ref[...].astype(jnp.float32)
    scale = lax.rsqrt(jnp.mean(hidden * hidden, axis=1, keepdims=True) + epsilon)
    for copy in loads:
        copy.wait()
    ext = held[0, :, 768:896]
    gains = gain_rows(ext)
    normed = (hidden * scale * gains[0:1]).astype(jnp.bfloat16)
    normed_ref[...] = normed
    for block in range(3):
        lanes = slice(block * 128, block * 128 + 128)
        query_raw = dot_nn(normed, held[0, :, block * 128 : block * 128 + 128])
        key_raw = dot_nn(normed, held[0, :, 384 + block * 128 : 512 + block * 128])
        query_raw_ref[:, lanes] = query_raw
        key_raw_ref[:, lanes] = key_raw
        query_ref[:, lanes] = pair_rms(query_raw, gains_ref[0:1])[0].astype(jnp.bfloat16)
        key_ref[:, lanes] = pair_rms(key_raw, gains_ref[1:2])[0].astype(jnp.bfloat16)
    value_ref[...] = dot_nn(normed, held[1, :, 0:384]).astype(jnp.bfloat16)
    gate_ref[...] = dot_nn(normed, held[1, :, 384:768])
    lane = lax.broadcasted_iota(jnp.int32, (384, 128), 1)
    logit = dot_nn(normed, ext) + bias_ref[...]
    logit = jnp.where(lane < 6, logit, 0.0)
    logit_ref[...] = logit
    log_sig = jnp.minimum(logit, 0.0) - jnp.log1p(jnp.exp(-jnp.abs(logit)))
    rows = lax.broadcasted_iota(jnp.int32, (384, 384), 0)
    columns = lax.broadcasted_iota(jnp.int32, (384, 384), 1)
    lower = (columns <= rows).astype(jnp.float32).astype(jnp.bfloat16)
    decay = exact_nn(lower, log_sig)
    decay_ref[...] = decay
    decay_t = decay.T
    for step in range(3):
        begin, count = step * 128, step * 128 + 128
        allowed = allowed_block(
            doc_col_ref[begin : begin + 128, :],
            doc_row_ref[:, 0:count],
            live_count,
            begin,
            128,
            count,
        )
        totals = jnp.zeros((128, 128), jnp.float32)
        small_lane = lax.broadcasted_iota(jnp.int32, (128, 128), 1)
        for block in range(3):
            lanes = slice(block * 128, block * 128 + 128)
            keys = key_ref[0:count, lanes]
            values = value_ref[0:count, lanes]
            query_pair = query_ref[begin : begin + 128, lanes]
            outs = []
            for half in range(2):
                head = block * 2 + half
                query = jnp.where(head_mask(128, half), query_pair, jnp.zeros_like(query_pair))
                scores = block_scores(
                    query,
                    keys,
                    lane_pick(decay[begin : begin + 128], head),
                    decay_t[head : head + 1, 0:count],
                    allowed,
                    inv_root,
                )
                peak = jnp.max(scores, axis=1, keepdims=True)
                grown = jnp.exp(scores - peak)
                total = jnp.sum(grown, axis=1, keepdims=True)
                totals = jnp.where(small_lane == head, peak + jnp.log(total), totals)
                probs = (grown * (1.0 / total)).astype(jnp.bfloat16)
                outs.append(dot_nn(probs, values))
            attended_ref[begin : begin + 128, lanes] = jnp.where(
                head_mask(128, 0), outs[0], outs[1]
            )
        total_ref[begin : begin + 128, :] = totals
    copies = [
        pltpu.make_async_copy(
            source, target.at[pl.ds(0, source.shape[0])], sems.at[4 + number]
        )
        for number, (source, target) in enumerate(
            ((raw_ref, raw_out), (heads_ref, heads_out), (lanes_ref, lanes_out))
        )
    ]
    for copy in copies:
        copy.start()
    gated = (attended_ref[...] * jax.nn.sigmoid(gate_ref[...])).astype(jnp.bfloat16)
    gated_mine_ref[...] = jnp.where(core == 0, gated[:, 0:256], gated[:, 128:384])
    gated_other_ref[...] = jnp.where(core == 0, gated[:, 128:384], gated[:, 0:256])
    part = dot_nt(gated[:, 0:128], held[0, :, 896:1024]) + dot_nt(
        gated[:, 128:384], held[1, :, 768:1024]
    )
    part_ref[...] = part.astype(jnp.bfloat16)
    for copy in copies:
        copy.wait()


def mlp_kernel(
    live_ref,
    tokens_ref,
    part_ref,
    peer_ref,
    cotangent_ref,
    ext_ref,
    mine_plain_ref,
    mine_ring_ref,
    other_plain_ref,
    other_ring_ref,
    middle_ref,
    normed_ref,
    hidden_mine_ref,
    hidden_other_ref,
    out_ref,
    grad_ref,
    held,
    sems,
):
    core, loads = load_halves(
        (mine_plain_ref, mine_ring_ref, other_plain_ref, other_ring_ref), held, sems
    )
    middle = tokens_ref[...].astype(jnp.float32) + (
        part_ref[...].astype(jnp.float32) + peer_ref[...].astype(jnp.float32)
    )
    middle_ref[...] = middle
    gains = gain_rows(ext_ref[...])
    scale = lax.rsqrt(jnp.mean(middle * middle, axis=1, keepdims=True) + epsilon)
    normed = (middle * scale * gains[1:2]).astype(jnp.bfloat16)
    normed_ref[...] = normed
    live_rows = lax.broadcasted_iota(jnp.int32, (384, 1), 0) < live_ref[0]
    grad_out = jnp.where(live_rows, cotangent_ref[...].astype(jnp.float32), 0.0)
    grad_out = grad_out.astype(jnp.bfloat16)
    for copy in loads:
        copy.wait()
    out_total = jnp.zeros((384, 768), jnp.float32)
    grad_total = jnp.zeros((384, 768), jnp.float32)
    parts = []
    for half in range(2):
        begin = half * 512
        gate_w = held[0, :, begin : begin + 512]
        up_w = held[1, :, begin : begin + 512]
        down_w = held[half, :, 1024:1536]
        gate = dot_nn(normed, gate_w)
        up = dot_nn(normed, up_w)
        sig = jax.nn.sigmoid(gate)
        silu = gate * sig
        active = (silu * up).astype(jnp.bfloat16)
        out_total = out_total + dot_nt(active, down_w)
        grad_act = dot_nn(grad_out, down_w)
        grad_up = (grad_act * silu).astype(jnp.bfloat16)
        grad_gate = (grad_act * up * (sig * (1.0 + gate * (1.0 - sig)))).astype(jnp.bfloat16)
        parts.append((grad_gate, grad_up, active))
        grad_total = grad_total + dot_nt(grad_gate, gate_w) + dot_nt(grad_up, up_w)
    for number in range(3):
        lanes = slice(number * 512, number * 512 + 512)
        first, second = parts[0][number], parts[1][number]
        hidden_mine_ref[:, lanes] = jnp.where(core == 0, first, second)
        hidden_other_ref[:, lanes] = jnp.where(core == 0, second, first)
    out_ref[...] = out_total.astype(jnp.bfloat16)
    grad_ref[...] = grad_total.astype(jnp.bfloat16)


def attend_back_kernel(
    after_ref,
    live_ref,
    tokens_ref,
    cotangent_ref,
    middle_ref,
    part_ref,
    peer_ref,
    mine_plain_ref,
    mine_ring_ref,
    other_plain_ref,
    other_ring_ref,
    gains_ref,
    doc_col_ref,
    doc_row_ref,
    normed_ref,
    raw_in,
    heads_in,
    lanes_in,
    grad_middle_ref,
    grad_middle_b_ref,
    proj_mine_ref,
    proj_other_ref,
    norm_part_ref,
    extra_ref,
    held,
    sems,
    grad_att_ref,
    grad_query_ref,
    grad_key_ref,
    grad_value_ref,
    grad_og_ref,
    column_ref,
    raw_ref,
    heads_ref,
    lanes_ref,
    settle,
):
    core, loads = load_halves(
        (mine_plain_ref, mine_ring_ref, other_plain_ref, other_ring_ref), held, sems
    )
    settle()
    copies = [
        pltpu.make_async_copy(
            source.at[pl.ds(0, target.shape[0])], target, sems.at[4 + number]
        )
        for number, (source, target) in enumerate(
            ((raw_in, raw_ref), (heads_in, heads_ref), (lanes_in, lanes_ref))
        )
    ]
    for copy in copies:
        copy.start()
    query_raw_ref, key_raw_ref, gate_ref, attended_ref = [raw_ref.at[n] for n in range(4)]
    query_ref, key_ref, value_ref = [heads_ref.at[n] for n in range(3)]
    logit_ref, decay_ref, total_ref = [lanes_ref.at[n] for n in range(3)]
    live_count = live_ref[0]
    inv_root = 0.125
    middle = middle_ref[...]
    grad_normed = part_ref[...].astype(jnp.float32)
    grad_normed = grad_normed + peer_ref[...].astype(jnp.float32)
    live_rows = lax.broadcasted_iota(jnp.int32, (384, 1), 0) < live_count
    grad_out = jnp.where(live_rows, cotangent_ref[...].astype(jnp.float32), 0.0)
    scale = lax.rsqrt(jnp.mean(middle * middle, axis=1, keepdims=True) + epsilon)
    for copy in loads:
        copy.wait()
    ext = held[0, :, 768:896]
    gains = gain_rows(ext)
    gained = grad_normed * gains[1:2]
    inner = jnp.mean(gained * middle, axis=1, keepdims=True)
    grad_middle = grad_out + (scale * gained - middle * (scale * scale * scale * inner))
    grad_gain = jnp.sum(grad_normed * middle * scale, axis=0, keepdims=True)
    grad_middle_ref[...] = grad_middle
    grad_middle_b = grad_middle.astype(jnp.bfloat16)
    grad_middle_b_ref[...] = grad_middle_b
    grad_gated = jnp.concatenate(
        [
            dot_nn(grad_middle_b, held[0, :, 896:1024]),
            dot_nn(grad_middle_b, held[1, :, 768:1024]),
        ],
        axis=1,
    )
    for copy in copies:
        copy.wait()
    sig = jax.nn.sigmoid(gate_ref[...])
    grad_att_ref[...] = (grad_gated * sig).astype(jnp.bfloat16)
    grad_og = (grad_gated * attended_ref[...] * sig * (1.0 - sig)).astype(jnp.bfloat16)
    grad_og_ref[...] = grad_og
    grad_key_ref[...] = jnp.zeros((384, 384), jnp.float32)
    grad_value_ref[...] = jnp.zeros((384, 384), jnp.float32)
    column_ref[...] = jnp.zeros((128, 384), jnp.float32)
    decay = decay_ref[...]
    decay_t = decay.T
    row_parts = []
    for step in range(3):
        begin, count = step * 128, step * 128 + 128
        allowed = allowed_block(
            doc_col_ref[begin : begin + 128, :],
            doc_row_ref[:, 0:count],
            live_count,
            begin,
            128,
            count,
        )
        small_lane = lax.broadcasted_iota(jnp.int32, (128, 128), 1)
        row_sums = jnp.zeros((128, 128), jnp.float32)
        for block in range(3):
            lanes = slice(block * 128, block * 128 + 128)
            keys = key_ref[0:count, lanes]
            values = value_ref[0:count, lanes]
            query_pair = query_ref[begin : begin + 128, lanes]
            att_pair = grad_att_ref[begin : begin + 128, lanes]
            outs = []
            key_outs = []
            value_outs = []
            for half in range(2):
                head = block * 2 + half
                mask = head_mask(128, half)
                query = jnp.where(mask, query_pair, jnp.zeros_like(query_pair))
                att = jnp.where(mask, att_pair, jnp.zeros_like(att_pair))
                scores = block_scores(
                    query,
                    keys,
                    lane_pick(decay[begin : begin + 128], head),
                    decay_t[head : head + 1, 0:count],
                    allowed,
                    inv_root,
                )
                probs = jnp.exp(scores - lane_pick(total_ref[begin : begin + 128, :], head))
                grad_probs = dot_nt(att, values)
                row_dot = jnp.sum(probs * grad_probs, axis=1, keepdims=True)
                grad_scores = (probs * (grad_probs - row_dot)).astype(jnp.bfloat16)
                grad_scores_f = grad_scores.astype(jnp.float32)
                row_sums = jnp.where(
                    small_lane == head,
                    jnp.sum(grad_scores_f, axis=1, keepdims=True),
                    row_sums,
                )
                column_ref[head : head + 1, 0:count] += jnp.sum(
                    grad_scores_f, axis=0, keepdims=True
                )
                outs.append(dot_nn(grad_scores, keys))
                key_outs.append(dot_tn(grad_scores, query))
                value_outs.append(dot_tn(probs.astype(jnp.bfloat16), att))
            grad_query_ref[begin : begin + 128, lanes] = jnp.where(
                head_mask(128, 0), outs[0], outs[1]
            )
            grad_key_ref[0:count, lanes] += key_outs[0] + key_outs[1]
            grad_value_ref[0:count, lanes] += value_outs[0] + value_outs[1]
        row_parts.append(row_sums)
    grad_decay = jnp.concatenate(row_parts, axis=0) - column_ref[...].T
    rows = lax.broadcasted_iota(jnp.int32, (384, 384), 0)
    columns = lax.broadcasted_iota(jnp.int32, (384, 384), 1)
    upper = (columns >= rows).astype(jnp.float32).astype(jnp.bfloat16)
    grad_logit = exact_nn(upper, grad_decay) * jax.nn.sigmoid(-logit_ref[...])
    lane = lax.broadcasted_iota(jnp.int32, (384, 128), 1)
    grad_logit = jnp.where(lane < 6, grad_logit, 0.0)
    grad_forget = grad_logit.astype(jnp.bfloat16)
    grad_vg = jnp.concatenate([grad_value_ref[...].astype(jnp.bfloat16), grad_og_ref[...]], axis=1)
    grad_qk = []
    gain_sums = []
    for number, raw_ref, out_ref in (
        (0, query_raw_ref, grad_query_ref),
        (1, key_raw_ref, grad_key_ref),
    ):
        gain = gains_ref[number : number + 1]
        gain_sum = jnp.zeros((1, 128), jnp.float32)
        for block in range(3):
            lanes = slice(block * 128, block * 128 + 128)
            raw = raw_ref[:, lanes]
            grad = (out_ref[:, lanes] * inv_root).astype(jnp.bfloat16).astype(jnp.float32)
            first = head_mask(384, 0)
            scaled = pair_rms(raw, 1.0)[1]
            weighted = grad * gain
            product = weighted * raw
            sum_first = jnp.sum(jnp.where(first, product, 0.0), axis=1, keepdims=True)
            sum_second = jnp.sum(jnp.where(first, 0.0, product), axis=1, keepdims=True)
            inner_head = jnp.where(first, sum_first, sum_second) * (1.0 / 64.0)
            gain_sum = gain_sum + jnp.sum(grad * raw * scaled, axis=0, keepdims=True)
            grad_raw = scaled * weighted - raw * (scaled * scaled * scaled * inner_head)
            grad_qk.append(grad_raw.astype(jnp.bfloat16))
        gain_sums.append(gain_sum)
    grad_qk = jnp.concatenate(grad_qk, axis=1)
    proj_mine_ref[...] = jnp.where(core == 0, grad_qk, grad_vg)
    proj_other_ref[...] = jnp.where(core == 0, grad_vg, grad_qk)
    part = dot_nt(grad_qk, held[0, :, 0:768])
    part = part + dot_nt(grad_vg, held[1, :, 0:768])
    part = part + dot_nt(grad_forget, ext)
    norm_part_ref[...] = part.astype(jnp.bfloat16)
    hidden = tokens_ref[...].astype(jnp.float32)
    scale = lax.rsqrt(jnp.mean(hidden * hidden, axis=1, keepdims=True) + epsilon)
    first_gain = jnp.sum(part * (hidden * scale), axis=0, keepdims=True)
    line = lax.broadcasted_iota(jnp.int32, (128, 768), 0)
    extra = jnp.where(line == 6, first_gain, jnp.where(line == 7, grad_gain, 0.0)).T
    extra = extra + dot_tn(normed_ref[...], grad_forget)
    bias_sum = jnp.sum(grad_forget.astype(jnp.float32), axis=0, keepdims=True)
    sums = [total + pltpu.roll(total, 64, 1) for total in (gain_sums[0], gain_sums[1], bias_sum)]
    line = lax.rem(lax.broadcasted_iota(jnp.int32, (768, 128), 0), 12)
    lane = lax.broadcasted_iota(jnp.int32, (768, 128), 1)
    for number in range(3):
        extra = jnp.where((line == number) & (lane >= 64), sums[number], extra)
    extra_ref[...] = extra.astype(jnp.bfloat16)


def wide_grad_kernel(*refs):
    normed, normed_peer, hidden, hidden_peer, grad, grad_peer, out_ref = refs
    for begin in range(0, 1536, 256):
        lanes = slice(begin, begin + 256)
        left, left_peer = (normed, normed_peer) if begin < 1024 else (grad, grad_peer)
        total = dot_tn(left[...], hidden[:, lanes]) + dot_tn(left_peer[...], hidden_peer[:, lanes])
        out_ref[:, lanes] = total.astype(jnp.bfloat16)


def proj_grad_kernel(after_ref, *refs):
    first, first_peer, left, left_peer, second, second_peer, right, right_peer = refs[:8]
    extra_ref, out_ref = refs[8], refs[9]
    out_ref[:, 1024:1152] = extra_ref[...]
    for begin in range(0, 1024, 256):
        if begin < 768:
            lanes = slice(begin, begin + 256)
            total = dot_tn(first[...], left[:, lanes])
            total = total + dot_tn(first_peer[...], left_peer[:, lanes])
        else:
            total = dot_tn(second[...], right[...]) + dot_tn(second_peer[...], right_peer[...])
        out_ref[:, begin : begin + 256] = total.astype(jnp.bfloat16)


def mirror(out_ref, block, start):
    out_ref[start : start + 256, start:768] = block.astype(jnp.bfloat16)
    for other in range(start + 256, 768, 256):
        piece = block[:, other - start : other - start + 256]
        out_ref[other : other + 256, start : start + 256] = piece.T.astype(jnp.bfloat16)


def plane_sum_kernel(*refs):
    blocks_ref, mine_ref, other_ref = refs[-3:]
    level = lax.rem(lax.axis_index("dp") // 2, 2)
    for start in range(0, blocks_ref.shape[2], 256):
        lanes = slice(start, start + 256)
        total = blocks_ref[0, :, lanes].astype(jnp.float32)
        for number in range(1, 16):
            total = total + blocks_ref[number, :, lanes].astype(jnp.float32)
        first, second = total[0:24], total[24:48]
        mine_ref[:, lanes] = jnp.where(level == 0, first, second)
        other_ref[:, lanes] = jnp.where(level == 0, second, first)


def momentum_kernel(
    mine_ref,
    other_ref,
    old_ref,
    tokens_ref,
    grad_middle_ref,
    norm_part_ref,
    norm_peer_ref,
    ext_ref,
    middle_ref,
    mlp_part_ref,
    mlp_peer_ref,
    new_ref,
    keep_ref,
    send_ref,
    small_ref,
    input_grad_ref,
    result_ref,
):
    place = lax.axis_index("dp")
    core, level = lax.rem(place, 2), lax.rem(place // 2, 2)
    mine, other = mine_ref[...], other_ref[...]
    even = jnp.where(core == 0, mine, other)
    odd = jnp.where(core == 0, other, mine)
    small_ref[...] = mine[:, 1024:1152] + other[:, 1024:1152]
    fresh = [even[:, 0:384], even[:, 384:768], odd[:, 0:384], odd[:, 384:768]]
    fresh.append(jnp.concatenate([even[:, 768:1024], odd[:, 896:1024]], axis=1))
    fresh = [muon_decay * old_ref[number] + fresh[number] for number in range(5)]
    for number in range(5):
        new_ref[number] = fresh[number]
    for number in range(4):
        keep_ref[number] = jnp.where(level == 0, fresh[4], fresh[number])
        send_ref[number] = jnp.where(level == 0, fresh[number], fresh[4])
    hidden = tokens_ref[...].astype(jnp.float32)
    gain = gain_rows(ext_ref[...])[0:1]
    added = mlp_part_ref[...].astype(jnp.float32) + mlp_peer_ref[...].astype(jnp.float32)
    result_ref[...] = (middle_ref[...] + added).astype(jnp.bfloat16)
    grad = norm_part_ref[...].astype(jnp.float32) + norm_peer_ref[...].astype(jnp.float32)
    scale = lax.rsqrt(jnp.mean(hidden * hidden, axis=1, keepdims=True) + epsilon)
    gained = grad * gain
    inner = jnp.mean(gained * hidden, axis=1, keepdims=True)
    input_grad_ref[...] = grad_middle_ref[...] + (
        scale * gained - hidden * (scale * scale * scale * inner)
    )


def small_kernel(
    mine_ref,
    peer_ref,
    norm_ref,
    qk_ref,
    forget_ref,
    bias_ref,
    m_norm_ref,
    m_qk_ref,
    m_forget_ref,
    m_bias_ref,
    after_ref,
    new_norm_ref,
    new_qk_ref,
    new_forget_ref,
    new_bias_ref,
    mom_norm_ref,
    mom_qk_ref,
    mom_forget_ref,
    mom_bias_ref,
):
    root_tokens = math.sqrt(24576.0)
    mine, both = mine_ref[...], mine_ref[...] + peer_ref[...]
    lane = lax.broadcasted_iota(jnp.int32, (12, 128), 1)
    norms = jnp.where(lane == 6, both, mine).T
    grads = (
        (norms[6:8, :], gain_rate, norm_ref, m_norm_ref, new_norm_ref, mom_norm_ref),
        (both[0:2, 64:128], qk_rate, qk_ref, m_qk_ref, new_qk_ref, mom_qk_ref),
        (mine[:, 0:6], forget_rate, forget_ref, m_forget_ref, new_forget_ref, mom_forget_ref),
        (mine[2:3, 64:70], bias_rate, bias_ref, m_bias_ref, new_bias_ref, mom_bias_ref),
    )
    for grad, rate, value_ref, old_ref, new_ref, mom_ref in grads:
        moment = plain_decay * old_ref[...] + grad
        mom_ref[...] = moment
        new_ref[...] = value_ref[...] - (rate / root_tokens) * moment


def newton_body(sources, out_ref, held, square_ref, poly_ref):
    total = jnp.zeros((1, 1), jnp.float32)
    for source in sources:
        for number in range(8):
            for start in (0, 48):
                piece = source[number, start : start + 48, :].astype(jnp.float32)
                piece = jnp.sum(piece * piece, axis=0, keepdims=True)
                total = total + jnp.sum(piece, axis=1, keepdims=True)
    scale = 1.0 / (jnp.sqrt(total) + 1e-07)
    for place, source in zip((0, 384), sources):
        for number in range(8):
            for start in (0, 48):
                piece = source[number, start : start + 48, :].astype(jnp.float32) * scale
                begin = place + (number % 4) * 96 + start
                held[0, number // 4, begin : begin + 48, :] = piece.astype(jnp.bfloat16)
    for repeat in range(5):
        now, later = repeat % 2, (repeat + 1) % 2
        for start in range(0, 768, 256):
            rows, right = slice(start, start + 256), slice(start, 768)
            square = dot_nt(held[now, 0, rows, :], held[now, 0, right, :])
            square = square + dot_nt(held[now, 1, rows, :], held[now, 1, right, :])
            mirror(square_ref, square, start)
        if repeat < 4:
            for start in range(0, 768, 256):
                rows, right = slice(start, start + 256), slice(start, 768)
                poly = coef_b * square_ref[rows, right].astype(jnp.float32)
                poly = poly + coef_c * dot_nn(square_ref[rows, :], square_ref[:, right])
                mirror(poly_ref, poly, start)
            for side in range(2):
                for start in range(0, 768, 256):
                    grown = coef_a * held[now, side, start : start + 256, :].astype(jnp.float32)
                    grown = grown + dot_nn(poly_ref[start : start + 256, :], held[now, side])
                    held[later, side, start : start + 256, :] = grown.astype(jnp.bfloat16)
        else:
            side = lax.axis_index("tensor")
            begin = pl.multiple_of((lax.axis_index("dp") // 16) * 96, 16)
            few = square_ref[pl.ds(begin, 96), :]
            poly = coef_b * few.astype(jnp.float32) + coef_c * dot_nn(few, square_ref[...])
            poly = poly.astype(jnp.bfloat16)
            grown = coef_a * held[now, side, pl.ds(begin, 96), :].astype(jnp.float32)
            grown = grown + dot_nn(poly, held[now, side])
            out_ref[...] = grown.astype(jnp.bfloat16)


def newton_kernel(wants_wide, after_ref, mine_ref, other_ref, out_ref, *scratch):
    place = lax.axis_index("dp")
    is_wide = (lax.rem(place // 2, 2) == 0) & (lax.rem(place // 4, 4) < 3)
    active = is_wide if wants_wide else jnp.logical_not(is_wide)

    @pl.when(active)
    def run():
        newton_body((mine_ref, other_ref), out_ref, *scratch)

    @pl.when(jnp.logical_not(active))
    def skip():
        out_ref[...] = jnp.zeros(out_ref.shape, jnp.bfloat16)


in_vmem = pl.BlockSpec(memory_space=pltpu.VMEM)
in_smem = pl.BlockSpec(memory_space=pltpu.SMEM)
in_any = pl.BlockSpec(memory_space=pl.ANY)
in_hbm = pl.BlockSpec(memory_space=pltpu.HBM)


def call_kernel(kernel, in_specs, outs, scratch, flops, limit=24, far=(), staged=False):
    near = [number for number in range(len(outs)) if number not in far]
    moved = [number for number, spec in enumerate(in_specs) if spec is in_vmem]
    count = len(in_specs) + len(outs) + len(scratch)

    def staged_kernel(*refs):
        refs, buffers = list(refs[:count]), refs[count:]
        sems = buffers[-1]
        loads = []
        for slot, number in enumerate(moved):
            loads.append(pltpu.make_async_copy(refs[number], buffers[slot], sems.at[slot]))
            refs[number] = buffers[slot]
        for copy in loads:
            copy.start()
        stores = []
        for slot, number in enumerate(near):
            place, slot = len(in_specs) + number, len(moved) + slot
            stores.append(pltpu.make_async_copy(buffers[slot], refs[place], sems.at[slot]))
            refs[place] = buffers[slot]

        def settle():
            for copy in loads:
                copy.wait()

        kernel(*refs, settle=settle)
        for copy in stores:
            copy.start()
        for copy in stores:
            copy.wait()

    def run(*operands):
        buffers = []
        if staged:
            buffers = [pltpu.VMEM(operands[n].shape, operands[n].dtype) for n in moved]
            buffers += [pltpu.VMEM(*outs[n]) for n in near]
            buffers.append(pltpu.SemaphoreType.DMA((len(buffers),)))
        out_specs = [in_hbm if staged or n in far else in_vmem for n in range(len(outs))]
        return pl.pallas_call(
            staged_kernel if staged else kernel,
            out_shape=[jax.ShapeDtypeStruct(shape, dtype) for shape, dtype in outs],
            in_specs=[in_any if staged and spec is in_vmem else spec for spec in in_specs],
            out_specs=out_specs,
            scratch_shapes=list(scratch) + buffers,
            compiler_params=pltpu.CompilerParams(vmem_limit_bytes=limit * 1024 * 1024),
            cost_estimate=pl.CostEstimate(flops=flops, bytes_accessed=1000, transcendentals=0),
        )(*operands)

    return run


def newton(wants_wide, after, mine, other):
    columns = mine.shape[2]
    return call_kernel(
        functools.partial(newton_kernel, wants_wide),
        [in_any] + [in_vmem] * 2,
        [((96, columns), jnp.bfloat16)],
        [
            pltpu.VMEM((2, 2, 768, columns), jnp.bfloat16),
            pltpu.VMEM((768, 768), jnp.bfloat16),
            pltpu.VMEM((768, 768), jnp.bfloat16),
        ],
        200000000000 if wants_wide else 1000,
    )(after, mine, other)[0]


def spread_slots(slots_b):
    column = place_of("x")

    def slot(step):
        number = jnp.minimum((column + step) % 4, slots_b.shape[0] - 1)
        return lax.dynamic_index_in_dim(slots_b, number, 0, keepdims=False)

    pieces = [slot(0)] + [fetch(slot(4 - step), "x", step) for step in (1, 2, 3)]
    return jnp.concatenate(pieces, axis=0)


def ring_order(rows, count):
    column = place_of("x")
    blocks = rows.reshape(4, 24, count)
    return jnp.stack(
        [lax.dynamic_index_in_dim(blocks, (n - column) % 4, 0, False) for n in range(4)]
    )


def on_device(
    tokens,
    cotangent,
    segment_ids,
    live_len,
    w_square,
    w_wide,
    norm_gain,
    qk_gain,
    forget_w,
    forget_b,
    m_square,
    m_wide,
    m_norm,
    m_qk,
    m_forget_w,
    m_forget_b,
    ema_square,
    ema_wide,
):
    half_width = w_square.shape[2]
    half_hidden = w_wide.shape[2]
    shard_rows = w_square.shape[1]
    head_local = forget_w.shape[1]
    head_dim = qk_gain.shape[1]
    dp_size = lax.axis_size("dp")
    full_width = shard_rows * dp_size
    full_hidden = half_hidden * lax.axis_size("tensor")
    my_place = lax.axis_index("dp")
    core = my_place % 2
    quarter_hidden = half_hidden // 2
    bf16, f32 = jnp.bfloat16, jnp.float32

    pack_mine, pack_other = call_kernel(
        pack_kernel, [in_vmem] * 4, [((shard_rows, 2560), bf16)] * 2, [], 1000, 8
    )(w_square, w_wide, norm_gain, forget_w)
    pair_rows = pair_join(core, pack_mine, core_swap(pack_other), 0)
    ring_rows = pair_rows[:, 1280:]
    ring_rows = pair_join(place_of("l"), ring_rows, fetch(ring_rows, "l", 1), 0)
    row_plane = exchange(spread_rows(ring_rows, pair_rows[:, :1280]), ("x", "l"))
    row_plane = row_plane.reshape(4, 48, 1280)
    blocks_y = fetch_ring(ring_rows, "y")

    def both_cores(after, plain, blocks):
        plain, ring = assemble(after, plain, blocks)
        return plain, ring, core_swap(plain), core_swap(ring)

    spread, stack = prepare(0, 512, pair_rows, row_plane, blocks_y)
    first_plane, first_blocks = exchange(spread, ("y",)), fetch_ring(stack, "x")
    first_weights = both_cores(pair_rows, first_plane, first_blocks)
    spread, stack = prepare(512, 768, first_weights[1], row_plane, blocks_y)
    late_plane, late_blocks = exchange(spread, ("y",)), fetch_ring(stack, "x")
    ext = by_core(core, first_weights[1][:, 256:384], first_weights[3][:, 256:384])

    gains_b = qk_gain.astype(bf16).astype(f32)
    gains = jnp.concatenate([gains_b, gains_b], axis=1)
    bias_row = jnp.pad(forget_b.astype(bf16).astype(f32), (0, 128 - head_local))[None]
    doc_row = segment_ids
    doc_col = segment_ids.reshape(-1, 1)
    live_mask = (jnp.arange(tokens.shape[0]) < live_len[0])[:, None]
    grad_out_b = jnp.where(live_mask, cotangent, jnp.zeros_like(cotangent))

    def paired(mine, other):
        return mine, core_swap(other)

    token_h = ((384, 768), bf16)
    token_f = ((384, 768), f32)
    (
        normed_one,
        raw,
        heads,
        gated_mine,
        gated_other,
        attn_part,
        head_lanes,
    ) = call_kernel(
        attend_kernel,
        [in_smem, in_vmem] + [in_any] * 4 + [in_vmem] * 4,
        [token_h, ((48, 384, 384), f32), ((100, 384, 384), bf16)]
        + [((384, 256), bf16)] * 2
        + [token_h, ((150, 384, 128), f32)],
        [
            pltpu.VMEM((2, 768, 1024), bf16),
            pltpu.SemaphoreType.DMA((7,)),
            pltpu.VMEM((4, 384, 384), f32),
            pltpu.VMEM((3, 384, 384), bf16),
            pltpu.VMEM((3, 384, 128), f32),
        ],
        1000,
        24,
        (1, 2, 6),
    )(live_len, tokens, *first_weights, gains, bias_row, doc_col, doc_row)
    second_weights = both_cores(core_swap(attn_part[:16, :128]), late_plane, late_blocks)
    normed_one_pair = paired(normed_one, normed_one)
    gated_pair = paired(gated_mine, gated_other)
    grad_out_pair = paired(grad_out_b, grad_out_b)
    middle, normed_two, hidden_mine, hidden_other, mlp_part, grad_part = call_kernel(
        mlp_kernel,
        [in_smem] + [in_vmem] * 5 + [in_any] * 4,
        [token_f, token_h, ((384, 1536), bf16), ((384, 1536), bf16), token_h, token_h],
        [pltpu.VMEM((2, 768, 1536), bf16), pltpu.SemaphoreType.DMA((4,))],
        1000,
        24,
    )(live_len, tokens, attn_part, tensor_swap(attn_part), cotangent, ext, *second_weights)
    grad_peer = tensor_swap(grad_part)

    normed_two_pair = paired(normed_two, normed_two)
    hidden_pair = paired(hidden_mine, hidden_other)
    grad_wide_b = call_kernel(
        wide_grad_kernel,
        [in_vmem] * 6,
        [((768, 1536), bf16)],
        [],
        1000,
        24,
    )(*normed_two_pair, *hidden_pair, *grad_out_pair)[0]
    level = place_of("l")
    wide_blocks = exchange(grad_wide_b.reshape(16, 48, 3 * quarter_hidden), ("y", "x"))

    (
        grad_middle,
        grad_middle_b,
        proj_mine,
        proj_other,
        norm_part,
        extra,
    ) = call_kernel(
        attend_back_kernel,
        [in_any, in_smem] + [in_vmem] * 5 + [in_any] * 4 + [in_vmem] * 4 + [in_hbm] * 3,
        [token_f, token_h, token_h, token_h, token_h, ((768, 128), bf16)],
        [
            pltpu.VMEM((2, 768, 1024), bf16),
            pltpu.SemaphoreType.DMA((7,)),
            pltpu.VMEM((384, 384), bf16),
            pltpu.VMEM((384, 384), f32),
            pltpu.VMEM((384, 384), f32),
            pltpu.VMEM((384, 384), f32),
            pltpu.VMEM((384, 384), bf16),
            pltpu.VMEM((128, 384), f32),
            pltpu.VMEM((4, 384, 384), f32),
            pltpu.VMEM((3, 384, 384), bf16),
            pltpu.VMEM((3, 384, 128), f32),
        ],
        100000000000,
        56,
        staged=True,
    )(
        grad_wide_b,
        live_len,
        tokens,
        cotangent,
        middle,
        grad_part,
        grad_peer,
        *first_weights,
        gains,
        doc_col,
        doc_row,
        normed_one,
        raw,
        heads,
        head_lanes,
    )
    proj_pair = paired(proj_mine, proj_other)
    grad_middle_pair = paired(grad_middle_b, grad_middle_b)
    mlp_peer = tensor_swap(mlp_part)
    grad_proj_b = call_kernel(
        proj_grad_kernel,
        [in_any] + [in_vmem] * 9,
        [((768, 1152), bf16)],
        [],
        1000,
        24,
    )(
        mlp_peer,
        *normed_one_pair,
        *proj_pair,
        *grad_middle_pair,
        *gated_pair,
        extra,
    )[0]
    norm_peer = tensor_swap(norm_part)
    mine, other = call_kernel(
        plane_sum_kernel,
        [in_any] * 2 + [in_vmem],
        [((24, 3 * quarter_hidden), f32)] * 2,
        [],
        1000,
    )(grad_proj_b, norm_peer, wide_blocks)
    other = other.astype(bf16)
    mine, other = pair_split(core, mine + fetch(other, "l", 1).astype(f32), 0)
    other = core_swap(other)
    wide_shard = jnp.stack(
        [
            pair_join(core, mine[:, start : start + 512], other[:, start : start + 512], 1)
            for start in (0, 512, 1024)
        ]
    )
    mom_wide = muon_decay * m_wide + wide_shard

    wide_slots = mom_wide.astype(bf16)
    wide_pair = jnp.concatenate([wide_slots, fetch(wide_slots, "l", 1)], axis=1)
    wide_rows = spread_slots(wide_pair)
    proj_blocks = exchange(grad_proj_b.reshape(32, 24, 1152), ("y", "x", "l"))
    proj_blocks, wide_rows = lax.optimization_barrier((proj_blocks, wide_rows))
    wide_own = gather(wide_rows, ("t", "y"))
    mine, other = pair_split(core, jnp.sum(proj_blocks.astype(f32), axis=0), 0)
    other = core_swap(other)
    mom_square, keep_slots, send_slots, small, input_grad, result = call_kernel(
        momentum_kernel,
        [in_vmem] * 11,
        [
            ((5, 12, half_width), f32),
            ((4, 12, half_width), f32),
            ((4, 12, half_width), f32),
            ((12, 128), f32),
            token_f,
            token_h,
        ],
        [],
        1000,
        24,
    )(
        mine,
        other,
        m_square,
        tokens,
        grad_middle,
        norm_part,
        norm_peer,
        ext,
        middle,
        mlp_part,
        mlp_peer,
    )
    keep_slots, send_slots = keep_slots.astype(bf16), send_slots.astype(bf16)
    proj_rows = spread_slots(pair_join(level, keep_slots, fetch(send_slots, "l", 1), 1))
    wide_own, proj_rows = lax.optimization_barrier((wide_own, proj_rows))
    wide_other = core_swap(wide_own)
    proj_own = gather(proj_rows, ("t", "y"))
    wide_rows = newton(True, small, wide_own, wide_other)
    proj_own, wide_rows = lax.optimization_barrier((proj_own, wide_rows))
    proj_rows = newton(False, wide_rows, proj_own, core_swap(proj_own))
    proj_rows = jnp.pad(proj_rows, ((0, 0), (0, half_hidden - half_width)))
    rows = ring_order(proj_rows + wide_rows, half_hidden).reshape(8, 12, half_hidden)
    update = exchange(rows, ("x", "l")).astype(f32)
    update_wide = update[0:6:2]
    update_square = jnp.concatenate([update[1::2], update[6:7]], axis=0)[:, :, :half_width]

    small_peer = tensor_swap(small)
    (
        new_norm,
        new_qk,
        new_forget_w,
        new_forget_b,
        mom_norm,
        mom_qk,
        mom_forget_w,
        mom_forget_b,
    ) = call_kernel(
        small_kernel,
        [in_vmem] * 10 + [in_any],
        [(value.shape, f32) for value in (norm_gain, qk_gain, forget_w)]
        + [((1, head_local), f32)]
        + [(value.shape, f32) for value in (norm_gain, qk_gain, forget_w)]
        + [((1, head_local), f32)],
        [],
        1000,
        16,
    )(
        small,
        small_peer,
        norm_gain,
        qk_gain,
        forget_w,
        forget_b[None],
        m_norm,
        m_qk,
        m_forget_w,
        m_forget_b[None],
        proj_rows,
    )
    new_forget_b, mom_forget_b = new_forget_b[0], mom_forget_b[0]
    new_square = w_square - update_square
    new_wide = w_wide - math.sqrt(full_hidden / full_width) * update_wide
    new_ema_square = ema_decay * ema_square + (1.0 - ema_decay) * new_square
    new_ema_wide = ema_decay * ema_wide + (1.0 - ema_decay) * new_wide
    return (
        result,
        input_grad,
        new_square,
        new_wide,
        new_norm,
        new_qk,
        new_forget_w,
        new_forget_b,
        mom_square,
        mom_wide,
        mom_norm,
        mom_qk,
        mom_forget_w,
        mom_forget_b,
        new_ema_square,
        new_ema_wide,
    )


def solution(mesh):
    placed = (
        P("dp", None),
        P("dp", None),
        P("dp", None),
        P("dp"),
        P(None, "dp", "tensor"),
        P(None, "dp", "tensor"),
        P(None, "dp"),
        P(),
        P("dp", "tensor"),
        P("tensor"),
        P(None, "dp", "tensor"),
        P(None, "dp", "tensor"),
        P(None, "dp"),
        P(),
        P("dp", "tensor"),
        P("tensor"),
        P(None, "dp", "tensor"),
        P(None, "dp", "tensor"),
    )
    return jax.shard_map(
        on_device,
        mesh=mesh,
        in_specs=placed,
        out_specs=(
            P("dp", None),
            P("dp", None),
            P(None, "dp", "tensor"),
            P(None, "dp", "tensor"),
            P(None, "dp"),
            P(),
            P("dp", "tensor"),
            P("tensor"),
            P(None, "dp", "tensor"),
            P(None, "dp", "tensor"),
            P(None, "dp"),
            P(),
            P("dp", "tensor"),
            P("tensor"),
            P(None, "dp", "tensor"),
            P(None, "dp", "tensor"),
        ),
        check_vma=False,
    )
```

```python
import functools
import math

import jax
import jax.numpy as jnp
from jax import lax
import numpy as np
from jax.experimental import pallas as pl
from jax.experimental.pallas import tpu as pltpu
from jax.sharding import PartitionSpec as P

epsilon = 1e-06
coef_a = 3.4445
coef_b = -4.775
coef_c = 2.0315
muon_decay = 0.95
plain_decay = 0.9
ema_decay = 0.7
gain_rate = 0.2
qk_rate = 0.05
forget_rate = 0.1
bias_rate = 0.5


grid_sizes = {"y": 4, "x": 4, "l": 2, "c": 2, "t": 2}
dp_names = ["y", "x", "l", "c"]


def ring_groups(names, over):
    order = [name for name in over if name not in names]
    table = np.arange(math.prod(grid_sizes[name] for name in over))
    table = table.reshape([grid_sizes[name] for name in over])
    table = table.transpose([over.index(name) for name in order + list(names)])
    return table.reshape(-1, math.prod(grid_sizes[name] for name in names)).tolist()


def exchange(blocks, names):
    axes = ("dp", "tensor") if "t" in names else "dp"
    return lax.all_to_all(
        blocks,
        axes,
        split_axis=0,
        concat_axis=0,
        tiled=True,
        axis_index_groups=ring_groups(names, dp_names + (["t"] if "t" in names else [])),
    )


def gather(block, names):
    count = math.prod(grid_sizes[name] for name in names)
    return exchange(jnp.broadcast_to(block[None], (count,) + block.shape), names)


def place_of(name):
    place = lax.axis_index("dp")
    return {"y": place // 16, "x": (place // 4) % 4, "l": (place // 2) % 2, "c": place % 2}[name]


def fetch(array, name, step):
    table = np.arange(64).reshape(4, 4, 2, 2)
    sources = np.roll(table, -step, axis=dp_names.index(name))
    pairs = [(int(a), int(b)) for a, b in zip(sources.ravel(), table.ravel())]
    return lax.ppermute(array, "dp", pairs)


def fetch_ring(array, name):
    return [array] + [fetch(array, name, step) for step in (1, 3, 2)]


ring_steps = (0, 1, 3, 2)


def core_swap(array):
    return fetch(array, "c", 1)


def tensor_swap(array):
    return lax.ppermute(array, "tensor", [(0, 1), (1, 0)])


def by_core(core, even, odd):
    return jnp.where(core == 0, even, odd)


def pair_join(place, mine, other, axis):
    return jnp.where(
        place == 0,
        jnp.concatenate([mine, other], axis=axis),
        jnp.concatenate([other, mine], axis=axis),
    )


def pair_split(core, array, axis):
    first, second = jnp.split(array, 2, axis=axis)
    return by_core(core, first, second), by_core(core, second, first)


def pack_kernel(square_ref, wide_ref, norm_ref, forget_ref, mine_ref, other_ref):
    core = lax.rem(lax.axis_index("dp"), 2)
    eye = lax.broadcasted_iota(jnp.int32, (12, 12), 0)
    eye = eye == lax.broadcasted_iota(jnp.int32, (12, 12), 1)
    lane = lax.broadcasted_iota(jnp.int32, (12, 128), 1)
    extra = jnp.concatenate([forget_ref[...], jnp.zeros((12, 122), jnp.float32)], axis=1)
    for number in range(2):
        gain = jnp.sum(jnp.where(eye, norm_ref[number : number + 1], 0.0), axis=1, keepdims=True)
        extra = jnp.where(lane == 6 + number, gain, extra)
    even = [square_ref[0], square_ref[1, :, 0:128], wide_ref[0, :, 0:768]]
    even += [square_ref[1, :, 128:384], extra, square_ref[4, :, 0:128]]
    even += [wide_ref[0, :, 768:1024], wide_ref[2, :, 0:512]]
    odd = [square_ref[2], square_ref[3, :, 0:128], wide_ref[1, :, 0:768]]
    odd += [square_ref[3, :, 128:384], square_ref[4, :, 128:384]]
    odd += [wide_ref[1, :, 768:1024], wide_ref[2, :, 512:1024]]
    even = jnp.concatenate(even, axis=1)
    odd = jnp.concatenate(odd, axis=1)
    mine_ref[...] = jnp.where(core == 0, even, odd).astype(jnp.bfloat16)
    other_ref[...] = jnp.where(core == 0, odd, even).astype(jnp.bfloat16)


def spread_kernel(after_ref, rows_ref, out_ref):
    for number in range(8):
        out_ref[number] = rows_ref[...]


def spread_rows(after, rows):
    return call_kernel(
        spread_kernel,
        [in_any, in_vmem],
        [((8,) + rows.shape, jnp.bfloat16)],
        [],
        1000,
        8,
    )(after, rows)[0]


def prepare_kernel(begin, after_ref, plane_ref, *refs):
    spread_ref, stack_ref = refs[4:]
    lanes = slice(begin, begin + spread_ref.shape[3])
    for number in range(4):
        spread_ref[number] = plane_ref[:, :, lanes]
        stack_ref[number] = refs[number][:, lanes]


def prepare(begin, width, after, plane, blocks):
    shapes = ((4, 4, 48, width), (4, 48, width))
    return pl.pallas_call(
        functools.partial(prepare_kernel, begin),
        out_shape=[jax.ShapeDtypeStruct(shape, jnp.bfloat16) for shape in shapes],
        in_specs=[pl.BlockSpec(memory_space=pl.ANY)]
        + [pl.BlockSpec(memory_space=pltpu.VMEM)] * 5,
        out_specs=[pl.BlockSpec(memory_space=pltpu.VMEM)] * 2,
        compiler_params=pltpu.CompilerParams(vmem_limit_bytes=16 * 1024 * 1024),
        cost_estimate=pl.CostEstimate(flops=0, bytes_accessed=1000, transcendentals=0),
    )(after, plane, *blocks)


def assemble_kernel(after_ref, later_ref, plain_ref, *refs):
    blocks, plain_out_ref, out_ref = refs[:4], refs[4], refs[5]
    width = out_ref.shape[3]
    place = lax.axis_index("dp")
    row, column = place // 16, lax.rem(place // 4, 4)
    plain_out_ref[...] = plain_ref[...]
    for number, step in enumerate(ring_steps):
        for inner, inner_step in enumerate(ring_steps):
            place = (lax.rem(row + inner_step, 4), lax.rem(column + step, 4))
            out_ref[place] = blocks[number][inner]
            if len(refs) > 6:
                refs[6][place] = blocks[number][inner, :, width - 256 : width]


def assemble(after, later, plain, blocks, tails):
    width = blocks[0].shape[2]
    shape = jax.ShapeDtypeStruct((4, 4, 48, width), jnp.bfloat16)
    tail_shape = jax.ShapeDtypeStruct((4, 4, 48, 256), jnp.bfloat16)
    plain, ring, *tail = pl.pallas_call(
        assemble_kernel,
        out_shape=[shape, shape] + [tail_shape] * tails,
        in_specs=[pl.BlockSpec(memory_space=pl.ANY)] * 2
        + [pl.BlockSpec(memory_space=pltpu.VMEM)] * 5,
        out_specs=[pl.BlockSpec(memory_space=pltpu.VMEM)] * (2 + tails),
        compiler_params=pltpu.CompilerParams(vmem_limit_bytes=16 * 1024 * 1024),
        cost_estimate=pl.CostEstimate(flops=0, bytes_accessed=1000, transcendentals=0),
    )(after, later, plain.reshape(4, 4, 48, width), *blocks)
    return plain.reshape(768, width), ring.reshape(768, width), *tail


def dot_nn(left, right):
    return jnp.dot(left, right, preferred_element_type=jnp.float32)


def dot_nt(left, right):
    return lax.dot_general(
        left, right, (((1,), (1,)), ((), ())), preferred_element_type=jnp.float32
    )


def dot_tn(left, right):
    return lax.dot_general(
        left, right, (((0,), (0,)), ((), ())), preferred_element_type=jnp.float32
    )


def three_parts(value):
    high = value.astype(jnp.bfloat16)
    rest = value - high.astype(jnp.float32)
    middle = rest.astype(jnp.bfloat16)
    low = (rest - middle.astype(jnp.float32)).astype(jnp.bfloat16)
    return high, middle, low


def exact_nn(ones, value):
    high, middle, low = three_parts(value)
    return dot_nn(ones, high) + dot_nn(ones, middle) + dot_nn(ones, low)


def gain_rows(ext):
    rows = lax.broadcasted_iota(jnp.int32, (16, 128), 0)
    columns = lax.broadcasted_iota(jnp.int32, (16, 128), 1)
    pick = (columns == rows + 6).astype(jnp.float32).astype(jnp.bfloat16)
    return dot_nt(pick, ext)


def head_mask(rows, head):
    lanes = lax.broadcasted_iota(jnp.int32, (rows, 128), 1)
    return (lanes // 64) == head


def lane_pick(array, lane):
    lanes = lax.broadcasted_iota(jnp.int32, array.shape, 1)
    return jnp.sum(jnp.where(lanes == lane, array, 0.0), axis=1, keepdims=True)


def pair_rms(raw, gain):
    first = head_mask(raw.shape[0], 0)
    square = raw * raw
    sum_first = jnp.sum(jnp.where(first, square, 0.0), axis=1, keepdims=True)
    sum_second = jnp.sum(jnp.where(first, 0.0, square), axis=1, keepdims=True)
    mean = jnp.where(first, sum_first, sum_second) * (1.0 / 64.0)
    scale = lax.rsqrt(mean + epsilon)
    return raw * scale * gain, scale


def gain_pair(ref):
    gain = ref[...].astype(jnp.bfloat16).astype(jnp.float32)
    return jnp.concatenate([gain, gain], axis=1)


def doc_columns(doc_row):
    return jnp.broadcast_to(doc_row, (128, doc_row.shape[1])).T[:, 0:1]


def block_scores(query, keys, decay_col, decay_row, allowed, inv_root):
    raw = dot_nt(query, keys) * inv_root + decay_col - decay_row
    return jnp.where(allowed, raw, -1e30)


def allowed_block(doc_col, doc_row, live_count, start, rows, columns):
    queries = start + lax.broadcasted_iota(jnp.int32, (rows, columns), 0)
    keys = lax.broadcasted_iota(jnp.int32, (rows, columns), 1)
    same = doc_col == doc_row
    return same & (keys <= queries) & ((keys < live_count) | (keys == queries))


def load_halves(refs, held, sems):
    core = lax.rem(lax.axis_index("dp"), 2)
    width = refs[0].shape[1]
    copies = []
    for number, ref in enumerate(refs):
        slot = core if number < 2 else 1 - core
        target = held.at[slot, :, pl.ds((number % 2) * width, width)]
        copies.append(pltpu.make_async_copy(ref, target, sems.at[number]))
    for copy in copies:
        copy.start()
    return core, copies


def attend_kernel(
    live_ref,
    tokens_ref,
    mine_plain_ref,
    mine_ring_ref,
    other_plain_ref,
    other_ring_ref,
    gains_ref,
    bias_ref,
    doc_row_ref,
    normed_ref,
    raw_out,
    heads_out,
    gated_mine_ref,
    gated_other_ref,
    gated_ref,
    lanes_out,
    held,
    sems,
    raw_ref,
    heads_ref,
    lanes_ref,
):
    core, loads = load_halves(
        (mine_plain_ref, mine_ring_ref, other_plain_ref, other_ring_ref), held, sems
    )
    query_raw_ref, key_raw_ref, gate_ref, attended_ref = [raw_ref.at[n] for n in range(4)]
    query_ref, key_ref, value_ref = [heads_ref.at[n] for n in range(3)]
    logit_ref, decay_ref, total_ref = [lanes_ref.at[n] for n in range(3)]
    live_count = live_ref[0]
    inv_root = 0.125
    head_gains = gain_pair(gains_ref)
    doc_row = doc_row_ref[...].astype(jnp.float32)
    doc_col = doc_columns(doc_row)
    hidden = tokens_ref[...].astype(jnp.float32)
    scale = lax.rsqrt(jnp.mean(hidden * hidden, axis=1, keepdims=True) + epsilon)
    for copy in loads:
        copy.wait()
    ext = held[0, :, 768:896]
    gains = gain_rows(ext)
    normed = (hidden * scale * gains[0:1]).astype(jnp.bfloat16)
    normed_ref[...] = normed
    for block in range(3):
        lanes = slice(block * 128, block * 128 + 128)
        query_raw = dot_nn(normed, held[0, :, block * 128 : block * 128 + 128])
        key_raw = dot_nn(normed, held[0, :, 384 + block * 128 : 512 + block * 128])
        query_raw_ref[:, lanes] = query_raw
        key_raw_ref[:, lanes] = key_raw
        query_ref[:, lanes] = pair_rms(query_raw, head_gains[0:1])[0].astype(jnp.bfloat16)
        key_ref[:, lanes] = pair_rms(key_raw, head_gains[1:2])[0].astype(jnp.bfloat16)
    value_ref[...] = dot_nn(normed, held[1, :, 0:384]).astype(jnp.bfloat16)
    gate_ref[...] = dot_nn(normed, held[1, :, 384:768])
    lane = lax.broadcasted_iota(jnp.int32, (384, 128), 1)
    bias = bias_ref[...].astype(jnp.bfloat16).astype(jnp.float32)
    bias = jnp.concatenate([bias, jnp.zeros((1, 122), jnp.float32)], axis=1)
    logit = dot_nn(normed, ext) + bias
    logit = jnp.where(lane < 6, logit, 0.0)
    logit_ref[...] = logit
    log_sig = jnp.minimum(logit, 0.0) - jnp.log1p(jnp.exp(-jnp.abs(logit)))
    rows = lax.broadcasted_iota(jnp.int32, (384, 384), 0)
    columns = lax.broadcasted_iota(jnp.int32, (384, 384), 1)
    lower = (columns <= rows).astype(jnp.float32).astype(jnp.bfloat16)
    decay = exact_nn(lower, log_sig)
    decay_ref[...] = decay
    decay_t = decay.T
    for step in range(3):
        begin, count = step * 128, step * 128 + 128
        allowed = allowed_block(
            doc_col[begin : begin + 128],
            doc_row[:, 0:count],
            live_count,
            begin,
            128,
            count,
        )
        totals = jnp.zeros((128, 128), jnp.float32)
        small_lane = lax.broadcasted_iota(jnp.int32, (128, 128), 1)
        for block in range(3):
            lanes = slice(block * 128, block * 128 + 128)
            keys = key_ref[0:count, lanes]
            values = value_ref[0:count, lanes]
            query_pair = query_ref[begin : begin + 128, lanes]
            outs = []
            for half in range(2):
                head = block * 2 + half
                query = jnp.where(head_mask(128, half), query_pair, jnp.zeros_like(query_pair))
                scores = block_scores(
                    query,
                    keys,
                    lane_pick(decay[begin : begin + 128], head),
                    decay_t[head : head + 1, 0:count],
                    allowed,
                    inv_root,
                )
                peak = jnp.max(scores, axis=1, keepdims=True)
                grown = jnp.exp(scores - peak)
                total = jnp.sum(grown, axis=1, keepdims=True)
                totals = jnp.where(small_lane == head, peak + jnp.log(total), totals)
                probs = (grown * (1.0 / total)).astype(jnp.bfloat16)
                outs.append(dot_nn(probs, values))
            attended_ref[begin : begin + 128, lanes] = jnp.where(
                head_mask(128, 0), outs[0], outs[1]
            )
        total_ref[begin : begin + 128, :] = totals
    copies = [
        pltpu.make_async_copy(
            source, target.at[pl.ds(0, source.shape[0])], sems.at[4 + number]
        )
        for number, (source, target) in enumerate(
            ((raw_ref, raw_out), (heads_ref, heads_out), (lanes_ref, lanes_out))
        )
    ]
    for copy in copies:
        copy.start()
    gated = (attended_ref[...] * jax.nn.sigmoid(gate_ref[...])).astype(jnp.bfloat16)
    gated_mine_ref[...] = jnp.where(core == 0, gated[:, 0:256], gated[:, 128:384])
    gated_other_ref[...] = jnp.where(core == 0, gated[:, 128:384], gated[:, 0:256])
    gated_ref[...] = gated
    for copy in copies:
        copy.wait()


def mlp_kernel(
    live_ref,
    tokens_ref,
    gated_ref,
    gated_peer_ref,
    cotangent_ref,
    ext_ref,
    mine_plain_ref,
    mine_ring_ref,
    other_plain_ref,
    other_ring_ref,
    near_mine_ref,
    near_other_ref,
    far_mine_ref,
    far_other_ref,
    middle_ref,
    normed_ref,
    hidden_mine_ref,
    hidden_other_ref,
    out_ref,
    grad_ref,
    held,
    sems,
    out_held,
):
    core, loads = load_halves(
        (mine_plain_ref, mine_ring_ref, other_plain_ref, other_ring_ref), held, sems
    )
    out_loads = []
    for number, ref in enumerate((near_mine_ref, near_other_ref, far_mine_ref, far_other_ref)):
        slot = (number // 2) * 2 + (core if number % 2 == 0 else 1 - core)
        source = ref.at[:, pl.ds(ref.shape[1] - 256, 256)]
        out_loads.append(pltpu.make_async_copy(source, out_held.at[slot], sems.at[4 + number]))
    for copy in out_loads:
        copy.start()
    for copy in out_loads:
        copy.wait()
    parts = []
    for number, ref in enumerate((gated_ref, gated_peer_ref)):
        part = dot_nt(ref[:, 0:128], out_held[2 * number, :, 128:256])
        parts.append(part + dot_nt(ref[:, 128:384], out_held[2 * number + 1]))
    middle = tokens_ref[...].astype(jnp.float32) + (parts[0] + parts[1])
    middle_ref[...] = middle
    gains = gain_rows(ext_ref[...])
    scale = lax.rsqrt(jnp.mean(middle * middle, axis=1, keepdims=True) + epsilon)
    normed = (middle * scale * gains[1:2]).astype(jnp.bfloat16)
    normed_ref[...] = normed
    live_rows = lax.broadcasted_iota(jnp.int32, (384, 1), 0) < live_ref[0]
    grad_out = jnp.where(live_rows, cotangent_ref[...].astype(jnp.float32), 0.0)
    grad_out = grad_out.astype(jnp.bfloat16)
    for copy in loads:
        copy.wait()
    out_total = jnp.zeros((384, 768), jnp.float32)
    grad_total = jnp.zeros((384, 768), jnp.float32)
    parts = []
    for half in range(2):
        begin = half * 512
        gate_w = held[0, :, begin : begin + 512]
        up_w = held[1, :, begin : begin + 512]
        down_w = held[half, :, 1024:1536]
        gate = dot_nn(normed, gate_w)
        up = dot_nn(normed, up_w)
        sig = jax.nn.sigmoid(gate)
        silu = gate * sig
        active = (silu * up).astype(jnp.bfloat16)
        out_total = out_total + dot_nt(active, down_w)
        grad_act = dot_nn(grad_out, down_w)
        grad_up = (grad_act * silu).astype(jnp.bfloat16)
        grad_gate = (grad_act * up * (sig * (1.0 + gate * (1.0 - sig)))).astype(jnp.bfloat16)
        parts.append((grad_gate, grad_up, active))
        grad_total = grad_total + dot_nt(grad_gate, gate_w) + dot_nt(grad_up, up_w)
    for number in range(3):
        lanes = slice(number * 512, number * 512 + 512)
        first, second = parts[0][number], parts[1][number]
        hidden_mine_ref[:, lanes] = jnp.where(core == 0, first, second)
        hidden_other_ref[:, lanes] = jnp.where(core == 0, second, first)
    out_ref[...] = out_total.astype(jnp.bfloat16)
    grad_ref[...] = grad_total.astype(jnp.bfloat16)


def attend_back_kernel(
    after_ref,
    live_ref,
    tokens_ref,
    cotangent_ref,
    middle_ref,
    part_ref,
    peer_ref,
    mine_plain_ref,
    mine_ring_ref,
    other_plain_ref,
    other_ring_ref,
    gains_ref,
    doc_row_ref,
    normed_ref,
    raw_in,
    heads_in,
    lanes_in,
    grad_middle_ref,
    grad_middle_b_ref,
    proj_mine_ref,
    proj_other_ref,
    norm_part_ref,
    extra_ref,
    held,
    sems,
    grad_att_ref,
    grad_query_ref,
    grad_key_ref,
    grad_value_ref,
    grad_og_ref,
    column_ref,
    raw_ref,
    heads_ref,
    lanes_ref,
    settle,
):
    core, loads = load_halves(
        (mine_plain_ref, mine_ring_ref, other_plain_ref, other_ring_ref), held, sems
    )
    settle()
    copies = [
        pltpu.make_async_copy(
            source.at[pl.ds(0, target.shape[0])], target, sems.at[4 + number]
        )
        for number, (source, target) in enumerate(
            ((raw_in, raw_ref), (heads_in, heads_ref), (lanes_in, lanes_ref))
        )
    ]
    for copy in copies:
        copy.start()
    query_raw_ref, key_raw_ref, gate_ref, attended_ref = [raw_ref.at[n] for n in range(4)]
    query_ref, key_ref, value_ref = [heads_ref.at[n] for n in range(3)]
    logit_ref, decay_ref, total_ref = [lanes_ref.at[n] for n in range(3)]
    live_count = live_ref[0]
    inv_root = 0.125
    head_gains = gain_pair(gains_ref)
    doc_row = doc_row_ref[...].astype(jnp.float32)
    doc_col = doc_columns(doc_row)
    middle = middle_ref[...]
    grad_normed = part_ref[...].astype(jnp.float32)
    grad_normed = grad_normed + peer_ref[...].astype(jnp.float32)
    live_rows = lax.broadcasted_iota(jnp.int32, (384, 1), 0) < live_count
    grad_out = jnp.where(live_rows, cotangent_ref[...].astype(jnp.float32), 0.0)
    scale = lax.rsqrt(jnp.mean(middle * middle, axis=1, keepdims=True) + epsilon)
    for copy in loads:
        copy.wait()
    ext = held[0, :, 768:896]
    gains = gain_rows(ext)
    gained = grad_normed * gains[1:2]
    inner = jnp.mean(gained * middle, axis=1, keepdims=True)
    grad_middle = grad_out + (scale * gained - middle * (scale * scale * scale * inner))
    grad_gain = jnp.sum(grad_normed * middle * scale, axis=0, keepdims=True)
    grad_middle_ref[...] = grad_middle
    grad_middle_b = grad_middle.astype(jnp.bfloat16)
    grad_middle_b_ref[...] = grad_middle_b
    grad_gated = jnp.concatenate(
        [
            dot_nn(grad_middle_b, held[0, :, 896:1024]),
            dot_nn(grad_middle_b, held[1, :, 768:1024]),
        ],
        axis=1,
    )
    for copy in copies:
        copy.wait()
    sig = jax.nn.sigmoid(gate_ref[...])
    grad_att_ref[...] = (grad_gated * sig).astype(jnp.bfloat16)
    grad_og = (grad_gated * attended_ref[...] * sig * (1.0 - sig)).astype(jnp.bfloat16)
    grad_og_ref[...] = grad_og
    grad_key_ref[...] = jnp.zeros((384, 384), jnp.float32)
    grad_value_ref[...] = jnp.zeros((384, 384), jnp.float32)
    column_ref[...] = jnp.zeros((128, 384), jnp.float32)
    decay = decay_ref[...]
    decay_t = decay.T
    row_parts = []
    for step in range(3):
        begin, count = step * 128, step * 128 + 128
        allowed = allowed_block(
            doc_col[begin : begin + 128],
            doc_row[:, 0:count],
            live_count,
            begin,
            128,
            count,
        )
        small_lane = lax.broadcasted_iota(jnp.int32, (128, 128), 1)
        row_sums = jnp.zeros((128, 128), jnp.float32)
        for block in range(3):
            lanes = slice(block * 128, block * 128 + 128)
            keys = key_ref[0:count, lanes]
            values = value_ref[0:count, lanes]
            query_pair = query_ref[begin : begin + 128, lanes]
            att_pair = grad_att_ref[begin : begin + 128, lanes]
            outs = []
            key_outs = []
            value_outs = []
            for half in range(2):
                head = block * 2 + half
                mask = head_mask(128, half)
                query = jnp.where(mask, query_pair, jnp.zeros_like(query_pair))
                att = jnp.where(mask, att_pair, jnp.zeros_like(att_pair))
                scores = block_scores(
                    query,
                    keys,
                    lane_pick(decay[begin : begin + 128], head),
                    decay_t[head : head + 1, 0:count],
                    allowed,
                    inv_root,
                )
                probs = jnp.exp(scores - lane_pick(total_ref[begin : begin + 128, :], head))
                grad_probs = dot_nt(att, values)
                row_dot = jnp.sum(probs * grad_probs, axis=1, keepdims=True)
                grad_scores = (probs * (grad_probs - row_dot)).astype(jnp.bfloat16)
                grad_scores_f = grad_scores.astype(jnp.float32)
                row_sums = jnp.where(
                    small_lane == head,
                    jnp.sum(grad_scores_f, axis=1, keepdims=True),
                    row_sums,
                )
                column_ref[head : head + 1, 0:count] += jnp.sum(
                    grad_scores_f, axis=0, keepdims=True
                )
                outs.append(dot_nn(grad_scores, keys))
                key_outs.append(dot_tn(grad_scores, query))
                value_outs.append(dot_tn(probs.astype(jnp.bfloat16), att))
            grad_query_ref[begin : begin + 128, lanes] = jnp.where(
                head_mask(128, 0), outs[0], outs[1]
            )
            grad_key_ref[0:count, lanes] += key_outs[0] + key_outs[1]
            grad_value_ref[0:count, lanes] += value_outs[0] + value_outs[1]
        row_parts.append(row_sums)
    grad_decay = jnp.concatenate(row_parts, axis=0) - column_ref[...].T
    rows = lax.broadcasted_iota(jnp.int32, (384, 384), 0)
    columns = lax.broadcasted_iota(jnp.int32, (384, 384), 1)
    upper = (columns >= rows).astype(jnp.float32).astype(jnp.bfloat16)
    grad_logit = exact_nn(upper, grad_decay) * jax.nn.sigmoid(-logit_ref[...])
    lane = lax.broadcasted_iota(jnp.int32, (384, 128), 1)
    grad_logit = jnp.where(lane < 6, grad_logit, 0.0)
    grad_forget = grad_logit.astype(jnp.bfloat16)
    grad_vg = jnp.concatenate([grad_value_ref[...].astype(jnp.bfloat16), grad_og_ref[...]], axis=1)
    grad_qk = []
    gain_sums = []
    for number, raw_ref, out_ref in (
        (0, query_raw_ref, grad_query_ref),
        (1, key_raw_ref, grad_key_ref),
    ):
        gain = head_gains[number : number + 1]
        gain_sum = jnp.zeros((1, 128), jnp.float32)
        for block in range(3):
            lanes = slice(block * 128, block * 128 + 128)
            raw = raw_ref[:, lanes]
            grad = (out_ref[:, lanes] * inv_root).astype(jnp.bfloat16).astype(jnp.float32)
            first = head_mask(384, 0)
            scaled = pair_rms(raw, 1.0)[1]
            weighted = grad * gain
            product = weighted * raw
            sum_first = jnp.sum(jnp.where(first, product, 0.0), axis=1, keepdims=True)
            sum_second = jnp.sum(jnp.where(first, 0.0, product), axis=1, keepdims=True)
            inner_head = jnp.where(first, sum_first, sum_second) * (1.0 / 64.0)
            gain_sum = gain_sum + jnp.sum(grad * raw * scaled, axis=0, keepdims=True)
            grad_raw = scaled * weighted - raw * (scaled * scaled * scaled * inner_head)
            grad_qk.append(grad_raw.astype(jnp.bfloat16))
        gain_sums.append(gain_sum)
    grad_qk = jnp.concatenate(grad_qk, axis=1)
    proj_mine_ref[...] = jnp.where(core == 0, grad_qk, grad_vg)
    proj_other_ref[...] = jnp.where(core == 0, grad_vg, grad_qk)
    part = dot_nt(grad_qk, held[0, :, 0:768])
    part = part + dot_nt(grad_vg, held[1, :, 0:768])
    part = part + dot_nt(grad_forget, ext)
    norm_part_ref[...] = part.astype(jnp.bfloat16)
    hidden = tokens_ref[...].astype(jnp.float32)
    scale = lax.rsqrt(jnp.mean(hidden * hidden, axis=1, keepdims=True) + epsilon)
    first_gain = jnp.sum(part * (hidden * scale), axis=0, keepdims=True)
    line = lax.broadcasted_iota(jnp.int32, (128, 768), 0)
    extra = jnp.where(line == 6, first_gain, jnp.where(line == 7, grad_gain, 0.0)).T
    extra = extra + dot_tn(normed_ref[...], grad_forget)
    bias_sum = jnp.sum(grad_forget.astype(jnp.float32), axis=0, keepdims=True)
    sums = [total + pltpu.roll(total, 64, 1) for total in (gain_sums[0], gain_sums[1], bias_sum)]
    line = lax.rem(lax.broadcasted_iota(jnp.int32, (768, 128), 0), 12)
    lane = lax.broadcasted_iota(jnp.int32, (768, 128), 1)
    for number in range(3):
        extra = jnp.where((line == number) & (lane >= 64), sums[number], extra)
    extra_ref[...] = extra.astype(jnp.bfloat16)


def wide_grad_kernel(*refs):
    normed, normed_peer, hidden, hidden_peer, grad, grad_peer, out_ref = refs
    for begin in range(0, 1536, 256):
        lanes = slice(begin, begin + 256)
        left, left_peer = (normed, normed_peer) if begin < 1024 else (grad, grad_peer)
        total = dot_tn(left[...], hidden[:, lanes]) + dot_tn(left_peer[...], hidden_peer[:, lanes])
        out_ref[:, lanes] = total.astype(jnp.bfloat16)


def proj_grad_kernel(after_ref, *refs):
    first, first_peer, left, left_peer, second, second_peer, right, right_peer = refs[:8]
    extra_ref, out_ref = refs[8], refs[9]
    out_ref[:, 1024:1152] = extra_ref[...]
    for begin in range(0, 1024, 256):
        if begin < 768:
            lanes = slice(begin, begin + 256)
            total = dot_tn(first[...], left[:, lanes])
            total = total + dot_tn(first_peer[...], left_peer[:, lanes])
        else:
            total = dot_tn(second[...], right[...]) + dot_tn(second_peer[...], right_peer[...])
        out_ref[:, begin : begin + 256] = total.astype(jnp.bfloat16)


def mirror(out_ref, block, start):
    out_ref[start : start + 256, start:768] = block.astype(jnp.bfloat16)
    for other in range(start + 256, 768, 256):
        piece = block[:, other - start : other - start + 256]
        out_ref[other : other + 256, start : start + 256] = piece.T.astype(jnp.bfloat16)


def plane_sum_kernel(*refs):
    blocks_ref, mine_ref, other_ref = refs[-3:]
    level = lax.rem(lax.axis_index("dp") // 2, 2)
    for start in range(0, blocks_ref.shape[2], 256):
        lanes = slice(start, start + 256)
        total = blocks_ref[0, :, lanes].astype(jnp.float32)
        for number in range(1, 16):
            total = total + blocks_ref[number, :, lanes].astype(jnp.float32)
        first, second = total[0:24], total[24:48]
        mine_ref[:, lanes] = jnp.where(level == 0, first, second)
        other_ref[:, lanes] = jnp.where(level == 0, second, first)


def momentum_kernel(
    mine_ref,
    other_ref,
    old_ref,
    tokens_ref,
    grad_middle_ref,
    norm_part_ref,
    norm_peer_ref,
    ext_ref,
    middle_ref,
    mlp_part_ref,
    mlp_peer_ref,
    new_ref,
    keep_ref,
    send_ref,
    small_ref,
    input_grad_ref,
    result_ref,
):
    place = lax.axis_index("dp")
    core, level = lax.rem(place, 2), lax.rem(place // 2, 2)
    mine, other = mine_ref[...], other_ref[...]
    even = jnp.where(core == 0, mine, other)
    odd = jnp.where(core == 0, other, mine)
    small_ref[...] = mine[:, 1024:1152] + other[:, 1024:1152]
    fresh = [even[:, 0:384], even[:, 384:768], odd[:, 0:384], odd[:, 384:768]]
    fresh.append(jnp.concatenate([even[:, 768:1024], odd[:, 896:1024]], axis=1))
    fresh = [muon_decay * old_ref[number] + fresh[number] for number in range(5)]
    for number in range(5):
        new_ref[number] = fresh[number]
    for number in range(4):
        keep_ref[number] = jnp.where(level == 0, fresh[4], fresh[number])
        send_ref[number] = jnp.where(level == 0, fresh[number], fresh[4])
    hidden = tokens_ref[...].astype(jnp.float32)
    gain = gain_rows(ext_ref[...])[0:1]
    added = mlp_part_ref[...].astype(jnp.float32) + mlp_peer_ref[...].astype(jnp.float32)
    result_ref[...] = (middle_ref[...] + added).astype(jnp.bfloat16)
    grad = norm_part_ref[...].astype(jnp.float32) + norm_peer_ref[...].astype(jnp.float32)
    scale = lax.rsqrt(jnp.mean(hidden * hidden, axis=1, keepdims=True) + epsilon)
    gained = grad * gain
    inner = jnp.mean(gained * hidden, axis=1, keepdims=True)
    input_grad_ref[...] = grad_middle_ref[...] + (
        scale * gained - hidden * (scale * scale * scale * inner)
    )


def small_kernel(
    mine_ref,
    peer_ref,
    norm_ref,
    qk_ref,
    forget_ref,
    bias_ref,
    m_norm_ref,
    m_qk_ref,
    m_forget_ref,
    m_bias_ref,
    after_ref,
    new_norm_ref,
    new_qk_ref,
    new_forget_ref,
    new_bias_ref,
    mom_norm_ref,
    mom_qk_ref,
    mom_forget_ref,
    mom_bias_ref,
):
    root_tokens = math.sqrt(24576.0)
    mine, both = mine_ref[...], mine_ref[...] + peer_ref[...]
    lane = lax.broadcasted_iota(jnp.int32, (12, 128), 1)
    norms = jnp.where(lane == 6, both, mine).T
    grads = (
        (norms[6:8, :], gain_rate, norm_ref, m_norm_ref, new_norm_ref, mom_norm_ref),
        (both[0:2, 64:128], qk_rate, qk_ref, m_qk_ref, new_qk_ref, mom_qk_ref),
        (mine[:, 0:6], forget_rate, forget_ref, m_forget_ref, new_forget_ref, mom_forget_ref),
        (mine[2:3, 64:70], bias_rate, bias_ref, m_bias_ref, new_bias_ref, mom_bias_ref),
    )
    for grad, rate, value_ref, old_ref, new_ref, mom_ref in grads:
        moment = plain_decay * old_ref[...] + grad
        mom_ref[...] = moment
        new_ref[...] = value_ref[...] - (rate / root_tokens) * moment


def newton_body(sources, out_ref, held, square_ref, poly_ref):
    columns, sides, width = sources[0].shape[2], held.shape[1], held.shape[3]
    total = jnp.zeros((1, 1), jnp.float32)
    for source in sources:
        for number in range(8):
            for start in (0, 48):
                piece = source[number, start : start + 48, :].astype(jnp.float32)
                piece = jnp.sum(piece * piece, axis=0, keepdims=True)
                total = total + jnp.sum(piece, axis=1, keepdims=True)
    scale = 1.0 / (jnp.sqrt(total) + 1e-07)
    for place, source in zip((0, 384), sources):
        for number in range(8):
            first = (number // 4) * columns
            lanes = slice(first % width, first % width + columns)
            for start in (0, 48):
                piece = source[number, start : start + 48, :].astype(jnp.float32) * scale
                begin = place + (number % 4) * 96 + start
                held[0, first // width, begin : begin + 48, lanes] = piece.astype(jnp.bfloat16)
    for repeat in range(5):
        now, later = repeat % 2, (repeat + 1) % 2
        for start in range(0, 768, 256):
            rows, right = slice(start, start + 256), slice(start, 768)
            square = dot_nt(held[now, 0, rows, :], held[now, 0, right, :])
            for side in range(1, sides):
                square = square + dot_nt(held[now, side, rows, :], held[now, side, right, :])
            mirror(square_ref, square, start)
        if repeat < 4:
            for start in range(0, 768, 256):
                rows, right = slice(start, start + 256), slice(start, 768)
                poly = coef_b * square_ref[rows, right].astype(jnp.float32)
                poly = poly + coef_c * dot_nn(square_ref[rows, :], square_ref[:, right])
                mirror(poly_ref, poly, start)
            for side in range(sides):
                for start in range(0, 768, 256):
                    grown = coef_a * held[now, side, start : start + 256, :].astype(jnp.float32)
                    grown = grown + dot_nn(poly_ref[start : start + 256, :], held[now, side])
                    held[later, side, start : start + 256, :] = grown.astype(jnp.bfloat16)
        else:
            half = lax.axis_index("tensor")
            side, first = (half, 0) if sides == 2 else (0, pl.multiple_of(half * columns, 128))
            begin = pl.multiple_of((lax.axis_index("dp") // 16) * 96, 16)
            few = square_ref[pl.ds(begin, 96), :]
            poly = coef_b * few.astype(jnp.float32) + coef_c * dot_nn(few, square_ref[...])
            poly = poly.astype(jnp.bfloat16)
            grown = held[now, side, pl.ds(begin, 96), pl.ds(first, columns)].astype(jnp.float32)
            grown = coef_a * grown + dot_nn(poly, held[now, side, :, pl.ds(first, columns)])
            out_ref[...] = grown.astype(jnp.bfloat16)


def newton_kernel(wants_wide, after_ref, mine_any, other_any, out_ref, *scratch):
    place = lax.axis_index("dp")
    is_wide = (lax.rem(place // 2, 2) == 0) & (lax.rem(place // 4, 4) < 3)
    active = is_wide if wants_wide else jnp.logical_not(is_wide)

    @pl.when(active)
    def run():
        sources, sems = scratch[3:5], scratch[5]
        loads = [
            pltpu.make_async_copy(source, target, sems.at[number])
            for number, (source, target) in enumerate(zip((mine_any, other_any), sources))
        ]
        for copy in loads:
            copy.start()
        for copy in loads:
            copy.wait()
        newton_body(sources, out_ref, *scratch[:3])

    @pl.when(jnp.logical_not(active))
    def skip():
        out_ref[...] = jnp.zeros(out_ref.shape, jnp.bfloat16)


in_vmem = pl.BlockSpec(memory_space=pltpu.VMEM)
in_smem = pl.BlockSpec(memory_space=pltpu.SMEM)
in_any = pl.BlockSpec(memory_space=pl.ANY)
in_hbm = pl.BlockSpec(memory_space=pltpu.HBM)


def call_kernel(kernel, in_specs, outs, scratch, flops, limit=24, far=(), staged=False):
    near = [number for number in range(len(outs)) if number not in far]
    moved = [number for number, spec in enumerate(in_specs) if spec is in_vmem]
    count = len(in_specs) + len(outs) + len(scratch)

    def staged_kernel(*refs):
        refs, buffers = list(refs[:count]), refs[count:]
        sems = buffers[-1]
        loads = []
        for slot, number in enumerate(moved):
            loads.append(pltpu.make_async_copy(refs[number], buffers[slot], sems.at[slot]))
            refs[number] = buffers[slot]
        for copy in loads:
            copy.start()
        stores = []
        for slot, number in enumerate(near):
            place, slot = len(in_specs) + number, len(moved) + slot
            stores.append(pltpu.make_async_copy(buffers[slot], refs[place], sems.at[slot]))
            refs[place] = buffers[slot]

        def settle():
            for copy in loads:
                copy.wait()

        kernel(*refs, settle=settle)
        for copy in stores:
            copy.start()
        for copy in stores:
            copy.wait()

    def run(*operands):
        buffers = []
        if staged:
            buffers = [pltpu.VMEM(operands[n].shape, operands[n].dtype) for n in moved]
            buffers += [pltpu.VMEM(*outs[n]) for n in near]
            buffers.append(pltpu.SemaphoreType.DMA((len(buffers),)))
        out_specs = [in_hbm if staged or n in far else in_vmem for n in range(len(outs))]
        return pl.pallas_call(
            staged_kernel if staged else kernel,
            out_shape=[jax.ShapeDtypeStruct(shape, dtype) for shape, dtype in outs],
            in_specs=[in_any if staged and spec is in_vmem else spec for spec in in_specs],
            out_specs=out_specs,
            scratch_shapes=list(scratch) + buffers,
            compiler_params=pltpu.CompilerParams(vmem_limit_bytes=limit * 1024 * 1024),
            cost_estimate=pl.CostEstimate(flops=flops, bytes_accessed=1000, transcendentals=0),
        )(*operands)

    return run


def newton(wants_wide, after, mine, other):
    columns = mine.shape[2]
    return call_kernel(
        functools.partial(newton_kernel, wants_wide),
        [in_any] * 3,
        [((96, columns), jnp.bfloat16)],
        [
            pltpu.VMEM((2, 2 * columns // max(columns, 768), 768, max(columns, 768)), jnp.bfloat16),
            pltpu.VMEM((768, 768), jnp.bfloat16),
            pltpu.VMEM((768, 768), jnp.bfloat16),
            pltpu.VMEM((8, 96, columns), jnp.bfloat16),
            pltpu.VMEM((8, 96, columns), jnp.bfloat16),
            pltpu.SemaphoreType.DMA((2,)),
        ],
        200000000000 if wants_wide else 1000,
    )(after, mine, other)[0]


def spread_slots(slots_b):
    column = place_of("x")

    def slot(step):
        number = jnp.minimum((column + step) % 4, slots_b.shape[0] - 1)
        return lax.dynamic_index_in_dim(slots_b, number, 0, keepdims=False)

    pieces = [slot(0)] + [fetch(slot(4 - step), "x", step) for step in (1, 2, 3)]
    return jnp.concatenate(pieces, axis=0)


def ring_order(rows, count):
    column = place_of("x")
    blocks = rows.reshape(4, 24, count)
    return jnp.stack(
        [lax.dynamic_index_in_dim(blocks, (n - column) % 4, 0, False) for n in range(4)]
    )


def on_device(
    tokens,
    cotangent,
    segment_ids,
    live_len,
    w_square,
    w_wide,
    norm_gain,
    qk_gain,
    forget_w,
    forget_b,
    m_square,
    m_wide,
    m_norm,
    m_qk,
    m_forget_w,
    m_forget_b,
    ema_square,
    ema_wide,
):
    half_width = w_square.shape[2]
    half_hidden = w_wide.shape[2]
    shard_rows = w_square.shape[1]
    head_local = forget_w.shape[1]
    head_dim = qk_gain.shape[1]
    dp_size = lax.axis_size("dp")
    full_width = shard_rows * dp_size
    full_hidden = half_hidden * lax.axis_size("tensor")
    my_place = lax.axis_index("dp")
    core = my_place % 2
    quarter_hidden = half_hidden // 2
    bf16, f32 = jnp.bfloat16, jnp.float32

    pack_mine, pack_other = call_kernel(
        pack_kernel, [in_vmem] * 4, [((shard_rows, 2560), bf16)] * 2, [], 1000, 8
    )(w_square, w_wide, norm_gain, forget_w)
    pair_rows = pair_join(core, pack_mine, core_swap(pack_other), 0)
    ring_rows = pair_rows[:, 1280:]
    ring_rows = pair_join(place_of("l"), ring_rows, fetch(ring_rows, "l", 1), 0)
    row_plane = exchange(spread_rows(ring_rows, pair_rows[:, :1280]), ("x", "l"))
    row_plane = row_plane.reshape(4, 48, 1280)
    blocks_y = fetch_ring(ring_rows, "y")

    def both_cores(after, later, plain, blocks, tails=0):
        plain, ring, *tail = assemble(after, later, plain, blocks, tails)
        return (plain, ring, core_swap(plain), core_swap(ring)), tail

    spread, stack = prepare(0, 512, pair_rows, row_plane, blocks_y)
    first_plane, first_blocks = exchange(spread, ("y",)), fetch_ring(stack, "x")
    first_weights, (out_tail,) = both_cores(pair_rows, pair_rows, first_plane, first_blocks, 1)
    out_tail = out_tail.reshape(768, 256)
    spread, stack = prepare(512, 768, first_weights[1], row_plane, blocks_y)
    late_plane, late_blocks = exchange(spread, ("y",)), fetch_ring(stack, "x")
    far_tail = tensor_swap(out_tail)
    far_tail_other = core_swap(far_tail)
    ext = by_core(core, first_weights[1][:, 256:384], first_weights[3][:, 256:384])

    bias_row = forget_b[None]
    live_mask = (jnp.arange(tokens.shape[0]) < live_len[0])[:, None]
    grad_out_b = jnp.where(live_mask, cotangent, jnp.zeros_like(cotangent))

    def paired(mine, other):
        return mine, core_swap(other)

    token_h = ((384, 768), bf16)
    token_f = ((384, 768), f32)
    (
        normed_one,
        raw,
        heads,
        gated_mine,
        gated_other,
        gated,
        head_lanes,
    ) = call_kernel(
        attend_kernel,
        [in_smem, in_vmem] + [in_any] * 4 + [in_vmem] * 3,
        [token_h, ((48, 384, 384), f32), ((100, 384, 384), bf16)]
        + [((384, 256), bf16)] * 2
        + [((384, 384), bf16), ((150, 384, 128), f32)],
        [
            pltpu.VMEM((2, 768, 1024), bf16),
            pltpu.SemaphoreType.DMA((7,)),
            pltpu.VMEM((4, 384, 384), f32),
            pltpu.VMEM((3, 384, 384), bf16),
            pltpu.VMEM((3, 384, 128), f32),
        ],
        1000,
        24,
        (1, 2, 6),
    )(live_len, tokens, *first_weights, qk_gain, bias_row, segment_ids)
    second_weights = both_cores(
        core_swap(gated[:16, :128]), far_tail, late_plane, late_blocks
    )[0]
    normed_one_pair = paired(normed_one, normed_one)
    gated_pair = paired(gated_mine, gated_other)
    grad_out_pair = paired(grad_out_b, grad_out_b)
    middle, normed_two, hidden_mine, hidden_other, mlp_part, grad_part = call_kernel(
        mlp_kernel,
        [in_smem] + [in_vmem] * 5 + [in_any] * 8,
        [token_f, token_h, ((384, 1536), bf16), ((384, 1536), bf16), token_h, token_h],
        [
            pltpu.VMEM((2, 768, 1536), bf16),
            pltpu.SemaphoreType.DMA((8,)),
            pltpu.VMEM((4, 768, 256), bf16),
        ],
        1000,
        24,
    )(
        live_len,
        tokens,
        gated,
        tensor_swap(gated),
        cotangent,
        ext,
        *second_weights,
        first_weights[1],
        first_weights[3],
        far_tail,
        far_tail_other,
    )
    grad_peer = tensor_swap(grad_part)

    normed_two_pair = paired(normed_two, normed_two)
    hidden_pair = paired(hidden_mine, hidden_other)
    grad_wide_b = call_kernel(
        wide_grad_kernel,
        [in_vmem] * 6,
        [((768, 1536), bf16)],
        [],
        1000,
        24,
    )(*normed_two_pair, *hidden_pair, *grad_out_pair)[0]
    level = place_of("l")
    wide_blocks = exchange(grad_wide_b.reshape(16, 48, 3 * quarter_hidden), ("y", "x"))

    (
        grad_middle,
        grad_middle_b,
        proj_mine,
        proj_other,
        norm_part,
        extra,
    ) = call_kernel(
        attend_back_kernel,
        [in_any, in_smem] + [in_vmem] * 5 + [in_any] * 4 + [in_vmem] * 3 + [in_hbm] * 3,
        [token_f, token_h, token_h, token_h, token_h, ((768, 128), bf16)],
        [
            pltpu.VMEM((2, 768, 1024), bf16),
            pltpu.SemaphoreType.DMA((7,)),
            pltpu.VMEM((384, 384), bf16),
            pltpu.VMEM((384, 384), f32),
            pltpu.VMEM((384, 384), f32),
            pltpu.VMEM((384, 384), f32),
            pltpu.VMEM((384, 384), bf16),
            pltpu.VMEM((128, 384), f32),
            pltpu.VMEM((4, 384, 384), f32),
            pltpu.VMEM((3, 384, 384), bf16),
            pltpu.VMEM((3, 384, 128), f32),
        ],
        100000000000,
        56,
        staged=True,
    )(
        grad_wide_b,
        live_len,
        tokens,
        cotangent,
        middle,
        grad_part,
        grad_peer,
        *first_weights,
        qk_gain,
        segment_ids,
        normed_one,
        raw,
        heads,
        head_lanes,
    )
    proj_pair = paired(proj_mine, proj_other)
    grad_middle_pair = paired(grad_middle_b, grad_middle_b)
    mlp_peer = tensor_swap(mlp_part)
    grad_proj_b = call_kernel(
        proj_grad_kernel,
        [in_any] + [in_vmem] * 9,
        [((768, 1152), bf16)],
        [],
        1000,
        24,
    )(
        mlp_peer,
        *normed_one_pair,
        *proj_pair,
        *grad_middle_pair,
        *gated_pair,
        extra,
    )[0]
    norm_peer = tensor_swap(norm_part)
    mine, other = call_kernel(
        plane_sum_kernel,
        [in_any] * 2 + [in_vmem],
        [((24, 3 * quarter_hidden), f32)] * 2,
        [],
        1000,
    )(grad_proj_b, norm_peer, wide_blocks)
    other = other.astype(bf16)
    mine, other = pair_split(core, mine + fetch(other, "l", 1).astype(f32), 0)
    other = core_swap(other)
    wide_shard = jnp.stack(
        [
            pair_join(core, mine[:, start : start + 512], other[:, start : start + 512], 1)
            for start in (0, 512, 1024)
        ]
    )
    mom_wide = muon_decay * m_wide + wide_shard

    wide_slots = mom_wide.astype(bf16)
    wide_pair = jnp.concatenate([wide_slots, fetch(wide_slots, "l", 1)], axis=1)
    wide_rows = spread_slots(wide_pair)
    proj_blocks = exchange(grad_proj_b.reshape(32, 24, 1152), ("y", "x", "l"))
    proj_blocks, wide_rows = lax.optimization_barrier((proj_blocks, wide_rows))
    wide_own = gather(wide_rows, ("t", "y"))
    mine, other = pair_split(core, jnp.sum(proj_blocks.astype(f32), axis=0), 0)
    other = core_swap(other)
    mom_square, keep_slots, send_slots, small, input_grad, result = call_kernel(
        momentum_kernel,
        [in_vmem] * 11,
        [
            ((5, 12, half_width), f32),
            ((4, 12, half_width), f32),
            ((4, 12, half_width), f32),
            ((12, 128), f32),
            token_f,
            token_h,
        ],
        [],
        1000,
        24,
    )(
        mine,
        other,
        m_square,
        tokens,
        grad_middle,
        norm_part,
        norm_peer,
        ext,
        middle,
        mlp_part,
        mlp_peer,
    )
    keep_slots, send_slots = keep_slots.astype(bf16), send_slots.astype(bf16)
    proj_rows = spread_slots(pair_join(level, keep_slots, fetch(send_slots, "l", 1), 1))
    wide_own, proj_rows = lax.optimization_barrier((wide_own, proj_rows))
    wide_other = core_swap(wide_own)
    proj_own = gather(proj_rows, ("t", "y"))
    wide_rows = newton(True, small, wide_own, wide_other)
    proj_own, wide_rows = lax.optimization_barrier((proj_own, wide_rows))
    proj_rows = newton(False, wide_rows, proj_own, core_swap(proj_own))
    proj_rows = jnp.pad(proj_rows, ((0, 0), (0, half_hidden - half_width)))
    rows = ring_order(proj_rows + wide_rows, half_hidden).reshape(8, 12, half_hidden)
    update = exchange(rows, ("x", "l")).astype(f32)
    update_wide = update[0:6:2]
    update_square = jnp.concatenate([update[1::2], update[6:7]], axis=0)[:, :, :half_width]

    small_peer = tensor_swap(small)
    (
        new_norm,
        new_qk,
        new_forget_w,
        new_forget_b,
        mom_norm,
        mom_qk,
        mom_forget_w,
        mom_forget_b,
    ) = call_kernel(
        small_kernel,
        [in_vmem] * 10 + [in_any],
        [(value.shape, f32) for value in (norm_gain, qk_gain, forget_w)]
        + [((1, head_local), f32)]
        + [(value.shape, f32) for value in (norm_gain, qk_gain, forget_w)]
        + [((1, head_local), f32)],
        [],
        1000,
        16,
    )(
        small,
        small_peer,
        norm_gain,
        qk_gain,
        forget_w,
        forget_b[None],
        m_norm,
        m_qk,
        m_forget_w,
        m_forget_b[None],
        proj_rows,
    )
    new_forget_b, mom_forget_b = new_forget_b[0], mom_forget_b[0]
    new_square = w_square - update_square
    new_wide = w_wide - math.sqrt(full_hidden / full_width) * update_wide
    new_ema_square = ema_decay * ema_square + (1.0 - ema_decay) * new_square
    new_ema_wide = ema_decay * ema_wide + (1.0 - ema_decay) * new_wide
    return (
        result,
        input_grad,
        new_square,
        new_wide,
        new_norm,
        new_qk,
        new_forget_w,
        new_forget_b,
        mom_square,
        mom_wide,
        mom_norm,
        mom_qk,
        mom_forget_w,
        mom_forget_b,
        new_ema_square,
        new_ema_wide,
    )


def solution(mesh):
    placed = (
        P("dp", None),
        P("dp", None),
        P("dp", None),
        P("dp"),
        P(None, "dp", "tensor"),
        P(None, "dp", "tensor"),
        P(None, "dp"),
        P(),
        P("dp", "tensor"),
        P("tensor"),
        P(None, "dp", "tensor"),
        P(None, "dp", "tensor"),
        P(None, "dp"),
        P(),
        P("dp", "tensor"),
        P("tensor"),
        P(None, "dp", "tensor"),
        P(None, "dp", "tensor"),
    )
    return jax.shard_map(
        on_device,
        mesh=mesh,
        in_specs=placed,
        out_specs=(
            P("dp", None),
            P("dp", None),
            P(None, "dp", "tensor"),
            P(None, "dp", "tensor"),
            P(None, "dp"),
            P(),
            P("dp", "tensor"),
            P("tensor"),
            P(None, "dp", "tensor"),
            P(None, "dp", "tensor"),
            P(None, "dp"),
            P(),
            P("dp", "tensor"),
            P("tensor"),
            P(None, "dp", "tensor"),
            P(None, "dp", "tensor"),
        ),
        check_vma=False,
    )
```

```python
import functools
import math

import jax
import jax.numpy as jnp
from jax import lax
import numpy as np
from jax.experimental import pallas as pl
from jax.experimental.pallas import tpu as pltpu
from jax.sharding import PartitionSpec as P

epsilon = 1e-06
coef_a = 3.4445
coef_b = -4.775
coef_c = 2.0315
muon_decay = 0.95
plain_decay = 0.9
ema_decay = 0.7
gain_rate = 0.2
qk_rate = 0.05
forget_rate = 0.1
bias_rate = 0.5


grid_sizes = {"y": 4, "x": 4, "l": 2, "c": 2, "t": 2}
dp_names = ["y", "x", "l", "c"]


def ring_groups(names, over):
    order = [name for name in over if name not in names]
    table = np.arange(math.prod(grid_sizes[name] for name in over))
    table = table.reshape([grid_sizes[name] for name in over])
    table = table.transpose([over.index(name) for name in order + list(names)])
    return table.reshape(-1, math.prod(grid_sizes[name] for name in names)).tolist()


def exchange(blocks, names):
    axes = ("dp", "tensor") if "t" in names else "dp"
    return lax.all_to_all(
        blocks,
        axes,
        split_axis=0,
        concat_axis=0,
        tiled=True,
        axis_index_groups=ring_groups(names, dp_names + (["t"] if "t" in names else [])),
    )


def gather(block, names):
    count = math.prod(grid_sizes[name] for name in names)
    return exchange(jnp.broadcast_to(block[None], (count,) + block.shape), names)


def place_of(name):
    place = lax.axis_index("dp")
    return {"y": place // 16, "x": (place // 4) % 4, "l": (place // 2) % 2, "c": place % 2}[name]


def fetch(array, name, step):
    table = np.arange(64).reshape(4, 4, 2, 2)
    sources = np.roll(table, -step, axis=dp_names.index(name))
    pairs = [(int(a), int(b)) for a, b in zip(sources.ravel(), table.ravel())]
    return lax.ppermute(array, "dp", pairs)


def fetch_ring(array, name):
    return [array] + [fetch(array, name, step) for step in (1, 3, 2)]


ring_steps = (0, 1, 3, 2)


def core_swap(array):
    return fetch(array, "c", 1)


def tensor_swap(array):
    return lax.ppermute(array, "tensor", [(0, 1), (1, 0)])


def by_core(core, even, odd):
    return jnp.where(core == 0, even, odd)


def pair_join(place, mine, other, axis):
    return jnp.where(
        place == 0,
        jnp.concatenate([mine, other], axis=axis),
        jnp.concatenate([other, mine], axis=axis),
    )


def pair_split(core, array, axis):
    first, second = jnp.split(array, 2, axis=axis)
    return by_core(core, first, second), by_core(core, second, first)


def pack_kernel(square_ref, wide_ref, norm_ref, forget_ref, mine_ref, other_ref):
    core = lax.rem(lax.axis_index("dp"), 2)
    eye = lax.broadcasted_iota(jnp.int32, (12, 12), 0)
    eye = eye == lax.broadcasted_iota(jnp.int32, (12, 12), 1)
    lane = lax.broadcasted_iota(jnp.int32, (12, 128), 1)
    extra = jnp.concatenate([forget_ref[...], jnp.zeros((12, 122), jnp.float32)], axis=1)
    for number in range(2):
        gain = jnp.sum(jnp.where(eye, norm_ref[number : number + 1], 0.0), axis=1, keepdims=True)
        extra = jnp.where(lane == 6 + number, gain, extra)
    even = [square_ref[0], square_ref[1, :, 0:128], wide_ref[0, :, 0:768]]
    even += [square_ref[1, :, 128:384], extra, square_ref[4, :, 0:128]]
    even += [wide_ref[0, :, 768:1024], wide_ref[2, :, 0:512]]
    odd = [square_ref[2], square_ref[3, :, 0:128], wide_ref[1, :, 0:768]]
    odd += [square_ref[3, :, 128:384], square_ref[4, :, 128:384]]
    odd += [wide_ref[1, :, 768:1024], wide_ref[2, :, 512:1024]]
    even = jnp.concatenate(even, axis=1)
    odd = jnp.concatenate(odd, axis=1)
    mine_ref[...] = jnp.where(core == 0, even, odd).astype(jnp.bfloat16)
    other_ref[...] = jnp.where(core == 0, odd, even).astype(jnp.bfloat16)


def spread_kernel(after_ref, rows_ref, out_ref):
    for number in range(8):
        out_ref[number] = rows_ref[...]


def spread_rows(after, rows):
    return call_kernel(
        spread_kernel,
        [in_any, in_vmem],
        [((8,) + rows.shape, jnp.bfloat16)],
        [],
        1000,
        8,
    )(after, rows)[0]


def prepare_kernel(begin, after_ref, plane_ref, *refs):
    spread_ref, stack_ref = refs[4:]
    lanes = slice(begin, begin + spread_ref.shape[3])
    for number in range(4):
        spread_ref[number] = plane_ref[:, :, lanes]
        stack_ref[number] = refs[number][:, lanes]


def prepare(begin, width, after, plane, blocks):
    shapes = ((4, 4, 48, width), (4, 48, width))
    return pl.pallas_call(
        functools.partial(prepare_kernel, begin),
        out_shape=[jax.ShapeDtypeStruct(shape, jnp.bfloat16) for shape in shapes],
        in_specs=[pl.BlockSpec(memory_space=pl.ANY)]
        + [pl.BlockSpec(memory_space=pltpu.VMEM)] * 5,
        out_specs=[pl.BlockSpec(memory_space=pltpu.VMEM)] * 2,
        compiler_params=pltpu.CompilerParams(vmem_limit_bytes=16 * 1024 * 1024),
        cost_estimate=pl.CostEstimate(flops=0, bytes_accessed=1000, transcendentals=0),
    )(after, plane, *blocks)


def assemble_kernel(after_ref, later_ref, plain_ref, *refs):
    blocks, plain_out_ref, out_ref = refs[:4], refs[4], refs[5]
    width = out_ref.shape[3]
    place = lax.axis_index("dp")
    row, column = place // 16, lax.rem(place // 4, 4)
    plain_out_ref[...] = plain_ref[...]
    for number, step in enumerate(ring_steps):
        for inner, inner_step in enumerate(ring_steps):
            place = (lax.rem(row + inner_step, 4), lax.rem(column + step, 4))
            out_ref[place] = blocks[number][inner]
            if len(refs) > 6:
                refs[6][place] = blocks[number][inner, :, width - 256 : width]


def assemble(after, later, plain, blocks, tails):
    width = blocks[0].shape[2]
    shape = jax.ShapeDtypeStruct((4, 4, 48, width), jnp.bfloat16)
    tail_shape = jax.ShapeDtypeStruct((4, 4, 48, 256), jnp.bfloat16)
    plain, ring, *tail = pl.pallas_call(
        assemble_kernel,
        out_shape=[shape, shape] + [tail_shape] * tails,
        in_specs=[pl.BlockSpec(memory_space=pl.ANY)] * 2
        + [pl.BlockSpec(memory_space=pltpu.VMEM)] * 5,
        out_specs=[pl.BlockSpec(memory_space=pltpu.VMEM)] * (2 + tails),
        compiler_params=pltpu.CompilerParams(vmem_limit_bytes=16 * 1024 * 1024),
        cost_estimate=pl.CostEstimate(flops=0, bytes_accessed=1000, transcendentals=0),
    )(after, later, plain.reshape(4, 4, 48, width), *blocks)
    return plain.reshape(768, width), ring.reshape(768, width), *tail


def dot_nn(left, right):
    return jnp.dot(left, right, preferred_element_type=jnp.float32)


def dot_nt(left, right):
    return lax.dot_general(
        left, right, (((1,), (1,)), ((), ())), preferred_element_type=jnp.float32
    )


def dot_tn(left, right):
    return lax.dot_general(
        left, right, (((0,), (0,)), ((), ())), preferred_element_type=jnp.float32
    )


def three_parts(value):
    high = value.astype(jnp.bfloat16)
    rest = value - high.astype(jnp.float32)
    middle = rest.astype(jnp.bfloat16)
    low = (rest - middle.astype(jnp.float32)).astype(jnp.bfloat16)
    return high, middle, low


def exact_nn(ones, value):
    high, middle, low = three_parts(value)
    return dot_nn(ones, high) + dot_nn(ones, middle) + dot_nn(ones, low)


def gain_rows(ext):
    rows = lax.broadcasted_iota(jnp.int32, (16, 128), 0)
    columns = lax.broadcasted_iota(jnp.int32, (16, 128), 1)
    pick = (columns == rows + 6).astype(jnp.float32).astype(jnp.bfloat16)
    return dot_nt(pick, ext)


def head_mask(rows, head):
    lanes = lax.broadcasted_iota(jnp.int32, (rows, 128), 1)
    return (lanes // 64) == head


def lane_pick(array, lane):
    lanes = lax.broadcasted_iota(jnp.int32, array.shape, 1)
    return jnp.sum(jnp.where(lanes == lane, array, 0.0), axis=1, keepdims=True)


def pair_rms(raw, gain):
    first = head_mask(raw.shape[0], 0)
    square = raw * raw
    sum_first = jnp.sum(jnp.where(first, square, 0.0), axis=1, keepdims=True)
    sum_second = jnp.sum(jnp.where(first, 0.0, square), axis=1, keepdims=True)
    mean = jnp.where(first, sum_first, sum_second) * (1.0 / 64.0)
    scale = lax.rsqrt(mean + epsilon)
    return raw * scale * gain, scale


def gain_pair(ref):
    gain = ref[...].astype(jnp.bfloat16).astype(jnp.float32)
    return jnp.concatenate([gain, gain], axis=1)


def doc_columns(doc_row):
    return jnp.broadcast_to(doc_row, (128, doc_row.shape[1])).T[:, 0:1]


def block_scores(query, keys, decay_col, decay_row, allowed, inv_root):
    raw = dot_nt(query, keys) * inv_root + decay_col - decay_row
    return jnp.where(allowed, raw, -1e30)


def allowed_block(doc_col, doc_row, live_count, start, rows, columns):
    queries = start + lax.broadcasted_iota(jnp.int32, (rows, columns), 0)
    keys = lax.broadcasted_iota(jnp.int32, (rows, columns), 1)
    same = doc_col == doc_row
    return same & (keys <= queries) & ((keys < live_count) | (keys == queries))


def load_halves(refs, held, sems):
    core = lax.rem(lax.axis_index("dp"), 2)
    width = refs[0].shape[1]
    copies = []
    for number, ref in enumerate(refs):
        slot = core if number < 2 else 1 - core
        target = held.at[slot, :, pl.ds((number % 2) * width, width)]
        copies.append(pltpu.make_async_copy(ref, target, sems.at[number]))
    for copy in copies:
        copy.start()
    return core, copies


def attend_kernel(
    live_ref,
    tokens_ref,
    mine_plain_ref,
    mine_ring_ref,
    other_plain_ref,
    other_ring_ref,
    gains_ref,
    bias_ref,
    doc_row_ref,
    normed_ref,
    raw_out,
    heads_out,
    gated_mine_ref,
    gated_other_ref,
    gated_ref,
    lanes_out,
    held,
    sems,
    raw_ref,
    heads_ref,
    lanes_ref,
):
    core, loads = load_halves(
        (mine_plain_ref, mine_ring_ref, other_plain_ref, other_ring_ref), held, sems
    )
    query_raw_ref, key_raw_ref, gate_ref, attended_ref = [raw_ref.at[n] for n in range(4)]
    query_ref, key_ref, value_ref = [heads_ref.at[n] for n in range(3)]
    logit_ref, decay_ref, total_ref = [lanes_ref.at[n] for n in range(3)]
    live_count = live_ref[0]
    inv_root = 0.125
    head_gains = gain_pair(gains_ref)
    doc_row = doc_row_ref[...].astype(jnp.float32)
    doc_col = doc_columns(doc_row)
    hidden = tokens_ref[...].astype(jnp.float32)
    scale = lax.rsqrt(jnp.mean(hidden * hidden, axis=1, keepdims=True) + epsilon)
    for copy in loads:
        copy.wait()
    ext = held[0, :, 768:896]
    gains = gain_rows(ext)
    normed = (hidden * scale * gains[0:1]).astype(jnp.bfloat16)
    normed_ref[...] = normed
    for block in range(3):
        lanes = slice(block * 128, block * 128 + 128)
        query_raw = dot_nn(normed, held[0, :, block * 128 : block * 128 + 128])
        key_raw = dot_nn(normed, held[0, :, 384 + block * 128 : 512 + block * 128])
        query_raw_ref[:, lanes] = query_raw
        key_raw_ref[:, lanes] = key_raw
        query_ref[:, lanes] = pair_rms(query_raw, head_gains[0:1])[0].astype(jnp.bfloat16)
        key_ref[:, lanes] = pair_rms(key_raw, head_gains[1:2])[0].astype(jnp.bfloat16)
    value_ref[...] = dot_nn(normed, held[1, :, 0:384]).astype(jnp.bfloat16)
    gate_ref[...] = dot_nn(normed, held[1, :, 384:768])
    lane = lax.broadcasted_iota(jnp.int32, (384, 128), 1)
    bias = bias_ref[...].astype(jnp.bfloat16).astype(jnp.float32)
    bias = jnp.concatenate([bias, jnp.zeros((1, 122), jnp.float32)], axis=1)
    logit = dot_nn(normed, ext) + bias
    logit = jnp.where(lane < 6, logit, 0.0)
    logit_ref[...] = logit
    log_sig = jnp.minimum(logit, 0.0) - jnp.log1p(jnp.exp(-jnp.abs(logit)))
    rows = lax.broadcasted_iota(jnp.int32, (384, 384), 0)
    columns = lax.broadcasted_iota(jnp.int32, (384, 384), 1)
    lower = (columns <= rows).astype(jnp.float32).astype(jnp.bfloat16)
    decay = exact_nn(lower, log_sig)
    decay_ref[...] = decay
    decay_t = decay.T
    for step in range(3):
        begin, count = step * 128, step * 128 + 128
        allowed = allowed_block(
            doc_col[begin : begin + 128],
            doc_row[:, 0:count],
            live_count,
            begin,
            128,
            count,
        )
        totals = jnp.zeros((128, 128), jnp.float32)
        small_lane = lax.broadcasted_iota(jnp.int32, (128, 128), 1)
        for block in range(3):
            lanes = slice(block * 128, block * 128 + 128)
            keys = key_ref[0:count, lanes]
            values = value_ref[0:count, lanes]
            query_pair = query_ref[begin : begin + 128, lanes]
            outs = []
            for half in range(2):
                head = block * 2 + half
                query = jnp.where(head_mask(128, half), query_pair, jnp.zeros_like(query_pair))
                scores = block_scores(
                    query,
                    keys,
                    lane_pick(decay[begin : begin + 128], head),
                    decay_t[head : head + 1, 0:count],
                    allowed,
                    inv_root,
                )
                peak = jnp.max(scores, axis=1, keepdims=True)
                grown = jnp.exp(scores - peak)
                total = jnp.sum(grown, axis=1, keepdims=True)
                totals = jnp.where(small_lane == head, peak + jnp.log(total), totals)
                probs = (grown * (1.0 / total)).astype(jnp.bfloat16)
                outs.append(dot_nn(probs, values))
            attended_ref[begin : begin + 128, lanes] = jnp.where(
                head_mask(128, 0), outs[0], outs[1]
            )
        total_ref[begin : begin + 128, :] = totals
    copies = [
        pltpu.make_async_copy(
            source, target.at[pl.ds(0, source.shape[0])], sems.at[4 + number]
        )
        for number, (source, target) in enumerate(
            ((raw_ref, raw_out), (heads_ref, heads_out), (lanes_ref, lanes_out))
        )
    ]
    for copy in copies:
        copy.start()
    gated = (attended_ref[...] * jax.nn.sigmoid(gate_ref[...])).astype(jnp.bfloat16)
    gated_mine_ref[...] = jnp.where(core == 0, gated[:, 0:256], gated[:, 128:384])
    gated_other_ref[...] = jnp.where(core == 0, gated[:, 128:384], gated[:, 0:256])
    gated_ref[...] = gated
    for copy in copies:
        copy.wait()


def mlp_kernel(
    live_ref,
    tokens_ref,
    gated_ref,
    gated_peer_ref,
    cotangent_ref,
    ext_ref,
    mine_plain_ref,
    mine_ring_ref,
    other_plain_ref,
    other_ring_ref,
    near_mine_ref,
    near_other_ref,
    far_mine_ref,
    far_other_ref,
    middle_ref,
    normed_ref,
    hidden_mine_ref,
    hidden_other_ref,
    out_ref,
    grad_ref,
    held,
    sems,
    out_held,
):
    core, loads = load_halves(
        (mine_plain_ref, mine_ring_ref, other_plain_ref, other_ring_ref), held, sems
    )
    out_loads = []
    for number, ref in enumerate((near_mine_ref, near_other_ref, far_mine_ref, far_other_ref)):
        slot = (number // 2) * 2 + (core if number % 2 == 0 else 1 - core)
        source = ref.at[:, pl.ds(ref.shape[1] - 256, 256)]
        out_loads.append(pltpu.make_async_copy(source, out_held.at[slot], sems.at[4 + number]))
    for copy in out_loads:
        copy.start()
    for copy in out_loads:
        copy.wait()
    parts = []
    for number, ref in enumerate((gated_ref, gated_peer_ref)):
        part = dot_nt(ref[:, 0:128], out_held[2 * number, :, 128:256])
        parts.append(part + dot_nt(ref[:, 128:384], out_held[2 * number + 1]))
    middle = tokens_ref[...].astype(jnp.float32) + (parts[0] + parts[1])
    middle_ref[...] = middle
    gains = gain_rows(ext_ref[...])
    scale = lax.rsqrt(jnp.mean(middle * middle, axis=1, keepdims=True) + epsilon)
    normed = (middle * scale * gains[1:2]).astype(jnp.bfloat16)
    normed_ref[...] = normed
    live_rows = lax.broadcasted_iota(jnp.int32, (384, 1), 0) < live_ref[0]
    grad_out = jnp.where(live_rows, cotangent_ref[...].astype(jnp.float32), 0.0)
    grad_out = grad_out.astype(jnp.bfloat16)
    for copy in loads:
        copy.wait()
    out_total = jnp.zeros((384, 768), jnp.float32)
    grad_total = jnp.zeros((384, 768), jnp.float32)
    parts = []
    for half in range(2):
        begin = half * 512
        gate_w = held[0, :, begin : begin + 512]
        up_w = held[1, :, begin : begin + 512]
        down_w = held[half, :, 1024:1536]
        gate = dot_nn(normed, gate_w)
        up = dot_nn(normed, up_w)
        sig = jax.nn.sigmoid(gate)
        silu = gate * sig
        active = (silu * up).astype(jnp.bfloat16)
        out_total = out_total + dot_nt(active, down_w)
        grad_act = dot_nn(grad_out, down_w)
        grad_up = (grad_act * silu).astype(jnp.bfloat16)
        grad_gate = (grad_act * up * (sig * (1.0 + gate * (1.0 - sig)))).astype(jnp.bfloat16)
        parts.append((grad_gate, grad_up, active))
        grad_total = grad_total + dot_nt(grad_gate, gate_w) + dot_nt(grad_up, up_w)
    for number in range(3):
        lanes = slice(number * 512, number * 512 + 512)
        first, second = parts[0][number], parts[1][number]
        hidden_mine_ref[:, lanes] = jnp.where(core == 0, first, second)
        hidden_other_ref[:, lanes] = jnp.where(core == 0, second, first)
    out_ref[...] = out_total.astype(jnp.bfloat16)
    grad_ref[...] = grad_total.astype(jnp.bfloat16)


def attend_back_kernel(
    after_ref,
    live_ref,
    tokens_ref,
    cotangent_ref,
    middle_ref,
    part_ref,
    peer_ref,
    mine_plain_ref,
    mine_ring_ref,
    other_plain_ref,
    other_ring_ref,
    gains_ref,
    doc_row_ref,
    normed_ref,
    raw_in,
    heads_in,
    lanes_in,
    grad_middle_ref,
    grad_middle_b_ref,
    proj_mine_ref,
    proj_other_ref,
    norm_part_ref,
    extra_ref,
    held,
    sems,
    grad_att_ref,
    grad_query_ref,
    grad_key_ref,
    grad_value_ref,
    grad_og_ref,
    column_ref,
    raw_ref,
    heads_ref,
    lanes_ref,
    settle,
):
    core, loads = load_halves(
        (mine_plain_ref, mine_ring_ref, other_plain_ref, other_ring_ref), held, sems
    )
    settle()
    copies = [
        pltpu.make_async_copy(
            source.at[pl.ds(0, target.shape[0])], target, sems.at[4 + number]
        )
        for number, (source, target) in enumerate(
            ((raw_in, raw_ref), (heads_in, heads_ref), (lanes_in, lanes_ref))
        )
    ]
    for copy in copies:
        copy.start()
    query_raw_ref, key_raw_ref, gate_ref, attended_ref = [raw_ref.at[n] for n in range(4)]
    query_ref, key_ref, value_ref = [heads_ref.at[n] for n in range(3)]
    logit_ref, decay_ref, total_ref = [lanes_ref.at[n] for n in range(3)]
    live_count = live_ref[0]
    inv_root = 0.125
    head_gains = gain_pair(gains_ref)
    doc_row = doc_row_ref[...].astype(jnp.float32)
    doc_col = doc_columns(doc_row)
    middle = middle_ref[...]
    grad_normed = part_ref[...].astype(jnp.float32)
    grad_normed = grad_normed + peer_ref[...].astype(jnp.float32)
    live_rows = lax.broadcasted_iota(jnp.int32, (384, 1), 0) < live_count
    grad_out = jnp.where(live_rows, cotangent_ref[...].astype(jnp.float32), 0.0)
    scale = lax.rsqrt(jnp.mean(middle * middle, axis=1, keepdims=True) + epsilon)
    for copy in loads:
        copy.wait()
    ext = held[0, :, 768:896]
    gains = gain_rows(ext)
    gained = grad_normed * gains[1:2]
    inner = jnp.mean(gained * middle, axis=1, keepdims=True)
    grad_middle = grad_out + (scale * gained - middle * (scale * scale * scale * inner))
    grad_gain = jnp.sum(grad_normed * middle * scale, axis=0, keepdims=True)
    grad_middle_ref[...] = grad_middle
    grad_middle_b = grad_middle.astype(jnp.bfloat16)
    grad_middle_b_ref[...] = grad_middle_b
    grad_gated = jnp.concatenate(
        [
            dot_nn(grad_middle_b, held[0, :, 896:1024]),
            dot_nn(grad_middle_b, held[1, :, 768:1024]),
        ],
        axis=1,
    )
    for copy in copies:
        copy.wait()
    sig = jax.nn.sigmoid(gate_ref[...])
    grad_att_ref[...] = (grad_gated * sig).astype(jnp.bfloat16)
    grad_og = (grad_gated * attended_ref[...] * sig * (1.0 - sig)).astype(jnp.bfloat16)
    grad_og_ref[...] = grad_og
    grad_key_ref[...] = jnp.zeros((384, 384), jnp.float32)
    grad_value_ref[...] = jnp.zeros((384, 384), jnp.float32)
    column_ref[...] = jnp.zeros((128, 384), jnp.float32)
    decay = decay_ref[...]
    decay_t = decay.T
    row_parts = []
    for step in range(3):
        begin, count = step * 128, step * 128 + 128
        allowed = allowed_block(
            doc_col[begin : begin + 128],
            doc_row[:, 0:count],
            live_count,
            begin,
            128,
            count,
        )
        small_lane = lax.broadcasted_iota(jnp.int32, (128, 128), 1)
        row_sums = jnp.zeros((128, 128), jnp.float32)
        for block in range(3):
            lanes = slice(block * 128, block * 128 + 128)
            keys = key_ref[0:count, lanes]
            values = value_ref[0:count, lanes]
            query_pair = query_ref[begin : begin + 128, lanes]
            att_pair = grad_att_ref[begin : begin + 128, lanes]
            outs = []
            key_outs = []
            value_outs = []
            for half in range(2):
                head = block * 2 + half
                mask = head_mask(128, half)
                query = jnp.where(mask, query_pair, jnp.zeros_like(query_pair))
                att = jnp.where(mask, att_pair, jnp.zeros_like(att_pair))
                scores = block_scores(
                    query,
                    keys,
                    lane_pick(decay[begin : begin + 128], head),
                    decay_t[head : head + 1, 0:count],
                    allowed,
                    inv_root,
                )
                probs = jnp.exp(scores - lane_pick(total_ref[begin : begin + 128, :], head))
                grad_probs = dot_nt(att, values)
                row_dot = jnp.sum(probs * grad_probs, axis=1, keepdims=True)
                grad_scores = (probs * (grad_probs - row_dot)).astype(jnp.bfloat16)
                grad_scores_f = grad_scores.astype(jnp.float32)
                row_sums = jnp.where(
                    small_lane == head,
                    jnp.sum(grad_scores_f, axis=1, keepdims=True),
                    row_sums,
                )
                column_ref[head : head + 1, 0:count] += jnp.sum(
                    grad_scores_f, axis=0, keepdims=True
                )
                outs.append(dot_nn(grad_scores, keys))
                key_outs.append(dot_tn(grad_scores, query))
                value_outs.append(dot_tn(probs.astype(jnp.bfloat16), att))
            grad_query_ref[begin : begin + 128, lanes] = jnp.where(
                head_mask(128, 0), outs[0], outs[1]
            )
            grad_key_ref[0:count, lanes] += key_outs[0] + key_outs[1]
            grad_value_ref[0:count, lanes] += value_outs[0] + value_outs[1]
        row_parts.append(row_sums)
    grad_decay = jnp.concatenate(row_parts, axis=0) - column_ref[...].T
    rows = lax.broadcasted_iota(jnp.int32, (384, 384), 0)
    columns = lax.broadcasted_iota(jnp.int32, (384, 384), 1)
    upper = (columns >= rows).astype(jnp.float32).astype(jnp.bfloat16)
    grad_logit = exact_nn(upper, grad_decay) * jax.nn.sigmoid(-logit_ref[...])
    lane = lax.broadcasted_iota(jnp.int32, (384, 128), 1)
    grad_logit = jnp.where(lane < 6, grad_logit, 0.0)
    grad_forget = grad_logit.astype(jnp.bfloat16)
    grad_vg = jnp.concatenate([grad_value_ref[...].astype(jnp.bfloat16), grad_og_ref[...]], axis=1)
    grad_qk = []
    gain_sums = []
    for number, raw_ref, out_ref in (
        (0, query_raw_ref, grad_query_ref),
        (1, key_raw_ref, grad_key_ref),
    ):
        gain = head_gains[number : number + 1]
        gain_sum = jnp.zeros((1, 128), jnp.float32)
        for block in range(3):
            lanes = slice(block * 128, block * 128 + 128)
            raw = raw_ref[:, lanes]
            grad = (out_ref[:, lanes] * inv_root).astype(jnp.bfloat16).astype(jnp.float32)
            first = head_mask(384, 0)
            scaled = pair_rms(raw, 1.0)[1]
            weighted = grad * gain
            product = weighted * raw
            sum_first = jnp.sum(jnp.where(first, product, 0.0), axis=1, keepdims=True)
            sum_second = jnp.sum(jnp.where(first, 0.0, product), axis=1, keepdims=True)
            inner_head = jnp.where(first, sum_first, sum_second) * (1.0 / 64.0)
            gain_sum = gain_sum + jnp.sum(grad * raw * scaled, axis=0, keepdims=True)
            grad_raw = scaled * weighted - raw * (scaled * scaled * scaled * inner_head)
            grad_qk.append(grad_raw.astype(jnp.bfloat16))
        gain_sums.append(gain_sum)
    grad_qk = jnp.concatenate(grad_qk, axis=1)
    proj_mine_ref[...] = jnp.where(core == 0, grad_qk, grad_vg)
    proj_other_ref[...] = jnp.where(core == 0, grad_vg, grad_qk)
    part = dot_nt(grad_qk, held[0, :, 0:768])
    part = part + dot_nt(grad_vg, held[1, :, 0:768])
    part = part + dot_nt(grad_forget, ext)
    norm_part_ref[...] = part.astype(jnp.bfloat16)
    hidden = tokens_ref[...].astype(jnp.float32)
    scale = lax.rsqrt(jnp.mean(hidden * hidden, axis=1, keepdims=True) + epsilon)
    first_gain = jnp.sum(part * (hidden * scale), axis=0, keepdims=True)
    line = lax.broadcasted_iota(jnp.int32, (128, 768), 0)
    extra = jnp.where(line == 6, first_gain, jnp.where(line == 7, grad_gain, 0.0)).T
    extra = extra + dot_tn(normed_ref[...], grad_forget)
    bias_sum = jnp.sum(grad_forget.astype(jnp.float32), axis=0, keepdims=True)
    sums = [total + pltpu.roll(total, 64, 1) for total in (gain_sums[0], gain_sums[1], bias_sum)]
    line = lax.rem(lax.broadcasted_iota(jnp.int32, (768, 128), 0), 12)
    lane = lax.broadcasted_iota(jnp.int32, (768, 128), 1)
    for number in range(3):
        extra = jnp.where((line == number) & (lane >= 64), sums[number], extra)
    extra_ref[...] = extra.astype(jnp.bfloat16)


def wide_grad_kernel(*refs):
    normed, normed_peer, hidden, hidden_peer, grad, grad_peer, out_ref = refs
    for begin in range(0, 1536, 256):
        lanes = slice(begin, begin + 256)
        left, left_peer = (normed, normed_peer) if begin < 1024 else (grad, grad_peer)
        total = dot_tn(left[...], hidden[:, lanes]) + dot_tn(left_peer[...], hidden_peer[:, lanes])
        out_ref[:, lanes] = total.astype(jnp.bfloat16)


def proj_grad_kernel(after_ref, *refs):
    first, first_peer, left, left_peer, second, second_peer, right, right_peer = refs[:8]
    extra_ref, out_ref = refs[8], refs[9]
    out_ref[:, 1024:1152] = extra_ref[...]
    for begin in range(0, 1024, 256):
        if begin < 768:
            lanes = slice(begin, begin + 256)
            total = dot_tn(first[...], left[:, lanes])
            total = total + dot_tn(first_peer[...], left_peer[:, lanes])
        else:
            total = dot_tn(second[...], right[...]) + dot_tn(second_peer[...], right_peer[...])
        out_ref[:, begin : begin + 256] = total.astype(jnp.bfloat16)


def mirror(out_ref, block, start):
    out_ref[start : start + 256, start:768] = block.astype(jnp.bfloat16)
    for other in range(start + 256, 768, 256):
        piece = block[:, other - start : other - start + 256]
        out_ref[other : other + 256, start : start + 256] = piece.T.astype(jnp.bfloat16)


def plane_sum_kernel(*refs):
    blocks_ref, mine_ref, other_ref = refs[-3:]
    level = lax.rem(lax.axis_index("dp") // 2, 2)
    for start in range(0, blocks_ref.shape[2], 256):
        lanes = slice(start, start + 256)
        total = blocks_ref[0, :, lanes].astype(jnp.float32)
        for number in range(1, 16):
            total = total + blocks_ref[number, :, lanes].astype(jnp.float32)
        first, second = total[0:24], total[24:48]
        mine_ref[:, lanes] = jnp.where(level == 0, first, second)
        other_ref[:, lanes] = jnp.where(level == 0, second, first)


def momentum_kernel(
    mine_ref,
    other_ref,
    old_ref,
    tokens_ref,
    grad_middle_ref,
    norm_part_ref,
    norm_peer_ref,
    ext_ref,
    middle_ref,
    mlp_part_ref,
    mlp_peer_ref,
    new_ref,
    keep_ref,
    send_ref,
    small_ref,
    input_grad_ref,
    result_ref,
):
    place = lax.axis_index("dp")
    core, level = lax.rem(place, 2), lax.rem(place // 2, 2)
    mine, other = mine_ref[...], other_ref[...]
    even = jnp.where(core == 0, mine, other)
    odd = jnp.where(core == 0, other, mine)
    small_ref[...] = mine[:, 1024:1152] + other[:, 1024:1152]
    fresh = [even[:, 0:384], even[:, 384:768], odd[:, 0:384], odd[:, 384:768]]
    fresh.append(jnp.concatenate([even[:, 768:1024], odd[:, 896:1024]], axis=1))
    fresh = [muon_decay * old_ref[number] + fresh[number] for number in range(5)]
    for number in range(5):
        new_ref[number] = fresh[number]
    for number in range(4):
        keep_ref[number] = jnp.where(level == 0, fresh[4], fresh[number])
        send_ref[number] = jnp.where(level == 0, fresh[number], fresh[4])
    hidden = tokens_ref[...].astype(jnp.float32)
    gain = gain_rows(ext_ref[...])[0:1]
    added = mlp_part_ref[...].astype(jnp.float32) + mlp_peer_ref[...].astype(jnp.float32)
    result_ref[...] = (middle_ref[...] + added).astype(jnp.bfloat16)
    grad = norm_part_ref[...].astype(jnp.float32) + norm_peer_ref[...].astype(jnp.float32)
    scale = lax.rsqrt(jnp.mean(hidden * hidden, axis=1, keepdims=True) + epsilon)
    gained = grad * gain
    inner = jnp.mean(gained * hidden, axis=1, keepdims=True)
    input_grad_ref[...] = grad_middle_ref[...] + (
        scale * gained - hidden * (scale * scale * scale * inner)
    )


def small_kernel(
    mine_ref,
    peer_ref,
    norm_ref,
    qk_ref,
    forget_ref,
    bias_ref,
    m_norm_ref,
    m_qk_ref,
    m_forget_ref,
    m_bias_ref,
    after_ref,
    new_norm_ref,
    new_qk_ref,
    new_forget_ref,
    new_bias_ref,
    mom_norm_ref,
    mom_qk_ref,
    mom_forget_ref,
    mom_bias_ref,
):
    root_tokens = math.sqrt(24576.0)
    mine, both = mine_ref[...], mine_ref[...] + peer_ref[...]
    lane = lax.broadcasted_iota(jnp.int32, (12, 128), 1)
    norms = jnp.where(lane == 6, both, mine).T
    grads = (
        (norms[6:8, :], gain_rate, norm_ref, m_norm_ref, new_norm_ref, mom_norm_ref),
        (both[0:2, 64:128], qk_rate, qk_ref, m_qk_ref, new_qk_ref, mom_qk_ref),
        (mine[:, 0:6], forget_rate, forget_ref, m_forget_ref, new_forget_ref, mom_forget_ref),
        (mine[2:3, 64:70], bias_rate, bias_ref, m_bias_ref, new_bias_ref, mom_bias_ref),
    )
    for grad, rate, value_ref, old_ref, new_ref, mom_ref in grads:
        moment = plain_decay * old_ref[...] + grad
        mom_ref[...] = moment
        new_ref[...] = value_ref[...] - (rate / root_tokens) * moment


def newton_body(columns, out_ref, held, square_ref, poly_ref, raw_ref):
    sides, width = held.shape[1], held.shape[3]
    scale = None
    for repeat in range(5):
        now, later = repeat % 2, (repeat + 1) % 2
        trace = jnp.zeros((1, 1), jnp.float32)
        for start in range(0, 768, 256):
            rows, right = slice(start, start + 256), slice(start, 768)
            square = dot_nt(held[now, 0, rows, :], held[now, 0, right, :])
            for side in range(1, sides):
                square = square + dot_nt(held[now, side, rows, :], held[now, side, right, :])
            if repeat > 0:
                mirror(square_ref, square, start)
            else:
                raw_ref[rows, right] = square
                block = square[:, 0:256]
                eye = lax.broadcasted_iota(jnp.int32, (256, 256), 0)
                eye = eye == lax.broadcasted_iota(jnp.int32, (256, 256), 1)
                line = jnp.sum(jnp.where(eye, block, 0.0), axis=0, keepdims=True)
                trace = trace + jnp.sum(line, axis=1, keepdims=True)
        if repeat == 0:
            scale = 1.0 / (jnp.sqrt(trace) + 1e-07)
            for start in range(0, 768, 256):
                square = raw_ref[start : start + 256, start:768]
                mirror(square_ref, square * scale * scale, start)
        if repeat < 4:
            for start in range(0, 768, 256):
                rows, right = slice(start, start + 256), slice(start, 768)
                poly = coef_b * square_ref[rows, right].astype(jnp.float32)
                poly = poly + coef_c * dot_nn(square_ref[rows, :], square_ref[:, right])
                mirror(poly_ref, poly, start)
            for side in range(sides):
                for start in range(0, 768, 256):
                    grown = coef_a * held[now, side, start : start + 256, :].astype(jnp.float32)
                    grown = grown + dot_nn(poly_ref[start : start + 256, :], held[now, side])
                    if repeat == 0:
                        grown = grown * scale
                    held[later, side, start : start + 256, :] = grown.astype(jnp.bfloat16)
        else:
            half = lax.axis_index("tensor")
            side, first = (half, 0) if sides == 2 else (0, pl.multiple_of(half * columns, 128))
            begin = pl.multiple_of((lax.axis_index("dp") // 16) * 96, 16)
            few = square_ref[pl.ds(begin, 96), :]
            poly = coef_b * few.astype(jnp.float32) + coef_c * dot_nn(few, square_ref[...])
            poly = poly.astype(jnp.bfloat16)
            grown = held[now, side, pl.ds(begin, 96), pl.ds(first, columns)].astype(jnp.float32)
            grown = coef_a * grown + dot_nn(poly, held[now, side, :, pl.ds(first, columns)])
            out_ref[...] = grown.astype(jnp.bfloat16)


def newton_kernel(wants_wide, after_ref, mine_any, other_any, out_ref, *scratch):
    place = lax.axis_index("dp")
    is_wide = (lax.rem(place // 2, 2) == 0) & (lax.rem(place // 4, 4) < 3)
    active = is_wide if wants_wide else jnp.logical_not(is_wide)

    @pl.when(active)
    def run():
        held, sems = scratch[0], scratch[4]
        columns, width = mine_any.shape[2], held.shape[3]
        loads = []
        for number in range(4):
            source = (mine_any, other_any)[number // 2].at[number % 2]
            first = (number % 2) * columns
            target = held.at[
                0, first // width, pl.ds((number // 2) * 384, 384), pl.ds(first % width, columns)
            ]
            loads.append(pltpu.make_async_copy(source, target, sems.at[number]))
        for copy in loads:
            copy.start()
        for copy in loads:
            copy.wait()
        newton_body(columns, out_ref, *scratch[:4])

    @pl.when(jnp.logical_not(active))
    def skip():
        out_ref[...] = jnp.zeros(out_ref.shape, jnp.bfloat16)


in_vmem = pl.BlockSpec(memory_space=pltpu.VMEM)
in_smem = pl.BlockSpec(memory_space=pltpu.SMEM)
in_any = pl.BlockSpec(memory_space=pl.ANY)
in_hbm = pl.BlockSpec(memory_space=pltpu.HBM)


def call_kernel(kernel, in_specs, outs, scratch, flops, limit=24, far=(), staged=False):
    near = [number for number in range(len(outs)) if number not in far]
    moved = [number for number, spec in enumerate(in_specs) if spec is in_vmem]
    count = len(in_specs) + len(outs) + len(scratch)

    def staged_kernel(*refs):
        refs, buffers = list(refs[:count]), refs[count:]
        sems = buffers[-1]
        loads = []
        for slot, number in enumerate(moved):
            loads.append(pltpu.make_async_copy(refs[number], buffers[slot], sems.at[slot]))
            refs[number] = buffers[slot]
        for copy in loads:
            copy.start()
        stores = []
        for slot, number in enumerate(near):
            place, slot = len(in_specs) + number, len(moved) + slot
            stores.append(pltpu.make_async_copy(buffers[slot], refs[place], sems.at[slot]))
            refs[place] = buffers[slot]

        def settle():
            for copy in loads:
                copy.wait()

        kernel(*refs, settle=settle)
        for copy in stores:
            copy.start()
        for copy in stores:
            copy.wait()

    def run(*operands):
        buffers = []
        if staged:
            buffers = [pltpu.VMEM(operands[n].shape, operands[n].dtype) for n in moved]
            buffers += [pltpu.VMEM(*outs[n]) for n in near]
            buffers.append(pltpu.SemaphoreType.DMA((len(buffers),)))
        out_specs = [in_hbm if staged or n in far else in_vmem for n in range(len(outs))]
        return pl.pallas_call(
            staged_kernel if staged else kernel,
            out_shape=[jax.ShapeDtypeStruct(shape, dtype) for shape, dtype in outs],
            in_specs=[in_any if staged and spec is in_vmem else spec for spec in in_specs],
            out_specs=out_specs,
            scratch_shapes=list(scratch) + buffers,
            compiler_params=pltpu.CompilerParams(vmem_limit_bytes=limit * 1024 * 1024),
            cost_estimate=pl.CostEstimate(flops=flops, bytes_accessed=1000, transcendentals=0),
        )(*operands)

    return run


def newton(wants_wide, after, mine, other):
    columns = mine.shape[2]
    return call_kernel(
        functools.partial(newton_kernel, wants_wide),
        [in_any] * 3,
        [((96, columns), jnp.bfloat16)],
        [
            pltpu.VMEM((2, 2 * columns // max(columns, 768), 768, max(columns, 768)), jnp.bfloat16),
            pltpu.VMEM((768, 768), jnp.bfloat16),
            pltpu.VMEM((768, 768), jnp.bfloat16),
            pltpu.VMEM((768, 768), jnp.float32),
            pltpu.SemaphoreType.DMA((4,)),
        ],
        200000000000 if wants_wide else 1000,
    )(after, mine.reshape(2, 384, columns), other.reshape(2, 384, columns))[0]


def spread_slots(slots_b):
    column = place_of("x")

    def slot(step):
        number = jnp.minimum((column + step) % 4, slots_b.shape[0] - 1)
        return lax.dynamic_index_in_dim(slots_b, number, 0, keepdims=False)

    pieces = [slot(0)] + [fetch(slot(4 - step), "x", step) for step in (1, 2, 3)]
    return jnp.concatenate(pieces, axis=0)


def ring_order(rows, count):
    column = place_of("x")
    blocks = rows.reshape(4, 24, count)
    return jnp.stack(
        [lax.dynamic_index_in_dim(blocks, (n - column) % 4, 0, False) for n in range(4)]
    )


def on_device(
    tokens,
    cotangent,
    segment_ids,
    live_len,
    w_square,
    w_wide,
    norm_gain,
    qk_gain,
    forget_w,
    forget_b,
    m_square,
    m_wide,
    m_norm,
    m_qk,
    m_forget_w,
    m_forget_b,
    ema_square,
    ema_wide,
):
    half_width = w_square.shape[2]
    half_hidden = w_wide.shape[2]
    shard_rows = w_square.shape[1]
    head_local = forget_w.shape[1]
    head_dim = qk_gain.shape[1]
    dp_size = lax.axis_size("dp")
    full_width = shard_rows * dp_size
    full_hidden = half_hidden * lax.axis_size("tensor")
    my_place = lax.axis_index("dp")
    core = my_place % 2
    quarter_hidden = half_hidden // 2
    bf16, f32 = jnp.bfloat16, jnp.float32

    pack_mine, pack_other = call_kernel(
        pack_kernel, [in_vmem] * 4, [((shard_rows, 2560), bf16)] * 2, [], 1000, 8
    )(w_square, w_wide, norm_gain, forget_w)
    pair_rows = pair_join(core, pack_mine, core_swap(pack_other), 0)
    ring_rows = pair_rows[:, 1280:]
    ring_rows = pair_join(place_of("l"), ring_rows, fetch(ring_rows, "l", 1), 0)
    row_plane = exchange(spread_rows(ring_rows, pair_rows[:, :1280]), ("x", "l"))
    row_plane = row_plane.reshape(4, 48, 1280)
    blocks_y = fetch_ring(ring_rows, "y")

    def both_cores(after, later, plain, blocks, tails=0):
        plain, ring, *tail = assemble(after, later, plain, blocks, tails)
        return (plain, ring, core_swap(plain), core_swap(ring)), tail

    spread, stack = prepare(0, 512, pair_rows, row_plane, blocks_y)
    first_plane, first_blocks = exchange(spread, ("y",)), fetch_ring(stack, "x")
    first_weights, (out_tail,) = both_cores(pair_rows, pair_rows, first_plane, first_blocks, 1)
    out_tail = out_tail.reshape(768, 256)
    spread, stack = prepare(512, 768, first_weights[1], row_plane, blocks_y)
    late_plane, late_blocks = exchange(spread, ("y",)), fetch_ring(stack, "x")
    far_tail = tensor_swap(out_tail)
    far_tail_other = core_swap(far_tail)
    ext = by_core(core, first_weights[1][:, 256:384], first_weights[3][:, 256:384])

    bias_row = forget_b[None]
    live_mask = (jnp.arange(tokens.shape[0]) < live_len[0])[:, None]
    grad_out_b = jnp.where(live_mask, cotangent, jnp.zeros_like(cotangent))

    def paired(mine, other):
        return mine, core_swap(other)

    token_h = ((384, 768), bf16)
    token_f = ((384, 768), f32)
    (
        normed_one,
        raw,
        heads,
        gated_mine,
        gated_other,
        gated,
        head_lanes,
    ) = call_kernel(
        attend_kernel,
        [in_smem, in_vmem] + [in_any] * 4 + [in_vmem] * 3,
        [token_h, ((48, 384, 384), f32), ((100, 384, 384), bf16)]
        + [((384, 256), bf16)] * 2
        + [((384, 384), bf16), ((150, 384, 128), f32)],
        [
            pltpu.VMEM((2, 768, 1024), bf16),
            pltpu.SemaphoreType.DMA((7,)),
            pltpu.VMEM((4, 384, 384), f32),
            pltpu.VMEM((3, 384, 384), bf16),
            pltpu.VMEM((3, 384, 128), f32),
        ],
        1000,
        24,
        (1, 2, 6),
    )(live_len, tokens, *first_weights, qk_gain, bias_row, segment_ids)
    second_weights = both_cores(
        core_swap(gated[:16, :128]), far_tail, late_plane, late_blocks
    )[0]
    normed_one_pair = paired(normed_one, normed_one)
    gated_pair = paired(gated_mine, gated_other)
    grad_out_pair = paired(grad_out_b, grad_out_b)
    middle, normed_two, hidden_mine, hidden_other, mlp_part, grad_part = call_kernel(
        mlp_kernel,
        [in_smem] + [in_vmem] * 5 + [in_any] * 8,
        [token_f, token_h, ((384, 1536), bf16), ((384, 1536), bf16), token_h, token_h],
        [
            pltpu.VMEM((2, 768, 1536), bf16),
            pltpu.SemaphoreType.DMA((8,)),
            pltpu.VMEM((4, 768, 256), bf16),
        ],
        1000,
        24,
    )(
        live_len,
        tokens,
        gated,
        tensor_swap(gated),
        cotangent,
        ext,
        *second_weights,
        first_weights[1],
        first_weights[3],
        far_tail,
        far_tail_other,
    )
    grad_peer = tensor_swap(grad_part)

    normed_two_pair = paired(normed_two, normed_two)
    hidden_pair = paired(hidden_mine, hidden_other)
    grad_wide_b = call_kernel(
        wide_grad_kernel,
        [in_vmem] * 6,
        [((768, 1536), bf16)],
        [],
        1000,
        24,
    )(*normed_two_pair, *hidden_pair, *grad_out_pair)[0]
    level = place_of("l")
    wide_blocks = exchange(grad_wide_b.reshape(16, 48, 3 * quarter_hidden), ("y", "x"))

    (
        grad_middle,
        grad_middle_b,
        proj_mine,
        proj_other,
        norm_part,
        extra,
    ) = call_kernel(
        attend_back_kernel,
        [in_any, in_smem] + [in_vmem] * 5 + [in_any] * 4 + [in_vmem] * 3 + [in_hbm] * 3,
        [token_f, token_h, token_h, token_h, token_h, ((768, 128), bf16)],
        [
            pltpu.VMEM((2, 768, 1024), bf16),
            pltpu.SemaphoreType.DMA((7,)),
            pltpu.VMEM((384, 384), bf16),
            pltpu.VMEM((384, 384), f32),
            pltpu.VMEM((384, 384), f32),
            pltpu.VMEM((384, 384), f32),
            pltpu.VMEM((384, 384), bf16),
            pltpu.VMEM((128, 384), f32),
            pltpu.VMEM((4, 384, 384), f32),
            pltpu.VMEM((3, 384, 384), bf16),
            pltpu.VMEM((3, 384, 128), f32),
        ],
        100000000000,
        56,
        staged=True,
    )(
        grad_wide_b,
        live_len,
        tokens,
        cotangent,
        middle,
        grad_part,
        grad_peer,
        *first_weights,
        qk_gain,
        segment_ids,
        normed_one,
        raw,
        heads,
        head_lanes,
    )
    proj_pair = paired(proj_mine, proj_other)
    grad_middle_pair = paired(grad_middle_b, grad_middle_b)
    mlp_peer = tensor_swap(mlp_part)
    grad_proj_b = call_kernel(
        proj_grad_kernel,
        [in_any] + [in_vmem] * 9,
        [((768, 1152), bf16)],
        [],
        1000,
        24,
    )(
        mlp_peer,
        *normed_one_pair,
        *proj_pair,
        *grad_middle_pair,
        *gated_pair,
        extra,
    )[0]
    norm_peer = tensor_swap(norm_part)
    mine, other = call_kernel(
        plane_sum_kernel,
        [in_any] * 2 + [in_vmem],
        [((24, 3 * quarter_hidden), f32)] * 2,
        [],
        1000,
    )(grad_proj_b, norm_peer, wide_blocks)
    other = other.astype(bf16)
    mine, other = pair_split(core, mine + fetch(other, "l", 1).astype(f32), 0)
    other = core_swap(other)
    wide_shard = jnp.stack(
        [
            pair_join(core, mine[:, start : start + 512], other[:, start : start + 512], 1)
            for start in (0, 512, 1024)
        ]
    )
    mom_wide = muon_decay * m_wide + wide_shard

    wide_slots = mom_wide.astype(bf16)
    wide_pair = jnp.concatenate([wide_slots, fetch(wide_slots, "l", 1)], axis=1)
    wide_rows = spread_slots(wide_pair)
    proj_blocks = exchange(grad_proj_b.reshape(32, 24, 1152), ("y", "x", "l"))
    proj_blocks, wide_rows = lax.optimization_barrier((proj_blocks, wide_rows))
    wide_own = gather(wide_rows, ("t", "y"))
    mine, other = pair_split(core, jnp.sum(proj_blocks.astype(f32), axis=0), 0)
    other = core_swap(other)
    mom_square, keep_slots, send_slots, small, input_grad, result = call_kernel(
        momentum_kernel,
        [in_vmem] * 11,
        [
            ((5, 12, half_width), f32),
            ((4, 12, half_width), f32),
            ((4, 12, half_width), f32),
            ((12, 128), f32),
            token_f,
            token_h,
        ],
        [],
        1000,
        24,
    )(
        mine,
        other,
        m_square,
        tokens,
        grad_middle,
        norm_part,
        norm_peer,
        ext,
        middle,
        mlp_part,
        mlp_peer,
    )
    keep_slots, send_slots = keep_slots.astype(bf16), send_slots.astype(bf16)
    proj_rows = spread_slots(pair_join(level, keep_slots, fetch(send_slots, "l", 1), 1))
    wide_own, proj_rows = lax.optimization_barrier((wide_own, proj_rows))
    wide_other = core_swap(wide_own)
    proj_own = gather(proj_rows, ("t", "y"))
    wide_rows = newton(True, small, wide_own, wide_other)
    proj_own, wide_rows = lax.optimization_barrier((proj_own, wide_rows))
    proj_rows = newton(False, wide_rows, proj_own, core_swap(proj_own))
    proj_rows = jnp.pad(proj_rows, ((0, 0), (0, half_hidden - half_width)))
    rows = ring_order(proj_rows + wide_rows, half_hidden).reshape(8, 12, half_hidden)
    update = exchange(rows, ("x", "l")).astype(f32)
    update_wide = update[0:6:2]
    update_square = jnp.concatenate([update[1::2], update[6:7]], axis=0)[:, :, :half_width]

    small_peer = tensor_swap(small)
    (
        new_norm,
        new_qk,
        new_forget_w,
        new_forget_b,
        mom_norm,
        mom_qk,
        mom_forget_w,
        mom_forget_b,
    ) = call_kernel(
        small_kernel,
        [in_vmem] * 10 + [in_any],
        [(value.shape, f32) for value in (norm_gain, qk_gain, forget_w)]
        + [((1, head_local), f32)]
        + [(value.shape, f32) for value in (norm_gain, qk_gain, forget_w)]
        + [((1, head_local), f32)],
        [],
        1000,
        16,
    )(
        small,
        small_peer,
        norm_gain,
        qk_gain,
        forget_w,
        forget_b[None],
        m_norm,
        m_qk,
        m_forget_w,
        m_forget_b[None],
        proj_rows,
    )
    new_forget_b, mom_forget_b = new_forget_b[0], mom_forget_b[0]
    new_square = w_square - update_square
    new_wide = w_wide - math.sqrt(full_hidden / full_width) * update_wide
    new_ema_square = ema_decay * ema_square + (1.0 - ema_decay) * new_square
    new_ema_wide = ema_decay * ema_wide + (1.0 - ema_decay) * new_wide
    return (
        result,
        input_grad,
        new_square,
        new_wide,
        new_norm,
        new_qk,
        new_forget_w,
        new_forget_b,
        mom_square,
        mom_wide,
        mom_norm,
        mom_qk,
        mom_forget_w,
        mom_forget_b,
        new_ema_square,
        new_ema_wide,
    )


def solution(mesh):
    placed = (
        P("dp", None),
        P("dp", None),
        P("dp", None),
        P("dp"),
        P(None, "dp", "tensor"),
        P(None, "dp", "tensor"),
        P(None, "dp"),
        P(),
        P("dp", "tensor"),
        P("tensor"),
        P(None, "dp", "tensor"),
        P(None, "dp", "tensor"),
        P(None, "dp"),
        P(),
        P("dp", "tensor"),
        P("tensor"),
        P(None, "dp", "tensor"),
        P(None, "dp", "tensor"),
    )
    return jax.shard_map(
        on_device,
        mesh=mesh,
        in_specs=placed,
        out_specs=(
            P("dp", None),
            P("dp", None),
            P(None, "dp", "tensor"),
            P(None, "dp", "tensor"),
            P(None, "dp"),
            P(),
            P("dp", "tensor"),
            P("tensor"),
            P(None, "dp", "tensor"),
            P(None, "dp", "tensor"),
            P(None, "dp"),
            P(),
            P("dp", "tensor"),
            P("tensor"),
            P(None, "dp", "tensor"),
            P(None, "dp", "tensor"),
        ),
        check_vma=False,
    )
```
